256 devices in a mesh: gx: 16 (over y_hi, x, core), gy: 16 (over y_lo, z).
Axes of the slice: x: 4, y: 4 (y_hi: 2, y_lo: 2; y = y_hi * 2 + y_lo), z: 8, core: 2. Of those that a mesh axis runs over, the one named last changes fastest.
Arguments:
- nodes: bfloat16 [16, 16, 64, 512], P('gx', 'gy'), may hold values from -6 to 6
- edges: bfloat16 [16, 16, 384, 512], P('gx', 'gy'), may hold values from -6 to 6
- senders: int32 [16, 16, 384], P('gx', 'gy'), may hold values from 0 to 127, as said below
- segments: int32 [16, 16, 384], P('gx', 'gy'), may hold values from 0 to 63, never falling along the last dimension, each value on 1 to 12 neighbouring positions
- send_lists: int32 [16, 16, 4, 16], P('gx', 'gy'), may hold values from 0 to 63
- cot_nodes: bfloat16 [16, 16, 64, 512], P('gx', 'gy'), may hold values from -6 to 6
- cot_edges: bfloat16 [16, 16, 384, 512], P('gx', 'gy'), may hold values from -6 to 6
- w_edge1: bfloat16 [1536, 512], replicated, may hold values from -0.15625 to 0.15625
- w_edge2: bfloat16 [512, 512], replicated, may hold values from -0.25 to 0.25
- w_node1: bfloat16 [1024, 512], replicated, may hold values from -0.1875 to 0.1875
- w_node2: bfloat16 [512, 512], replicated, may hold values from -0.25 to 0.25
Outputs:
- node_next: bfloat16 [16, 16, 64, 512], P('gx', 'gy')
- grad_nodes: bfloat16 [16, 16, 64, 512], P('gx', 'gy')
- grad_edges: bfloat16 [16, 16, 384, 512], P('gx', 'gy')
- grad_we1: bfloat16 [1536, 512], replicated
- grad_we2: bfloat16 [512, 512], replicated
- grad_wn1: bfloat16 [1024, 512], replicated
- grad_wn2: bfloat16 [512, 512], replicated
The draws below stay inside these ranges and needn't reach their ends.
Inputs may be any that keep to these rules, and one draw needn't show every extreme that they name: `senders`: below 64 an edge's sender is an owned node; a value 64 + k * 16 + r names row r of halo block k (lower row, upper row, lower column, upper column neighbour); blocks of neighbours outside the grid are never named. `segments`: never falls along a tile's edge list; every owned node receives 1 to 12 edges. `send_lists`: entries may repeat; not every sent row need be named by a receiving edge.
All inputs are finite; a program needn't handle non-finite values.
Results may differ from the reference program's by a relative error of at most 0.012.
Values may be sent and summed in bfloat16 or wider, within the bound.
No kernel may reach another device: no remote copies, remote signals or barrier semaphores. Data moves between devices by JAX's collectives and lax.ppermute only.
A program may use at most 64 MiB of HBM per device.

```python
import math
import jax
import jax.numpy as jnp
import numpy as np
from jax import lax

D = 512
NODE_DEV = 64
MAX_IN = 12
EDGE_DEV = 384
HALO = 16
TILES_X = 16
TILES_Y = 16
EDGES = 98304


def draw_senders(key, part):
    key = jax.random.fold_in(key, 7)
    top = NODE_DEV + 4 * HALO
    picks = jax.random.randint(key, (TILES_X, TILES_Y, EDGE_DEV), 0, top, dtype=jnp.int32)
    row_idx = jnp.arange(TILES_X, dtype=jnp.int32)[:, None, None]
    col_idx = jnp.arange(TILES_Y, dtype=jnp.int32)[None, :, None]
    block = (picks - NODE_DEV) // HALO
    valid = picks < NODE_DEV
    valid = valid | (block == 0) & (row_idx > 0) | (block == 1) & (row_idx < TILES_X - 1)
    valid = valid | (block == 2) & (col_idx > 0) | (block == 3) & (col_idx < TILES_Y - 1)
    result = jnp.where(valid, picks, picks % NODE_DEV)
    result = result.at[:, :, 0].set(0)
    upper_ok = jnp.broadcast_to(col_idx[:, :, 0] < TILES_Y - 1, (TILES_X, TILES_Y))
    result = result.at[:, :, -1].set(jnp.where(upper_ok, top - 1, result[:, :, -1]))
    return result


def with_ends(values, own_key, least, top_value):
    longest = values.shape.index(max(values.shape))
    spots = []
    for shift in (0, 1):
        where = [jax.random.randint(jax.random.fold_in(own_key, axis), (), 0, length) for axis, length in enumerate(values.shape)]
        where[longest] = (where[longest] + shift) % values.shape[longest]
        spots.append(tuple(where))
    return values.at[spots[0]].set(least).at[spots[1]].set(top_value)


def block_scale(own_key, shape, split, low, top_value):
    level = 1.0
    for dim, shards_of in split:
        steps = jax.random.uniform(jax.random.fold_in(jax.random.fold_in(own_key, 6), dim), (shards_of,), jnp.float32, low / len(split), top_value / len(split))
        level = level * jnp.repeat(jnp.exp(steps), shape[dim] // shards_of).reshape((-1,) + (1,) * (len(shape) - 1 - dim))
    return level


def split_up(number_of, total, limit, lean):
    weights = [(1 << 20) // math.isqrt(rank ** lean) + 1 for rank in range(2, number_of + 1)]
    spare, holding = total - limit - (number_of - 1), [1] * (number_of - 1)
    while spare > 0:
        movable = [i for i in range(number_of - 1) if holding[i] < limit]
        whole, budget = sum([weights[i] for i in movable]), spare
        for i in movable:
            more = min(limit - holding[i], max(1, budget * weights[i] // whole), spare)
            holding[i] = holding[i] + more
            spare = spare - more
    return np.array([limit] + holding)


def uneven_parts(own_key, amount, total, limit, lean):
    if amount == 2:
        one = jax.random.randint(own_key, (), max(1, total - limit), min(limit, total - 1) + 1)
        return jnp.stack([one, total - one])
    tallies = jnp.asarray(split_up(amount, total, limit, lean), jnp.int32)
    couples = (amount - 1) // 2
    donor, sink = tallies[1:1 + 2 * couples:2], tallies[2:2 + 2 * couples:2]
    margin = jnp.minimum(donor - 1, limit - sink)
    passed = jax.random.randint(jax.random.fold_in(own_key, 1), (couples,), 0, 1 << 20) % (margin + 1)
    tallies = tallies.at[1:1 + 2 * couples:2].set(donor - passed).at[2:2 + 2 * couples:2].set(sink + passed)
    return tallies[jax.random.permutation(jax.random.fold_in(own_key, 2), amount)]


def noise(stream_key, dims, deviation, reach, cuts=(), kind=jnp.bfloat16):
    level = block_scale(stream_key, dims, cuts, -0.22, 0.18) if cuts else 1.0
    array = jax.random.normal(stream_key, dims, jnp.float32) * deviation * level
    return jnp.minimum(jnp.maximum(array, -reach), reach).astype(kind)


def setup_inputs(seed: int = 0) -> dict:
    arg_keys = jax.random.split(jax.random.key(seed), 12)
    return {
        "nodes": noise(arg_keys[0], (TILES_X, TILES_Y, NODE_DEV, D), 1.0, 6.0, ((0, 16), (1, 16))),
        "edges": noise(arg_keys[1], (TILES_X, TILES_Y, EDGE_DEV, D), 1.0, 6.0, ((0, 16), (1, 16))),
        "senders": draw_senders(jax.random.fold_in(arg_keys[11], 71), 0),
        "segments": jax.vmap(lambda own: jnp.searchsorted(jnp.cumsum(uneven_parts(own, NODE_DEV, EDGE_DEV, MAX_IN, 2)), jnp.arange(EDGE_DEV), side="right"))(jax.random.split(arg_keys[3], TILES_X * TILES_Y)).reshape((TILES_X, TILES_Y, EDGE_DEV)).astype(jnp.int32),
        "send_lists": with_ends(jax.random.randint(arg_keys[4], (TILES_X, TILES_Y, 4, HALO), 0, NODE_DEV), jax.random.fold_in(arg_keys[4], 1), 0, NODE_DEV - 1).astype(jnp.int32),
        "cot_nodes": noise(arg_keys[5], (TILES_X, TILES_Y, NODE_DEV, D), 1.0, 6.0, ((0, 16), (1, 16))),
        "cot_edges": noise(arg_keys[6], (TILES_X, TILES_Y, EDGE_DEV, D), 1.0, 6.0, ((0, 16), (1, 16))),
        "w_edge1": noise(arg_keys[7], (3 * D, D), (3 * D) ** -0.5, 0.15625),
        "w_edge2": noise(arg_keys[8], (D, D), D ** -0.5, 0.25),
        "w_node1": noise(arg_keys[9], (2 * D, D), (2 * D) ** -0.5, 0.1875),
        "w_node2": noise(arg_keys[10], (D, D), D ** -0.5, 0.25),
    }


def layer_norm(values):
    mean = lax.optimization_barrier(jnp.mean(values, axis=-1, keepdims=True))
    centred = values - mean
    scale = lax.rsqrt(lax.optimization_barrier(jnp.mean(centred * centred, axis=-1, keepdims=True)) + 1e-05)
    return (centred * scale, scale)

def norm_back(grad, normed, scale):
    first = lax.optimization_barrier(jnp.mean(grad, axis=-1, keepdims=True))
    second = lax.optimization_barrier(jnp.mean(grad * normed, axis=-1, keepdims=True))
    return scale * (grad - first - normed * second)

def silu_slope(values):
    sig = jax.nn.sigmoid(values)
    return sig * (1.0 + values * (1.0 - sig))

def inner_rows(left, right):
    return lax.dot_general(left, right, (((0,), (0,)), ((), ())), preferred_element_type=jnp.float32)

def outer_cols(left, right):
    return lax.dot_general(left, right, (((1,), (1,)), ((), ())), preferred_element_type=jnp.float32)

def local_pass(edge_lat, node_lat, ext, senders, segments, cot_node, cot_edge, w_edge1, w_edge2, w_node1, w_node2):
    count = node_lat.shape[0]
    width = node_lat.shape[1]
    sent = jnp.take(ext, senders, axis=0)
    recv = jnp.take(node_lat, segments, axis=0)
    x_edge = jnp.concatenate([edge_lat, sent, recv], axis=1)
    z_one = jnp.dot(x_edge, w_edge1, preferred_element_type=jnp.float32)
    a_one = jax.nn.silu(z_one).astype(jnp.bfloat16)
    z_two = jnp.dot(a_one, w_edge2, preferred_element_type=jnp.float32)
    n_two, s_two = layer_norm(z_two)
    e_new = (edge_lat.astype(jnp.float32) + n_two).astype(jnp.bfloat16)
    onehot = segments[None, :] == jnp.arange(count, dtype=jnp.int32)[:, None]
    agg = jnp.dot(onehot.astype(jnp.bfloat16), e_new, preferred_element_type=jnp.float32).astype(jnp.bfloat16)
    y_node = jnp.concatenate([node_lat, agg], axis=1)
    z_three = jnp.dot(y_node, w_node1, preferred_element_type=jnp.float32)
    a_three = jax.nn.silu(z_three).astype(jnp.bfloat16)
    z_four = jnp.dot(a_three, w_node2, preferred_element_type=jnp.float32)
    n_four, s_four = layer_norm(z_four)
    node_new = (node_lat.astype(jnp.float32) + n_four).astype(jnp.bfloat16)
    g_node = cot_node.astype(jnp.float32)
    dz_four = norm_back(g_node, n_four, s_four).astype(jnp.bfloat16)
    dw_node2 = inner_rows(a_three, dz_four)
    da_three = outer_cols(dz_four, w_node2)
    dz_three = (da_three * silu_slope(z_three)).astype(jnp.bfloat16)
    dw_node1 = inner_rows(y_node, dz_three)
    d_ynode = outer_cols(dz_three, w_node1)
    de_new = cot_edge.astype(jnp.float32) + jnp.take(d_ynode[:, width:], segments, axis=0)
    dz_two = norm_back(de_new, n_two, s_two).astype(jnp.bfloat16)
    dw_edge2 = inner_rows(a_one, dz_two)
    da_one = outer_cols(dz_two, w_edge2)
    dz_one = (da_one * silu_slope(z_one)).astype(jnp.bfloat16)
    dw_edge1 = inner_rows(x_edge, dz_one)
    d_xedge = outer_cols(dz_one, w_edge1)
    grad_edge = (de_new + d_xedge[:, :width]).astype(jnp.bfloat16)
    by_recv = jnp.dot(onehot.astype(jnp.float32), d_xedge[:, 2 * width:], precision=lax.Precision.HIGHEST)
    by_send = jax.ops.segment_sum(d_xedge[:, width:2 * width], senders, num_segments=ext.shape[0])
    d_node = g_node + d_ynode[:, :width] + by_recv + by_send[:count]
    return (node_new, grad_edge, d_node, by_send[count:], (dw_edge1, dw_edge2, dw_node1, dw_node2))

def shift_lower(values, axis):
    zero = jnp.zeros_like(lax.slice_in_dim(values, 0, 1, axis=axis))
    return jnp.concatenate([zero, lax.slice_in_dim(values, 0, values.shape[axis] - 1, axis=axis)], axis)

def shift_upper(values, axis):
    zero = jnp.zeros_like(lax.slice_in_dim(values, 0, 1, axis=axis))
    return jnp.concatenate([lax.slice_in_dim(values, 1, values.shape[axis], axis=axis), zero], axis)

def reference(nodes, edges, senders, segments, send_lists, cot_nodes, cot_edges, w_edge1, w_edge2, w_node1, w_node2):
    tiles_a, tiles_b, count, width = nodes.shape
    rows = send_lists.shape[-1]
    packs = jax.vmap(jax.vmap(lambda lat, idx: jnp.take(lat, idx, axis=0)))(nodes, send_lists)
    received = jnp.stack([shift_lower(packs[:, :, 1], 0), shift_upper(packs[:, :, 0], 0), shift_lower(packs[:, :, 3], 1), shift_upper(packs[:, :, 2], 1)], axis=2)
    ext = jnp.concatenate([nodes, received.reshape(tiles_a, tiles_b, 4 * rows, width)], axis=2)
    tiles = tiles_a * tiles_b

    def flat(values):
        return values.reshape((tiles,) + values.shape[2:])

    def step(carry, inputs):
        edge_lat, node_lat, ext_lat, send_idx, seg_idx, cot_node, cot_edge = inputs
        node_new, grad_edge, d_node, halo_grad, weights = local_pass(edge_lat, node_lat, ext_lat, send_idx, seg_idx, cot_node, cot_edge, w_edge1, w_edge2, w_node1, w_node2)
        carry = tuple((total + part for total, part in zip(carry, weights)))
        return (carry, (node_new, grad_edge, d_node, halo_grad))
    start = (jnp.zeros(w_edge1.shape, jnp.float32), jnp.zeros(w_edge2.shape, jnp.float32), jnp.zeros(w_node1.shape, jnp.float32), jnp.zeros(w_node2.shape, jnp.float32))
    sums, outputs = lax.scan(step, start, (flat(edges), flat(nodes), flat(ext), flat(senders), flat(segments), flat(cot_nodes), flat(cot_edges)))
    node_new, grad_edge, d_node, halo_grad = outputs
    node_new = node_new.reshape(nodes.shape)
    grad_edge = grad_edge.reshape(edges.shape)
    d_node = d_node.reshape(tiles_a, tiles_b, count, width)
    halo_grad = halo_grad.reshape(tiles_a, tiles_b, 4, rows, width)
    returned = jnp.stack([shift_lower(halo_grad[:, :, 1], 0), shift_upper(halo_grad[:, :, 0], 0), shift_lower(halo_grad[:, :, 3], 1), shift_upper(halo_grad[:, :, 2], 1)], axis=2)

    def add_back(grad, idx, back):
        return grad.at[idx.reshape(-1)].add(back.reshape(-1, width))
    d_node = jax.vmap(jax.vmap(add_back))(d_node, send_lists, returned)
    factor = 1.0 / jnp.sqrt(jnp.float32(EDGES))
    grads = tuple(((total * factor).astype(jnp.bfloat16) for total in sums))
    return (node_new, d_node.astype(jnp.bfloat16), grad_edge, grads[0], grads[1], grads[2], grads[3])
```

```python
import jax
import jax.numpy as jnp
from jax import lax
from jax.experimental import pallas as pl
from jax.experimental.pallas import tpu as pltpu
from jax.sharding import Mesh
from jax.sharding import PartitionSpec as P

BF = jnp.bfloat16
F32 = jnp.float32
GX = ("yh", "x", "c")
GY = ("yl", "z")
PLANE = ("yh", "x", "yl")
VMEM = pl.BlockSpec(memory_space=pltpu.VMEM)
ANY = pl.BlockSpec(memory_space=pl.ANY)


def dot(left, right):
    return jnp.dot(left, right, preferred_element_type=F32)


def dot_rows(left, right):
    return lax.dot_general(left, right, (((0,), (0,)), ((), ())), preferred_element_type=F32)


def dot_cols(left, right):
    return lax.dot_general(left, right, (((1,), (1,)), ((), ())), preferred_element_type=F32)


def hi_lo(values):
    high = values.astype(BF)
    low = (values - high.astype(F32)).astype(BF)
    return jnp.concatenate([high, low], axis=0)


def fold(values):
    half = values.shape[0] // 2
    return values[:half] + values[half:]


def layer_norm(values):
    mean = jnp.mean(values, axis=-1, keepdims=True)
    centred = values - mean
    scale = lax.rsqrt(jnp.mean(centred * centred, axis=-1, keepdims=True) + 1e-05)
    return centred * scale, scale


def norm_back(grad, normed, scale):
    first = jnp.mean(grad, axis=-1, keepdims=True)
    second = jnp.mean(grad * normed, axis=-1, keepdims=True)
    return scale * (grad - first - normed * second)


def silu_and_slope(values):
    sig = 1.0 / (1.0 + jnp.exp(-values))
    return values * sig, sig * (1.0 + values * (1.0 - sig))


def pick(row, count):
    rows = lax.broadcasted_iota(jnp.int32, (count, row.shape[-1]), 0)
    return jnp.where(rows == row, 1.0, 0.0)


def pack_kernel(nodes, lists, *packs):
    lat = nodes[0, 0]
    for side in range(4):
        chosen = pick(lists[0, 0, side : side + 1, :], lat.shape[0]).astype(BF)
        packs[side][...] = dot_rows(chosen, lat).astype(BF)


def layer_kernel(
    nodes,
    edges,
    halo0,
    halo1,
    halo2,
    halo3,
    senders,
    segments,
    cot_nodes,
    cot_edges,
    w_edge1,
    w_edge2,
    w_node1,
    w_node2,
    node_next,
    grad_edges,
    d_node,
    back0,
    back1,
    back2,
    back3,
    keep,
    send,
):
    core = lax.axis_index("c")
    node = nodes[0, 0]
    edge = edges[0, 0]
    width = node.shape[1]
    count = node.shape[0]
    half = keep.shape[0]

    def put(start, value):
        stop = start + value.shape[0]
        value = value.astype(BF)
        for side in range(2):
            low, high = max(start, side * half), min(stop, (side + 1) * half)
            if low >= high:
                continue
            part = value[low - start : high - start]

            @pl.when(core == side)
            def _():
                keep[low - side * half : high - side * half, :] = part

            @pl.when(core != side)
            def _():
                send[low - side * half : high - side * half, :] = part

    ext = jnp.concatenate([node, halo0[...], halo1[...], halo2[...], halo3[...]], axis=0)
    by_send = pick(senders[0], ext.shape[0])
    by_recv = pick(segments[0], count)
    from_ext = by_send.T.astype(BF)
    from_node = by_recv.T.astype(BF)
    to_ext = by_send.astype(BF)
    to_node = by_recv.astype(BF)

    wide = jnp.concatenate([from_ext, from_ext, from_node, from_node], axis=1)
    terms = jnp.concatenate(
        [
            hi_lo(dot(ext, w_edge1[width : 2 * width, :])),
            hi_lo(dot(node, w_edge1[2 * width :, :])),
        ],
        axis=0,
    )
    z_one = dot(edge, w_edge1[:width, :]) + dot(wide, terms)
    act, slope_one = silu_and_slope(z_one)
    a_one = act.astype(BF)
    n_two, s_two = layer_norm(dot(a_one, w_edge2[...]))
    e_new = (edge.astype(F32) + n_two).astype(BF)
    agg = dot(to_node, e_new).astype(BF)
    z_three = dot(node, w_node1[:width, :]) + dot(agg, w_node1[width:, :])
    act, slope_three = silu_and_slope(z_three)
    a_three = act.astype(BF)
    n_four, s_four = layer_norm(dot(a_three, w_node2[...]))
    node_next[0, 0] = (node.astype(F32) + n_four).astype(BF)

    g_node = cot_nodes[0, 0].astype(F32)
    dz_four = norm_back(g_node, n_four, s_four).astype(BF)
    dz_three = (dot_cols(dz_four, w_node2[...]) * slope_three).astype(BF)
    dy_node = dot_cols(dz_three, w_node1[:width, :])
    dy_agg = dot_cols(dz_three, w_node1[width:, :])
    put(4 * width, dot_rows(node, dz_three))
    put(5 * width, dot_rows(agg, dz_three))
    put(6 * width, dot_rows(a_three, dz_four))

    twice = jnp.concatenate([from_node, from_node], axis=1)
    de_new = cot_edges[0, 0].astype(F32) + dot(twice, hi_lo(dy_agg))
    dz_two = norm_back(de_new, n_two, s_two).astype(BF)
    dz_one = (dot_cols(dz_two, w_edge2[...]) * slope_one).astype(BF)
    put(3 * width, dot_rows(a_one, dz_two))
    put(0, dot_rows(edge, dz_one))
    grad_edges[0, 0] = (de_new + dot_cols(dz_one, w_edge1[:width, :])).astype(BF)

    sum_send = hi_lo(dot(to_ext, dz_one))
    sum_recv = hi_lo(dot(to_node, dz_one))
    put(width, dot_rows(jnp.concatenate([ext, ext], axis=0), sum_send))
    put(2 * width, dot_rows(jnp.concatenate([node, node], axis=0), sum_recv))
    d_ext = fold(dot_cols(sum_send, w_edge1[width : 2 * width, :]))
    d_recv = fold(dot_cols(sum_recv, w_edge1[2 * width :, :]))
    d_node[...] = g_node + dy_node + d_recv + d_ext[:count]
    rows = back0.shape[0]
    for side, back in enumerate((back0, back1, back2, back3)):
        back[...] = d_ext[count + side * rows : count + (side + 1) * rows].astype(BF)


def return_kernel(d_node, lists, ret0, ret1, ret2, ret3, out):
    total = d_node[...]
    for side, ret in enumerate((ret0, ret1, ret2, ret3)):
        chosen = pick(lists[0, 0, side : side + 1, :], total.shape[0]).astype(BF)
        total = total + dot(chosen, ret[...])
    out[0, 0] = total.astype(BF)


def pair_sum_kernel(mine, other, out):
    out[...] = (mine[...].astype(F32) + other[...].astype(F32)).astype(BF)


def plane_sum_kernel(parts, out):
    rows, lanes = out.shape[1], out.shape[2]
    for block in range(out.shape[0]):
        r, c = block % 2 * rows, block // 2 * lanes
        total = parts[0, r : r + rows, c : c + lanes].astype(F32)
        for part in range(1, parts.shape[0]):
            total = total + parts[part, r : r + rows, c : c + lanes].astype(F32)
        out[block] = total


def line_sum_kernel(factor, parts, out):
    total = parts[0]
    for part in range(1, parts.shape[0]):
        total = total + parts[part]
    total = (total * factor).astype(BF)
    for part in range(out.shape[0]):
        out[part] = total


def spread_kernel(blocks, out):
    rows, lanes = blocks.shape[1], blocks.shape[2]
    tops = jnp.concatenate([blocks[2 * i] for i in range(4)], axis=1)
    ends = jnp.concatenate([blocks[2 * i + 1] for i in range(4)], axis=1)
    whole = jnp.concatenate([tops, ends], axis=0)
    for part in range(out.shape[0]):
        out[part] = whole


def finish_kernel(mine, other, *refs):
    outs, sem = refs[:4], refs[4]
    core = lax.axis_index("c")
    half = mine.shape[0]

    def copies(low_half, high_half):
        made = []
        start = 0
        for out in outs:
            stop = start + out.shape[0]
            for side, source in enumerate((low_half, high_half)):
                low, high = max(start, side * half), min(stop, (side + 1) * half)
                if low < high:
                    made.append(
                        pltpu.make_async_copy(
                            source.at[pl.ds(low - side * half, high - low)],
                            out.at[pl.ds(low - start, high - low)],
                            sem.at[len(made)],
                        )
                    )
            start = stop
        for copy in made:
            copy.start()
        for copy in made:
            copy.wait()

    @pl.when(core == 0)
    def _():
        copies(mine, other)

    @pl.when(core != 0)
    def _():
        copies(other, mine)


def call(kernel, outs, n_in, limit=32, **kwargs):
    return pl.pallas_call(
        kernel,
        out_shape=outs,
        in_specs=[VMEM] * n_in,
        out_specs=jax.tree.map(lambda _: VMEM, outs),
        compiler_params=pltpu.CompilerParams(vmem_limit_bytes=limit << 20),
        **kwargs,
    )


def shape(dims, kind=BF):
    return jax.ShapeDtypeStruct(dims, kind)


def cycle(count, step):
    return [(i, (i + step) % count) for i in range(count)]


def local(
    nodes,
    edges,
    senders,
    segments,
    send_lists,
    cot_nodes,
    cot_edges,
    w_edge1,
    w_edge2,
    w_node1,
    w_node2,
):
    width = nodes.shape[3]
    rows = send_lists.shape[3]
    nx, ny = lax.axis_size(GX), lax.axis_size(GY)
    block = [shape((rows, width))] * 4
    packs = call(pack_kernel, block, 2)(nodes, send_lists)
    halo0 = lax.ppermute(packs[1], GX, cycle(nx, 1))
    halo1 = lax.ppermute(packs[0], GX, cycle(nx, -1))
    halo2 = lax.ppermute(packs[3], GY, cycle(ny, 1))
    halo3 = lax.ppermute(packs[2], GY, cycle(ny, -1))
    total = w_edge1.shape[0] + w_edge2.shape[0] + w_node1.shape[0] + w_node2.shape[0]
    half = shape((total // 2, width))
    node_next, grad_edges, d_node, back0, back1, back2, back3, keep, send = call(
        layer_kernel,
        [shape(nodes.shape), shape(edges.shape), shape((nodes.shape[2], width), F32)]
        + block
        + [half, half],
        14,
        limit=48,
    )(
        nodes,
        edges,
        halo0,
        halo1,
        halo2,
        halo3,
        senders,
        segments,
        cot_nodes,
        cot_edges,
        w_edge1,
        w_edge2,
        w_node1,
        w_node2,
    )

    got = lax.ppermute(send, "c", cycle(2, 1))
    pair = call(pair_sum_kernel, half, 2)(keep, got)
    ret0 = lax.ppermute(back1, GX, cycle(nx, 1))
    ret1 = lax.ppermute(back0, GX, cycle(nx, -1))
    ret2 = lax.ppermute(back3, GY, cycle(ny, 1))
    ret3 = lax.ppermute(back2, GY, cycle(ny, -1))
    grad_nodes = call(return_kernel, shape(nodes.shape), 6)(
        d_node, send_lists, ret0, ret1, ret2, ret3
    )

    plane, line = lax.axis_size(PLANE), lax.axis_size("z")
    strip = total // 2 // plane
    cut = (line, strip // 2, width * 2 // line)
    pieces = lax.all_to_all(pair, PLANE, 0, 0, tiled=True).reshape(plane, strip, width)
    pieces = call(plane_sum_kernel, shape(cut, F32), 1)(pieces)
    pieces = lax.all_to_all(pieces, "z", 0, 0, tiled=True)
    factor = float(edges.shape[2] * nx * ny) ** -0.5
    pieces = call(lambda a, b: line_sum_kernel(factor, a, b), shape(cut), 1)(pieces)
    pieces = lax.all_to_all(pieces, "z", 0, 0, tiled=True)
    pieces = call(spread_kernel, shape((plane, strip, width)), 1)(pieces)
    mine = lax.all_to_all(pieces, PLANE, 0, 0, tiled=True).reshape(total // 2, width)
    other = lax.ppermute(mine, "c", cycle(2, 1))
    grads = pl.pallas_call(
        finish_kernel,
        out_shape=[shape(w.shape) for w in (w_edge1, w_edge2, w_node1, w_node2)],
        in_specs=[ANY] * 2,
        out_specs=[ANY] * 4,
        scratch_shapes=[pltpu.SemaphoreType.DMA((5,))],
    )(mine, other)
    return (node_next, grad_nodes, grad_edges, *grads)


def solution(mesh):
    fine = Mesh(mesh.devices.reshape(2, 4, 2, 2, 8), ("yh", "x", "c", "yl", "z"))
    tile = P(GX, GY)
    return jax.shard_map(
        local,
        mesh=fine,
        in_specs=(tile,) * 7 + (P(),) * 4,
        out_specs=(tile,) * 3 + (P(),) * 4,
        check_vma=False,
    )
```

```python
import functools

import jax
import jax.numpy as jnp
from jax import lax
from jax.experimental import pallas as pl
from jax.experimental.pallas import tpu as pltpu
from jax.sharding import Mesh
from jax.sharding import PartitionSpec as P

BF = jnp.bfloat16
F32 = jnp.float32
GX = ("yh", "x", "c")
GY = ("yl", "z")
PLANE = ("yh", "x", "yl")
VMEM = pl.BlockSpec(memory_space=pltpu.VMEM)
ANY = pl.BlockSpec(memory_space=pl.ANY)


def dot(left, right):
    return jnp.dot(left, right, preferred_element_type=F32)


def dot_rows(left, right):
    return lax.dot_general(left, right, (((0,), (0,)), ((), ())), preferred_element_type=F32)


def dot_cols(left, right):
    return lax.dot_general(left, right, (((1,), (1,)), ((), ())), preferred_element_type=F32)


def hi_lo(values):
    high = values.astype(BF)
    low = (values - high.astype(F32)).astype(BF)
    return jnp.concatenate([high, low], axis=0)


def fold(values):
    half = values.shape[0] // 2
    return values[:half] + values[half:]


def layer_norm(values):
    mean = jnp.mean(values, axis=-1, keepdims=True)
    centred = values - mean
    scale = lax.rsqrt(jnp.mean(centred * centred, axis=-1, keepdims=True) + 1e-05)
    return centred * scale, scale


def norm_back(grad, normed, scale):
    first = jnp.mean(grad, axis=-1, keepdims=True)
    second = jnp.mean(grad * normed, axis=-1, keepdims=True)
    return scale * (grad - first - normed * second)


def silu_and_slope(values):
    sig = 1.0 / (1.0 + jnp.exp(-values))
    return values * sig, sig * (1.0 + values * (1.0 - sig))


def pick(row, count):
    rows = lax.broadcasted_iota(jnp.int32, (count, row.shape[-1]), 0)
    return jnp.where(rows == row, 1.0, 0.0)


def fetch(sources, targets, sems):
    copies = [
        pltpu.make_async_copy(source, target, sems.at[i])
        for i, (source, target) in enumerate(zip(sources, targets, strict=True))
    ]
    for copy in copies:
        copy.start()

    def ready(i):
        copies[i].wait()
        return targets[i]

    return ready


def parities():
    return lax.axis_index("c"), lax.rem(lax.axis_index("z"), 2)


def side_of(step, row_odd, col_odd):
    return (1 - row_odd, row_odd, 3 - col_odd, 2 + col_odd)[step]


def pack_kernel(nodes_hbm, lists_hbm, *refs):
    packs, (nodes, lists, sems) = refs[:4], refs[4:]
    ready = fetch((nodes_hbm.at[0, 0], lists_hbm.at[0, 0]), (nodes, lists), sems)
    odd = parities()
    ready(1)
    lat = ready(0)[...]
    for step in range(4):
        row = lists[pl.ds(side_of(step, *odd), 1), :]
        packs[step][...] = dot_rows(pick(row, lat.shape[0]).astype(BF), lat).astype(BF)


def layer_kernel(
    nodes_hbm,
    edges_hbm,
    halo0,
    halo1,
    halo2,
    halo3,
    senders_hbm,
    segments_hbm,
    cot_nodes_hbm,
    cot_edges_hbm,
    w_edge1_hbm,
    w_edge2_hbm,
    w_node1_hbm,
    w_node2_hbm,
    node_next,
    grad_edges,
    d_node,
    back0,
    back1,
    back2,
    back3,
    keep,
    send,
    nodes,
    edges,
    senders,
    segments,
    cot_nodes,
    cot_edges,
    w_edge1,
    w_edge2,
    w_node1,
    w_node2,
    ext_twice,
    node_twice,
    a_one,
    agg,
    a_three,
    d_ext,
    sems,
):
    ready = fetch(
        (
            senders_hbm.at[0],
            segments_hbm.at[0],
            nodes_hbm.at[0, 0],
            edges_hbm.at[0, 0],
            w_edge1_hbm,
            w_edge2_hbm,
            w_node1_hbm,
            w_node2_hbm,
            cot_nodes_hbm.at[0, 0],
            cot_edges_hbm.at[0, 0],
        ),
        (
            senders,
            segments,
            nodes,
            edges,
            w_edge1,
            w_edge2,
            w_node1,
            w_node2,
            cot_nodes,
            cot_edges,
        ),
        sems,
    )
    odd = parities()
    width = nodes.shape[1]
    count = nodes.shape[0]
    rows = halo0.shape[0]
    part = width // 2

    def put(block, left, right):
        for target, side in ((send, 1 - odd[0]), (keep, odd[0])):
            columns = pl.ds(pl.multiple_of(side * part, part), part)
            target[block * part : (block + 1) * part, :] = dot_rows(
                left[:, columns], right
            ).astype(BF)

    reach = ext_twice.shape[0] // 2
    by_send = pick(ready(0)[...], reach)
    by_recv = pick(ready(1)[...], count)
    from_ext = by_send.T.astype(BF)
    from_node = by_recv.T.astype(BF)
    to_ext = by_send.astype(BF)
    to_node = by_recv.astype(BF)
    wide = jnp.concatenate([from_ext, from_ext, from_node, from_node], axis=1)

    node = ready(2)[...]
    for start in (0, reach):
        ext_twice[start : start + count, :] = node
        for step, halo in enumerate((halo0, halo1, halo2, halo3)):
            place = start + count + side_of(step, *odd) * rows
            ext_twice[pl.ds(pl.multiple_of(place, rows), rows), :] = halo[...]
    for start in (0, count):
        node_twice[start : start + count, :] = node
    ext = ext_twice[:reach, :]
    edge = ready(3)[...]
    ready(4)

    terms = jnp.concatenate(
        [
            hi_lo(dot(ext, w_edge1[width : 2 * width, :])),
            hi_lo(dot(node, w_edge1[2 * width :, :])),
        ],
        axis=0,
    )
    z_one = dot(edge, w_edge1[:width, :]) + dot(wide, terms)
    act, slope_one = silu_and_slope(z_one)
    a_one[...] = act.astype(BF)
    ready(5)
    n_two, s_two = layer_norm(dot(a_one[...], w_edge2[...]))
    e_new = (edge.astype(F32) + n_two).astype(BF)
    agg[...] = dot(to_node, e_new).astype(BF)
    ready(6)
    z_three = dot(node, w_node1[:width, :]) + dot(agg[...], w_node1[width:, :])
    act, slope_three = silu_and_slope(z_three)
    a_three[...] = act.astype(BF)
    ready(7)
    n_four, s_four = layer_norm(dot(a_three[...], w_node2[...]))
    node_next[0, 0] = (node.astype(F32) + n_four).astype(BF)

    g_node = ready(8)[...].astype(F32)
    dz_four = norm_back(g_node, n_four, s_four).astype(BF)
    dz_three = (dot_cols(dz_four, w_node2[...]) * slope_three).astype(BF)
    dy_node = dot_cols(dz_three, w_node1[:width, :])
    dy_agg = dot_cols(dz_three, w_node1[width:, :])

    twice = jnp.concatenate([from_node, from_node], axis=1)
    de_new = ready(9)[...].astype(F32) + dot(twice, hi_lo(dy_agg))
    dz_two = norm_back(de_new, n_two, s_two).astype(BF)
    dz_one = (dot_cols(dz_two, w_edge2[...]) * slope_one).astype(BF)
    sum_send = hi_lo(dot(to_ext, dz_one))
    sum_recv = hi_lo(dot(to_node, dz_one))
    put(0, edges, dz_one)
    put(1, ext_twice, sum_send)
    put(2, node_twice, sum_recv)
    put(3, a_one, dz_two)
    put(4, nodes, dz_three)
    put(5, agg, dz_three)
    put(6, a_three, dz_four)
    grad_edges[0, 0] = (de_new + dot_cols(dz_one, w_edge1[:width, :])).astype(BF)
    d_ext[...] = fold(dot_cols(sum_send, w_edge1[width : 2 * width, :]))
    d_recv = fold(dot_cols(sum_recv, w_edge1[2 * width :, :]))
    d_node[...] = g_node + dy_node + d_recv + d_ext[:count, :]
    for step, back in enumerate((back0, back1, back2, back3)):
        place = count + side_of(step, *odd) * rows
        back[...] = d_ext[pl.ds(pl.multiple_of(place, rows), rows), :].astype(BF)


def pair_sum_kernel(mine, other, out):
    out[...] = (mine[...].astype(F32) + other[...].astype(F32)).astype(BF)


def plane_sum_kernel(parts, d_node, lists, ret0, ret1, ret2, ret3, out, grad_nodes):
    rows, lanes = out.shape[1], out.shape[2]
    for block in range(out.shape[0]):
        r, c = block % 2 * rows, block // 2 * lanes
        total = parts[0, r : r + rows, c : c + lanes].astype(F32)
        for part in range(1, parts.shape[0]):
            total = total + parts[part, r : r + rows, c : c + lanes].astype(F32)
        out[block] = total
    odd = parities()
    total = d_node[...]
    for step, ret in enumerate((ret0, ret1, ret2, ret3)):
        row = lists[0, 0, pl.ds(side_of(step, *odd), 1), :]
        total = total + dot(pick(row, total.shape[0]).astype(BF), ret[...])
    grad_nodes[0, 0] = total.astype(BF)


def line_sum_kernel(factor, parts, out):
    total = parts[0]
    for part in range(1, parts.shape[0]):
        total = total + parts[part]
    total = (total * factor).astype(BF)
    for part in range(out.shape[0]):
        out[part] = total


def spread_kernel(blocks, out):
    tops = jnp.concatenate([blocks[2 * i] for i in range(4)], axis=1)
    ends = jnp.concatenate([blocks[2 * i + 1] for i in range(4)], axis=1)
    whole = jnp.concatenate([tops, ends], axis=0)
    for part in range(out.shape[0]):
        out[part] = whole


def place_kernel(other_core, half, *refs):
    outs, sems = refs[-5:-1], refs[-1]
    part = outs[0].shape[1] // 2
    side = lax.axis_index("c")
    side = 1 - side if other_core else side
    copies = []
    for out in outs:
        for block in range(out.shape[0] // (2 * part)):
            place = pl.multiple_of((2 * block + side) * part, part)
            start = len(copies) * part
            copies.append(
                pltpu.make_async_copy(
                    half.at[start : start + part], out.at[pl.ds(place, part)], sems.at[len(copies)]
                )
            )
    for copy in copies:
        copy.start()
    for copy in copies:
        copy.wait()


def call(kernel, outs, ins, limit=24, scratch=(), **kwargs):
    return pl.pallas_call(
        kernel,
        out_shape=outs,
        in_specs=ins,
        out_specs=jax.tree.map(lambda _: VMEM, outs),
        scratch_shapes=list(scratch),
        compiler_params=pltpu.CompilerParams(vmem_limit_bytes=limit << 20),
        **kwargs,
    )


def shape(dims, kind=BF):
    return jax.ShapeDtypeStruct(dims, kind)


def in_hbm(*arrays):
    return [pltpu.with_memory_space_constraint(array, pltpu.HBM) for array in arrays]


def pairs(count, first):
    made = []
    for i in range(first, count + first, 2):
        made += [(i, (i + 1) % count), ((i + 1) % count, i)]
    return made


def exchange(blocks):
    nx, ny = lax.axis_size(GX), lax.axis_size(GY)
    return [
        lax.ppermute(blocks[0], GX, pairs(nx, 0)),
        lax.ppermute(blocks[1], GX, pairs(nx, 1)),
        lax.ppermute(blocks[2], GY, pairs(ny, 0)),
        lax.ppermute(blocks[3], GY, pairs(ny, 1)),
    ]


def local(
    nodes,
    edges,
    senders,
    segments,
    send_lists,
    cot_nodes,
    cot_edges,
    w_edge1,
    w_edge2,
    w_node1,
    w_node2,
):
    count, width = nodes.shape[2:]
    lines = edges.shape[2]
    rows = send_lists.shape[3]
    weights = (w_edge1, w_edge2, w_node1, w_node2)
    total = sum(w.shape[0] for w in weights)
    block = [shape((rows, width))] * 4
    packs = call(
        pack_kernel,
        block,
        [ANY] * 2,
        scratch=[
            pltpu.VMEM((count, width), BF),
            pltpu.VMEM((4, rows), jnp.int32),
            pltpu.SemaphoreType.DMA((2,)),
        ],
    )(*in_hbm(nodes, send_lists))
    halos = exchange(packs)
    half = shape((total // 2, width))
    reach = count + 4 * rows
    node_next, grad_edges, d_node, *backs, keep, send = call(
        layer_kernel,
        [shape(nodes.shape), shape(edges.shape), shape((count, width), F32)] + block + [half] * 2,
        [ANY] * 2 + [VMEM] * 4 + [ANY] * 8,
        limit=28,
        scratch=[
            pltpu.VMEM((count, width), BF),
            pltpu.VMEM((lines, width), BF),
            pltpu.VMEM((1, lines), jnp.int32),
            pltpu.VMEM((1, lines), jnp.int32),
            pltpu.VMEM((count, width), BF),
            pltpu.VMEM((lines, width), BF),
            *[pltpu.VMEM(w.shape, BF) for w in weights],
            pltpu.VMEM((2 * reach, width), BF),
            pltpu.VMEM((2 * count, width), BF),
            pltpu.VMEM((lines, width), BF),
            pltpu.VMEM((count, width), BF),
            pltpu.VMEM((count, width), BF),
            pltpu.VMEM((reach, width), F32),
            pltpu.SemaphoreType.DMA((10,)),
        ],
    )(
        *in_hbm(nodes, edges),
        *halos,
        *in_hbm(senders, segments, cot_nodes, cot_edges, *weights),
    )

    returned = exchange(backs)
    got = lax.ppermute(send, "c", pairs(2, 0))
    pair = call(pair_sum_kernel, half, [VMEM] * 2)(keep, got)

    plane, line = lax.axis_size(PLANE), lax.axis_size("z")
    strip = total // 2 // plane
    cut = (line, strip // 2, width * 2 // line)
    pieces = lax.all_to_all(pair, PLANE, 0, 0, tiled=True).reshape(plane, strip, width)
    pieces, grad_nodes = call(
        plane_sum_kernel, [shape(cut, F32), shape(nodes.shape)], [VMEM] * 7
    )(pieces, d_node, send_lists, *returned)
    pieces = lax.all_to_all(pieces, "z", 0, 0, tiled=True)
    factor = float(lines * plane * line * 2) ** -0.5
    pieces = call(functools.partial(line_sum_kernel, factor), shape(cut), [VMEM])(pieces)
    pieces = lax.all_to_all(pieces, "z", 0, 0, tiled=True)
    pieces = call(spread_kernel, shape((plane, strip, width)), [VMEM])(pieces)
    mine = lax.all_to_all(pieces, PLANE, 0, 0, tiled=True).reshape(total // 2, width)
    other = lax.ppermute(mine, "c", pairs(2, 0))
    outs = [shape(w.shape) for w in weights]
    sems = [pltpu.SemaphoreType.DMA((total // width,))]
    grads = pl.pallas_call(
        functools.partial(place_kernel, False),
        out_shape=outs,
        in_specs=[VMEM],
        out_specs=[ANY] * 4,
        scratch_shapes=sems,
    )(mine)
    grads = pl.pallas_call(
        functools.partial(place_kernel, True),
        out_shape=outs,
        in_specs=[VMEM] + [ANY] * 4,
        out_specs=[ANY] * 4,
        scratch_shapes=sems,
        input_output_aliases={1: 0, 2: 1, 3: 2, 4: 3},
    )(other, *grads)
    return (node_next, grad_nodes, grad_edges, *grads)


def solution(mesh):
    fine = Mesh(mesh.devices.reshape(2, 4, 2, 2, 8), ("yh", "x", "c", "yl", "z"))
    tile = P(GX, GY)
    return jax.shard_map(
        local,
        mesh=fine,
        in_specs=(tile,) * 7 + (P(),) * 4,
        out_specs=(tile,) * 3 + (P(),) * 4,
        check_vma=False,
    )
```

```python
import functools

import jax
import jax.numpy as jnp
from jax import lax
from jax.experimental import pallas as pl
from jax.experimental.pallas import tpu as pltpu
from jax.sharding import Mesh
from jax.sharding import PartitionSpec as P

BF = jnp.bfloat16
F32 = jnp.float32
GX = ("yh", "x", "c")
GY = ("yl", "z")
PLANE = ("yh", "x", "yl")
VMEM = pl.BlockSpec(memory_space=pltpu.VMEM)
ANY = pl.BlockSpec(memory_space=pl.ANY)


def dot(left, right):
    return jnp.dot(left, right, preferred_element_type=F32)


def dot_rows(left, right):
    return lax.dot_general(left, right, (((0,), (0,)), ((), ())), preferred_element_type=F32)


def dot_cols(left, right):
    return lax.dot_general(left, right, (((1,), (1,)), ((), ())), preferred_element_type=F32)


def hi_lo(values):
    high = values.astype(BF)
    low = (values - high.astype(F32)).astype(BF)
    return jnp.concatenate([high, low], axis=0)


def fold(values):
    half = values.shape[0] // 2
    return values[:half] + values[half:]


def layer_norm(values):
    mean = jnp.mean(values, axis=-1, keepdims=True)
    centred = values - mean
    scale = lax.rsqrt(jnp.mean(centred * centred, axis=-1, keepdims=True) + 1e-05)
    return centred * scale, scale


def norm_back(grad, normed, scale):
    first = jnp.mean(grad, axis=-1, keepdims=True)
    second = jnp.mean(grad * normed, axis=-1, keepdims=True)
    return scale * (grad - first - normed * second)


def silu_and_slope(values):
    sig = 1.0 / (1.0 + jnp.exp(-values))
    return values * sig, sig * (1.0 + values * (1.0 - sig))


def pick(row, count):
    rows = lax.broadcasted_iota(jnp.int32, (count, row.shape[-1]), 0)
    return jnp.where(rows == row, 1.0, 0.0)


def fetch(sources, targets, sems):
    copies = [
        pltpu.make_async_copy(source, target, sems.at[i])
        for i, (source, target) in enumerate(zip(sources, targets, strict=True))
    ]
    for copy in copies:
        copy.start()

    def ready(i):
        copies[i].wait()
        return targets[i]

    return ready


def parities():
    return lax.axis_index("c"), lax.rem(lax.axis_index("z"), 2)


def side_of(step, row_odd, col_odd):
    return (2 + col_odd, row_odd, 1 - row_odd, 3 - col_odd)[step]


def pack_kernel(nodes_hbm, lists_hbm, *refs):
    packs, (nodes, lists, sems) = refs[:4], refs[4:]
    ready = fetch((nodes_hbm.at[0, 0], lists_hbm.at[0, 0]), (nodes, lists), sems)
    odd = parities()
    ready(1)
    lat = ready(0)[...]
    for step in range(4):
        row = lists[pl.ds(side_of(step, *odd), 1), :]
        packs[step][...] = dot_rows(pick(row, lat.shape[0]).astype(BF), lat).astype(BF)


def layer_kernel(
    nodes_hbm,
    edges_hbm,
    halo0,
    halo1,
    halo2,
    halo3,
    senders_hbm,
    segments_hbm,
    cot_nodes_hbm,
    cot_edges_hbm,
    w_edge1_hbm,
    w_edge2_hbm,
    w_node1_hbm,
    w_node2_hbm,
    node_next,
    grad_edges,
    d_node,
    back0,
    back1,
    back2,
    back3,
    keep,
    send,
    nodes,
    edges,
    senders,
    segments,
    cot_nodes,
    cot_edges,
    w_edge1,
    w_edge2,
    w_node1,
    w_node2,
    ext_twice,
    node_twice,
    a_one,
    agg,
    a_three,
    d_ext,
    sems,
):
    ready = fetch(
        (
            senders_hbm.at[0],
            segments_hbm.at[0],
            nodes_hbm.at[0, 0],
            edges_hbm.at[0, 0],
            w_edge1_hbm,
            w_edge2_hbm,
            w_node1_hbm,
            w_node2_hbm,
            cot_nodes_hbm.at[0, 0],
            cot_edges_hbm.at[0, 0],
        ),
        (
            senders,
            segments,
            nodes,
            edges,
            w_edge1,
            w_edge2,
            w_node1,
            w_node2,
            cot_nodes,
            cot_edges,
        ),
        sems,
    )
    odd = parities()
    width = nodes.shape[1]
    count = nodes.shape[0]
    rows = halo0.shape[0]
    part = width // 2

    def put(block, left, right):
        for target, side in ((send, 1 - odd[0]), (keep, odd[0])):
            columns = pl.ds(pl.multiple_of(side * part, part), part)
            target[block * part : (block + 1) * part, :] = dot_rows(
                left[:, columns], right
            ).astype(BF)

    reach = ext_twice.shape[0] // 2
    by_send = pick(ready(0)[...], reach)
    by_recv = pick(ready(1)[...], count)
    from_ext = by_send.T.astype(BF)
    from_node = by_recv.T.astype(BF)
    to_ext = by_send.astype(BF)
    to_node = by_recv.astype(BF)
    wide = jnp.concatenate([from_ext, from_ext, from_node, from_node], axis=1)

    node = ready(2)[...]
    for start in (0, reach):
        ext_twice[start : start + count, :] = node
        for step, halo in enumerate((halo0, halo1, halo2, halo3)):
            place = start + count + side_of(step, *odd) * rows
            ext_twice[pl.ds(pl.multiple_of(place, rows), rows), :] = halo[...]
    for start in (0, count):
        node_twice[start : start + count, :] = node
    ext = ext_twice[:reach, :]
    edge = ready(3)[...]
    ready(4)

    terms = jnp.concatenate(
        [
            hi_lo(dot(ext, w_edge1[width : 2 * width, :])),
            hi_lo(dot(node, w_edge1[2 * width :, :])),
        ],
        axis=0,
    )
    z_one = dot(edge, w_edge1[:width, :]) + dot(wide, terms)
    act, slope_one = silu_and_slope(z_one)
    a_one[...] = act.astype(BF)
    ready(5)
    n_two, s_two = layer_norm(dot(a_one[...], w_edge2[...]))
    e_new = (edge.astype(F32) + n_two).astype(BF)
    agg[...] = dot(to_node, e_new).astype(BF)
    ready(6)
    z_three = dot(node, w_node1[:width, :]) + dot(agg[...], w_node1[width:, :])
    act, slope_three = silu_and_slope(z_three)
    a_three[...] = act.astype(BF)
    ready(7)
    n_four, s_four = layer_norm(dot(a_three[...], w_node2[...]))
    node_next[0, 0] = (node.astype(F32) + n_four).astype(BF)

    g_node = ready(8)[...].astype(F32)
    dz_four = norm_back(g_node, n_four, s_four).astype(BF)
    dz_three = (dot_cols(dz_four, w_node2[...]) * slope_three).astype(BF)
    dy_node = dot_cols(dz_three, w_node1[:width, :])
    dy_agg = dot_cols(dz_three, w_node1[width:, :])

    twice = jnp.concatenate([from_node, from_node], axis=1)
    de_new = ready(9)[...].astype(F32) + dot(twice, hi_lo(dy_agg))
    dz_two = norm_back(de_new, n_two, s_two).astype(BF)
    dz_one = (dot_cols(dz_two, w_edge2[...]) * slope_one).astype(BF)
    sum_send = hi_lo(dot(to_ext, dz_one))
    sum_recv = hi_lo(dot(to_node, dz_one))
    put(0, edges, dz_one)
    put(1, ext_twice, sum_send)
    put(2, node_twice, sum_recv)
    put(3, a_one, dz_two)
    put(4, nodes, dz_three)
    put(5, agg, dz_three)
    put(6, a_three, dz_four)
    grad_edges[0, 0] = (de_new + dot_cols(dz_one, w_edge1[:width, :])).astype(BF)
    d_ext[...] = fold(dot_cols(sum_send, w_edge1[width : 2 * width, :]))
    d_recv = fold(dot_cols(sum_recv, w_edge1[2 * width :, :]))
    d_node[...] = g_node + dy_node + d_recv + d_ext[:count, :]
    for step, back in enumerate((back0, back1, back2, back3)):
        place = count + side_of(step, *odd) * rows
        back[...] = d_ext[pl.ds(pl.multiple_of(place, rows), rows), :].astype(BF)


def pair_sum_kernel(mine, other, out):
    out[...] = (mine[...].astype(F32) + other[...].astype(F32)).astype(BF)


def plane_sum_kernel(parts, *refs):
    backs, out, onward = refs[:4], refs[4], refs[5:]
    for back, ref in zip(backs, onward, strict=True):
        ref[...] = back[...]
    rows, lanes = out.shape[1], out.shape[2]
    for block in range(out.shape[0]):
        r, c = block % 2 * rows, block // 2 * lanes
        total = parts[0, r : r + rows, c : c + lanes].astype(F32)
        for part in range(1, parts.shape[0]):
            total = total + parts[part, r : r + rows, c : c + lanes].astype(F32)
        out[block] = total.astype(BF)


def line_sum_kernel(factor, parts, out):
    total = parts[0].astype(F32)
    for part in range(1, parts.shape[0]):
        total = total + parts[part].astype(F32)
    total = (total * factor).astype(BF)
    for part in range(out.shape[0]):
        out[part] = total


def spread_kernel(blocks, d_node, lists, ret0, ret1, ret2, ret3, out, grad_nodes):
    tops = jnp.concatenate([blocks[2 * i] for i in range(4)], axis=1)
    ends = jnp.concatenate([blocks[2 * i + 1] for i in range(4)], axis=1)
    whole = jnp.concatenate([tops, ends], axis=0)
    for part in range(out.shape[0]):
        out[part] = whole
    odd = parities()
    total = d_node[...]
    for step, ret in enumerate((ret0, ret1, ret2, ret3)):
        row = lists[0, 0, pl.ds(side_of(step, *odd), 1), :]
        total = total + dot(pick(row, total.shape[0]).astype(BF), ret[...])
    grad_nodes[0, 0] = total.astype(BF)


def place_kernel(other_core, half, *refs):
    outs, sems = refs[-5:-1], refs[-1]
    part = outs[0].shape[1] // 2
    side = lax.axis_index("c")
    side = 1 - side if other_core else side
    copies = []
    for out in outs:
        for block in range(out.shape[0] // (2 * part)):
            place = pl.multiple_of((2 * block + side) * part, part)
            start = len(copies) * part
            copies.append(
                pltpu.make_async_copy(
                    half.at[start : start + part], out.at[pl.ds(place, part)], sems.at[len(copies)]
                )
            )
    for copy in copies:
        copy.start()
    for copy in copies:
        copy.wait()


def call(kernel, outs, ins, limit=24, scratch=(), **kwargs):
    return pl.pallas_call(
        kernel,
        out_shape=outs,
        in_specs=ins,
        out_specs=jax.tree.map(lambda _: VMEM, outs),
        scratch_shapes=list(scratch),
        compiler_params=pltpu.CompilerParams(vmem_limit_bytes=limit << 20),
        **kwargs,
    )


def shape(dims, kind=BF):
    return jax.ShapeDtypeStruct(dims, kind)


def in_hbm(*arrays):
    return [pltpu.with_memory_space_constraint(array, pltpu.HBM) for array in arrays]


def pairs(count, first):
    made = []
    for i in range(first, count + first, 2):
        made += [(i, (i + 1) % count), ((i + 1) % count, i)]
    return made


def exchange(blocks):
    nx, ny = lax.axis_size(GX), lax.axis_size(GY)
    return [
        lax.ppermute(blocks[0], GY, pairs(ny, 1)),
        lax.ppermute(blocks[1], GX, pairs(nx, 1)),
        lax.ppermute(blocks[2], GX, pairs(nx, 0)),
        lax.ppermute(blocks[3], GY, pairs(ny, 0)),
    ]


def local(
    nodes,
    edges,
    senders,
    segments,
    send_lists,
    cot_nodes,
    cot_edges,
    w_edge1,
    w_edge2,
    w_node1,
    w_node2,
):
    count, width = nodes.shape[2:]
    lines = edges.shape[2]
    rows = send_lists.shape[3]
    weights = (w_edge1, w_edge2, w_node1, w_node2)
    total = sum(w.shape[0] for w in weights)
    block = [shape((rows, width))] * 4
    packs = call(
        pack_kernel,
        block,
        [ANY] * 2,
        scratch=[
            pltpu.VMEM((count, width), BF),
            pltpu.VMEM((4, rows), jnp.int32),
            pltpu.SemaphoreType.DMA((2,)),
        ],
    )(*in_hbm(nodes, send_lists))
    halos = exchange(packs)
    half = shape((total // 2, width))
    reach = count + 4 * rows
    node_next, grad_edges, d_node, *backs, keep, send = call(
        layer_kernel,
        [shape(nodes.shape), shape(edges.shape), shape((count, width), F32)] + block + [half] * 2,
        [ANY] * 2 + [VMEM] * 4 + [ANY] * 8,
        limit=28,
        scratch=[
            pltpu.VMEM((count, width), BF),
            pltpu.VMEM((lines, width), BF),
            pltpu.VMEM((1, lines), jnp.int32),
            pltpu.VMEM((1, lines), jnp.int32),
            pltpu.VMEM((count, width), BF),
            pltpu.VMEM((lines, width), BF),
            *[pltpu.VMEM(w.shape, BF) for w in weights],
            pltpu.VMEM((2 * reach, width), BF),
            pltpu.VMEM((2 * count, width), BF),
            pltpu.VMEM((lines, width), BF),
            pltpu.VMEM((count, width), BF),
            pltpu.VMEM((count, width), BF),
            pltpu.VMEM((reach, width), F32),
            pltpu.SemaphoreType.DMA((10,)),
        ],
    )(
        *in_hbm(nodes, edges),
        *halos,
        *in_hbm(senders, segments, cot_nodes, cot_edges, *weights),
    )

    got = lax.ppermute(send, "c", pairs(2, 0))
    pair = call(pair_sum_kernel, half, [VMEM] * 2, limit=8)(keep, got)

    plane, line = lax.axis_size(PLANE), lax.axis_size("z")
    strip = total // 2 // plane
    cut = (line, strip // 2, width * 2 // line)
    pieces = lax.all_to_all(pair, PLANE, 0, 0, tiled=True).reshape(plane, strip, width)
    pieces, *backs = call(plane_sum_kernel, [shape(cut)] + block, [VMEM] * 5, limit=8)(
        pieces, *backs
    )
    returned = exchange(backs)
    pieces = lax.all_to_all(pieces, "z", 0, 0, tiled=True)
    factor = float(lines * plane * line * 2) ** -0.5
    pieces = call(functools.partial(line_sum_kernel, factor), shape(cut), [VMEM], limit=8)(pieces)
    pieces = lax.all_to_all(pieces, "z", 0, 0, tiled=True)
    pieces, grad_nodes = call(
        spread_kernel, [shape((plane, strip, width)), shape(nodes.shape)], [VMEM] * 7, limit=8
    )(pieces, d_node, send_lists, *returned)
    mine = lax.all_to_all(pieces, PLANE, 0, 0, tiled=True).reshape(total // 2, width)
    other = lax.ppermute(mine, "c", pairs(2, 0))
    outs = [shape(w.shape) for w in weights]
    sems = [pltpu.SemaphoreType.DMA((total // width,))]
    grads = pl.pallas_call(
        functools.partial(place_kernel, False),
        out_shape=outs,
        in_specs=[VMEM],
        out_specs=[ANY] * 4,
        scratch_shapes=sems,
        compiler_params=pltpu.CompilerParams(vmem_limit_bytes=4 << 20),
    )(mine)
    grads = pl.pallas_call(
        functools.partial(place_kernel, True),
        out_shape=outs,
        in_specs=[VMEM] + [ANY] * 4,
        out_specs=[ANY] * 4,
        scratch_shapes=sems,
        compiler_params=pltpu.CompilerParams(vmem_limit_bytes=4 << 20),
        input_output_aliases={1: 0, 2: 1, 3: 2, 4: 3},
    )(other, *grads)
    return (node_next, grad_nodes, grad_edges, *grads)


def solution(mesh):
    fine = Mesh(mesh.devices.reshape(2, 4, 2, 2, 8), ("yh", "x", "c", "yl", "z"))
    tile = P(GX, GY)
    return jax.shard_map(
        local,
        mesh=fine,
        in_specs=(tile,) * 7 + (P(),) * 4,
        out_specs=(tile,) * 3 + (P(),) * 4,
        check_vma=False,
    )
```

```python
import functools

import jax
import jax.numpy as jnp
from jax import lax
from jax.experimental import pallas as pl
from jax.experimental.pallas import tpu as pltpu
from jax.sharding import Mesh
from jax.sharding import PartitionSpec as P

BF = jnp.bfloat16
F32 = jnp.float32
GX = ("yh", "x", "c")
GY = ("yl", "z")
PLANE = ("yh", "x", "yl")
VMEM = pl.BlockSpec(memory_space=pltpu.VMEM)
ANY = pl.BlockSpec(memory_space=pl.ANY)


def dot(left, right):
    return jnp.dot(left, right, preferred_element_type=F32)


def dot_rows(left, right):
    return lax.dot_general(left, right, (((0,), (0,)), ((), ())), preferred_element_type=F32)


def dot_cols(left, right):
    return lax.dot_general(left, right, (((1,), (1,)), ((), ())), preferred_element_type=F32)


def hi_lo(values):
    high = values.astype(BF)
    low = (values - high.astype(F32)).astype(BF)
    return jnp.concatenate([high, low], axis=0)


def fold(values):
    half = values.shape[0] // 2
    return values[:half] + values[half:]


def layer_norm(values):
    mean = jnp.mean(values, axis=-1, keepdims=True)
    centred = values - mean
    scale = lax.rsqrt(jnp.mean(centred * centred, axis=-1, keepdims=True) + 1e-05)
    return centred * scale, scale


def norm_back(grad, normed, scale):
    first = jnp.mean(grad, axis=-1, keepdims=True)
    second = jnp.mean(grad * normed, axis=-1, keepdims=True)
    return scale * (grad - first - normed * second)


def silu_and_slope(values):
    sig = 1.0 / (1.0 + jnp.exp(-values))
    return values * sig, sig * (1.0 + values * (1.0 - sig))


def pick(row, count):
    rows = lax.broadcasted_iota(jnp.int32, (count, row.shape[-1]), 0)
    return jnp.where(rows == row, 1.0, 0.0)


def fetch(sources, targets, sems):
    copies = [
        pltpu.make_async_copy(source, target, sems.at[i])
        for i, (source, target) in enumerate(zip(sources, targets, strict=True))
    ]
    for copy in copies:
        copy.start()

    def ready(i):
        copies[i].wait()
        return targets[i]

    return ready


def parities():
    return lax.axis_index("c"), lax.rem(lax.axis_index("z"), 2)


def side_of(step, row_odd, col_odd):
    return (2 + col_odd, row_odd, 1 - row_odd, 3 - col_odd)[step]


def pack_kernel(nodes_hbm, lists_hbm, *refs):
    packs, (nodes, lists, sems) = refs[:4], refs[4:]
    ready = fetch((nodes_hbm.at[0, 0], lists_hbm.at[0, 0]), (nodes, lists), sems)
    odd = parities()
    ready(1)
    lat = ready(0)[...]
    for step in range(4):
        row = lists[pl.ds(side_of(step, *odd), 1), :]
        packs[step][...] = dot_rows(pick(row, lat.shape[0]).astype(BF), lat).astype(BF)


def load_kernel(
    packs,
    nodes_hbm,
    edges_hbm,
    senders_hbm,
    segments_hbm,
    cot_nodes_hbm,
    cot_edges_hbm,
    w_edge1_hbm,
    w_edge2_hbm,
    w_node1_hbm,
    w_node2_hbm,
    node,
    edge,
    cot_node,
    cot_edge,
    w_edge1,
    w_edge2,
    w_node1,
    w_node2,
    to_ext,
    to_node,
    from_node,
    from_halo,
    z_part,
    senders,
    segments,
    sems,
):
    del packs
    ready = fetch(
        (
            senders_hbm.at[0],
            segments_hbm.at[0],
            nodes_hbm.at[0, 0],
            w_edge1_hbm,
            edges_hbm.at[0, 0],
            w_edge2_hbm,
            w_node1_hbm,
            w_node2_hbm,
            cot_nodes_hbm.at[0, 0],
            cot_edges_hbm.at[0, 0],
        ),
        (
            senders,
            segments,
            node,
            w_edge1,
            edge,
            w_edge2,
            w_node1,
            w_node2,
            cot_node,
            cot_edge,
        ),
        sems,
    )
    count, width = node.shape
    by_send = pick(ready(0)[...], to_ext.shape[0])
    by_recv = pick(ready(1)[...], count)
    to_ext[...] = by_send.astype(BF)
    to_node[...] = by_recv.astype(BF)
    own = by_send[:count].T.astype(BF)
    halo = by_send[count:].T.astype(BF)
    recv = by_recv.T.astype(BF)
    from_halo[...] = jnp.concatenate([halo, halo], axis=1)
    from_node[...] = jnp.concatenate([recv, recv], axis=1)
    wide = jnp.concatenate([own, own, recv, recv], axis=1)
    lat = ready(2)[...]
    ready(3)
    terms = jnp.concatenate(
        [
            hi_lo(dot(lat, w_edge1[width : 2 * width, :])),
            hi_lo(dot(lat, w_edge1[2 * width :, :])),
        ],
        axis=0,
    )
    z_part[...] = dot(ready(4)[...], w_edge1[:width, :]) + dot(wide, terms)
    for i in range(5, 10):
        ready(i)


def put_half(target, side, pairs_of_block):
    for block, (left, right) in enumerate(pairs_of_block):
        part = left.shape[1] // 2
        columns = pl.ds(pl.multiple_of(side * part, part), part)
        target[block * part : (block + 1) * part, :] = dot_rows(
            left[:, columns], right[...]
        ).astype(BF)


def layer_kernel(
    halo0,
    halo1,
    halo2,
    halo3,
    node,
    edge,
    cot_node,
    cot_edge,
    w_edge1,
    w_edge2,
    w_node1,
    w_node2,
    to_ext,
    to_node,
    from_node,
    from_halo,
    z_part,
    node_next,
    send,
    ext_twice,
    node_twice,
    a_one,
    agg,
    a_three,
    dz_one,
    dz_two,
    dz_three,
    dz_four,
    sum_send,
    sum_recv,
    de_new,
    dn_part,
):
    odd = parities()
    count, width = node.shape
    rows = halo0.shape[0]
    reach = ext_twice.shape[0] // 2
    lat = node[...]
    for start in (0, reach):
        ext_twice[start : start + count, :] = lat
        for step, halo in enumerate((halo0, halo1, halo2, halo3)):
            place = start + count + side_of(step, *odd) * rows
            ext_twice[pl.ds(pl.multiple_of(place, rows), rows), :] = halo[...]
    for start in (0, count):
        node_twice[start : start + count, :] = lat

    terms = hi_lo(dot(ext_twice[count:reach, :], w_edge1[width : 2 * width, :]))
    z_one = z_part[...] + dot(from_halo[...], terms)
    act, slope_one = silu_and_slope(z_one)
    a_one[...] = act.astype(BF)
    n_two, s_two = layer_norm(dot(a_one[...], w_edge2[...]))
    e_new = (edge[...].astype(F32) + n_two).astype(BF)
    agg[...] = dot(to_node[...], e_new).astype(BF)
    z_three = dot(lat, w_node1[:width, :]) + dot(agg[...], w_node1[width:, :])
    act, slope_three = silu_and_slope(z_three)
    a_three[...] = act.astype(BF)
    n_four, s_four = layer_norm(dot(a_three[...], w_node2[...]))
    node_next[0, 0] = (lat.astype(F32) + n_four).astype(BF)

    g_node = cot_node[...].astype(F32)
    dz_four[...] = norm_back(g_node, n_four, s_four).astype(BF)
    dz_three[...] = (dot_cols(dz_four[...], w_node2[...]) * slope_three).astype(BF)
    dn_part[...] = g_node + dot_cols(dz_three[...], w_node1[:width, :])
    dy_agg = dot_cols(dz_three[...], w_node1[width:, :])

    de = cot_edge[...].astype(F32) + dot(from_node[...], hi_lo(dy_agg))
    de_new[...] = de
    dz_two[...] = norm_back(de, n_two, s_two).astype(BF)
    dz_one[...] = (dot_cols(dz_two[...], w_edge2[...]) * slope_one).astype(BF)
    sum_send[...] = hi_lo(dot(to_ext[...], dz_one[...]))
    sum_recv[...] = hi_lo(dot(to_node[...], dz_one[...]))
    put_half(
        send,
        1 - odd[0],
        (
            (edge, dz_one),
            (ext_twice, sum_send),
            (node_twice, sum_recv),
            (a_one, dz_two),
            (node, dz_three),
            (agg, dz_three),
            (a_three, dz_four),
        ),
    )


def rest_kernel(
    node,
    edge,
    w_edge1,
    ext_twice,
    node_twice,
    a_one,
    agg,
    a_three,
    dz_one,
    dz_two,
    dz_three,
    dz_four,
    sum_send,
    sum_recv,
    de_new,
    dn_part,
    keep,
    grad_edges,
    d_node,
    back0,
    back1,
    back2,
    back3,
    d_ext,
):
    odd = parities()
    count, width = node.shape
    rows = back0.shape[0]
    put_half(
        keep,
        odd[0],
        (
            (edge, dz_one),
            (ext_twice, sum_send),
            (node_twice, sum_recv),
            (a_one, dz_two),
            (node, dz_three),
            (agg, dz_three),
            (a_three, dz_four),
        ),
    )
    grad_edges[0, 0] = (de_new[...] + dot_cols(dz_one[...], w_edge1[:width, :])).astype(BF)
    d_ext[...] = fold(dot_cols(sum_send[...], w_edge1[width : 2 * width, :]))
    d_recv = fold(dot_cols(sum_recv[...], w_edge1[2 * width :, :]))
    d_node[...] = dn_part[...] + d_recv + d_ext[:count, :]
    for step, back in enumerate((back0, back1, back2, back3)):
        place = count + side_of(step, *odd) * rows
        back[...] = d_ext[pl.ds(pl.multiple_of(place, rows), rows), :].astype(BF)


def pair_sum_kernel(mine, other, out):
    out[...] = (mine[...].astype(F32) + other[...].astype(F32)).astype(BF)


def plane_sum_kernel(parts, *refs):
    backs, out, onward = refs[:4], refs[4], refs[5:]
    for back, ref in zip(backs, onward, strict=True):
        ref[...] = back[...]
    total = parts[0].astype(F32)
    for part in range(1, parts.shape[0]):
        total = total + parts[part].astype(F32)
    total = total.astype(BF)
    for part in range(out.shape[0]):
        out[part] = total


def line_sum_kernel(factor, parts, d_node, lists, ret0, ret1, ret2, ret3, out, grad_nodes):
    total = parts[0].astype(F32)
    for part in range(1, parts.shape[0]):
        total = total + parts[part].astype(F32)
    total = (total * factor).astype(BF)
    for part in range(out.shape[0]):
        out[part] = total
    odd = parities()
    grad = d_node[...]
    for step, ret in enumerate((ret0, ret1, ret2, ret3)):
        row = lists[0, 0, pl.ds(side_of(step, *odd), 1), :]
        grad = grad + dot(pick(row, grad.shape[0]).astype(BF), ret[...])
    grad_nodes[0, 0] = grad.astype(BF)


def place_kernel(other_core, half, *refs):
    outs, sems = refs[-5:-1], refs[-1]
    part = outs[0].shape[1] // 2
    side = lax.axis_index("c")
    side = 1 - side if other_core else side
    copies = []
    for out in outs:
        for block in range(out.shape[0] // (2 * part)):
            place = pl.multiple_of((2 * block + side) * part, part)
            start = len(copies) * part
            copies.append(
                pltpu.make_async_copy(
                    half.at[start : start + part], out.at[pl.ds(place, part)], sems.at[len(copies)]
                )
            )
    for copy in copies:
        copy.start()
    for copy in copies:
        copy.wait()


def call(kernel, outs, ins, limit=24, scratch=(), **kwargs):
    return pl.pallas_call(
        kernel,
        out_shape=outs,
        in_specs=ins,
        out_specs=jax.tree.map(lambda _: VMEM, outs),
        scratch_shapes=list(scratch),
        compiler_params=pltpu.CompilerParams(vmem_limit_bytes=limit << 20),
        **kwargs,
    )


def shape(dims, kind=BF):
    return jax.ShapeDtypeStruct(dims, kind)


def in_hbm(*arrays):
    return [pltpu.with_memory_space_constraint(array, pltpu.HBM) for array in arrays]


def pairs(count, first):
    made = []
    for i in range(first, count + first, 2):
        made += [(i, (i + 1) % count), ((i + 1) % count, i)]
    return made


def exchange(blocks):
    nx, ny = lax.axis_size(GX), lax.axis_size(GY)
    return [
        lax.ppermute(blocks[0], GY, pairs(ny, 1)),
        lax.ppermute(blocks[1], GX, pairs(nx, 1)),
        lax.ppermute(blocks[2], GX, pairs(nx, 0)),
        lax.ppermute(blocks[3], GY, pairs(ny, 0)),
    ]


def load(packs, nodes, edges, senders, segments, cot_nodes, cot_edges, weights):
    count, width = nodes.shape[2:]
    lines = edges.shape[2]
    reach = count + 4 * packs.shape[0]
    return call(
        load_kernel,
        [shape((count, width)), shape((lines, width))] * 2
        + [shape(w.shape) for w in weights]
        + [shape((reach, lines)), shape((count, lines))]
        + [shape((lines, 2 * count)), shape((lines, 2 * (reach - count)))]
        + [shape((lines, width), F32)],
        [VMEM] + [ANY] * 10,
        limit=12,
        scratch=[
            pltpu.VMEM((1, lines), jnp.int32),
            pltpu.VMEM((1, lines), jnp.int32),
            pltpu.SemaphoreType.DMA((10,)),
        ],
    )(packs, *in_hbm(nodes, edges, senders, segments, cot_nodes, cot_edges, *weights))


def layer(halos, loaded):
    node, edge, w_edge1 = loaded[0], loaded[1], loaded[4]
    (count, width), lines, rows = node.shape, edge.shape[0], halos[0].shape[0]
    reach = count + 4 * rows
    half = shape((sum(w.shape[0] for w in loaded[4:8]) // 2, width))
    on_edges, on_nodes = shape((lines, width)), shape((count, width))
    node_next, send, *state = call(
        layer_kernel,
        [shape((1, 1, count, width)), half]
        + [shape((2 * reach, width)), shape((2 * count, width)), on_edges, on_nodes, on_nodes]
        + [on_edges, on_edges, on_nodes, on_nodes]
        + [shape((2 * reach, width)), shape((2 * count, width))]
        + [shape((lines, width), F32), shape((count, width), F32)],
        [VMEM] * (4 + len(loaded)),
        limit=16,
    )(*halos, *loaded)
    keep, grad_edges, d_node, *backs = call(
        rest_kernel,
        [half, shape((1, 1, lines, width)), shape((count, width), F32)] + [shape((rows, width))] * 4,
        [VMEM] * (3 + len(state)),
        limit=12,
        scratch=[pltpu.VMEM((reach, width), F32)],
        cost_estimate=pl.CostEstimate(
            flops=2 * width * width * (4 * lines + 8 * reach),
            bytes_accessed=12 << 20,
            transcendentals=0,
        ),
    )(node, edge, w_edge1, *state)
    return node_next, send, keep, grad_edges, d_node, backs


def local(
    nodes,
    edges,
    senders,
    segments,
    send_lists,
    cot_nodes,
    cot_edges,
    w_edge1,
    w_edge2,
    w_node1,
    w_node2,
):
    count, width = nodes.shape[2:]
    lines = edges.shape[2]
    rows = send_lists.shape[3]
    weights = (w_edge1, w_edge2, w_node1, w_node2)
    total = sum(w.shape[0] for w in weights)
    block = [shape((rows, width))] * 4
    packs = call(
        pack_kernel,
        block,
        [ANY] * 2,
        scratch=[
            pltpu.VMEM((count, width), BF),
            pltpu.VMEM((4, rows), jnp.int32),
            pltpu.SemaphoreType.DMA((2,)),
        ],
    )(*in_hbm(nodes, send_lists))
    halos = exchange(packs)
    loaded = load(packs[0], nodes, edges, senders, segments, cot_nodes, cot_edges, weights)
    node_next, send, keep, grad_edges, d_node, backs = layer(halos, loaded)

    got = lax.ppermute(send, "c", pairs(2, 0))
    pair = call(pair_sum_kernel, shape(keep.shape), [VMEM] * 2, limit=8)(keep, got)

    plane, line = lax.axis_size(PLANE), lax.axis_size("z")
    strip = total // 2 // plane
    pieces = lax.all_to_all(pair, PLANE, 0, 0, tiled=True).reshape(plane, strip, width)
    pieces, *backs = call(
        plane_sum_kernel, [shape((line, strip, width))] + block, [VMEM] * 5, limit=8
    )(pieces, *backs)
    returned = exchange(backs)
    pieces = lax.all_to_all(pieces, "z", 0, 0, tiled=True)
    factor = float(lines * plane * line * 2) ** -0.5
    pieces, grad_nodes = call(
        functools.partial(line_sum_kernel, factor),
        [shape((plane, strip, width)), shape(nodes.shape)],
        [VMEM] * 7,
        limit=8,
    )(pieces, d_node, send_lists, *returned)
    mine = lax.all_to_all(pieces, PLANE, 0, 0, tiled=True).reshape(total // 2, width)
    other = lax.ppermute(mine, "c", pairs(2, 0))
    outs = [shape(w.shape) for w in weights]
    sems = [pltpu.SemaphoreType.DMA((total // width,))]
    grads = pl.pallas_call(
        functools.partial(place_kernel, False),
        out_shape=outs,
        in_specs=[VMEM],
        out_specs=[ANY] * 4,
        scratch_shapes=sems,
        compiler_params=pltpu.CompilerParams(vmem_limit_bytes=4 << 20),
    )(mine)
    grads = pl.pallas_call(
        functools.partial(place_kernel, True),
        out_shape=outs,
        in_specs=[VMEM] + [ANY] * 4,
        out_specs=[ANY] * 4,
        scratch_shapes=sems,
        compiler_params=pltpu.CompilerParams(vmem_limit_bytes=4 << 20),
        input_output_aliases={1: 0, 2: 1, 3: 2, 4: 3},
    )(other, *grads)
    return (node_next, grad_nodes, grad_edges, *grads)


def solution(mesh):
    fine = Mesh(mesh.devices.reshape(2, 4, 2, 2, 8), ("yh", "x", "c", "yl", "z"))
    tile = P(GX, GY)
    return jax.shard_map(
        local,
        mesh=fine,
        in_specs=(tile,) * 7 + (P(),) * 4,
        out_specs=(tile,) * 3 + (P(),) * 4,
        check_vma=False,
    )
```

```python
import functools

import jax
import jax.numpy as jnp
from jax import lax
from jax.experimental import pallas as pl
from jax.experimental.pallas import tpu as pltpu
from jax.sharding import Mesh
from jax.sharding import PartitionSpec as P

BF = jnp.bfloat16
F32 = jnp.float32
GX = ("yh", "x", "c")
GY = ("yl", "zh", "zl")
NEAR = ("yh", "x", "yl", "zl")
FAR = "zh"
VMEM = pl.BlockSpec(memory_space=pltpu.VMEM)
ANY = pl.BlockSpec(memory_space=pl.ANY)


def dot(left, right):
    return jnp.dot(left, right, preferred_element_type=F32)


def dot_rows(left, right):
    return lax.dot_general(left, right, (((0,), (0,)), ((), ())), preferred_element_type=F32)


def dot_cols(left, right):
    return lax.dot_general(left, right, (((1,), (1,)), ((), ())), preferred_element_type=F32)


def hi_lo(values):
    high = values.astype(BF)
    low = (values - high.astype(F32)).astype(BF)
    return jnp.concatenate([high, low], axis=0)


def fold(values):
    half = values.shape[0] // 2
    return values[:half] + values[half:]


def layer_norm(values):
    mean = jnp.mean(values, axis=-1, keepdims=True)
    centred = values - mean
    scale = lax.rsqrt(jnp.mean(centred * centred, axis=-1, keepdims=True) + 1e-05)
    return centred * scale, scale


def norm_back(grad, normed, scale):
    first = jnp.mean(grad, axis=-1, keepdims=True)
    second = jnp.mean(grad * normed, axis=-1, keepdims=True)
    return scale * (grad - first - normed * second)


def silu_and_slope(values):
    sig = 1.0 / (1.0 + jnp.exp(-values))
    return values * sig, sig * (1.0 + values * (1.0 - sig))


def pick(row, count):
    rows = lax.broadcasted_iota(jnp.int32, (count, row.shape[-1]), 0)
    return jnp.where(rows == row, 1.0, 0.0)


def fetch(sources, targets, sems):
    copies = [
        pltpu.make_async_copy(source, target, sems.at[i])
        for i, (source, target) in enumerate(zip(sources, targets, strict=True))
    ]
    for copy in copies:
        copy.start()

    def ready(i):
        copies[i].wait()
        return targets[i]

    return ready


def parities():
    return lax.axis_index("c"), lax.axis_index("zl")


def side_of(step, row_odd, col_odd):
    return (2 + col_odd, row_odd, 1 - row_odd, 3 - col_odd)[step]


def pack_kernel(nodes_hbm, lists_hbm, *refs):
    packs, (nodes, lists, sems) = refs[:4], refs[4:]
    ready = fetch((nodes_hbm.at[0, 0], lists_hbm.at[0, 0]), (nodes, lists), sems)
    odd = parities()
    ready(1)
    lat = ready(0)[...]
    for step in range(4):
        row = lists[pl.ds(side_of(step, *odd), 1), :]
        packs[step][...] = dot_rows(pick(row, lat.shape[0]).astype(BF), lat).astype(BF)


def load_kernel(
    packs,
    nodes_hbm,
    edges_hbm,
    senders_hbm,
    segments_hbm,
    cot_nodes_hbm,
    cot_edges_hbm,
    w_edge1_hbm,
    w_edge2_hbm,
    w_node1_hbm,
    w_node2_hbm,
    node,
    edge,
    cot_node,
    cot_edge,
    w_edge1,
    w_edge2,
    w_node1,
    w_node2,
    to_ext,
    to_node,
    from_node,
    from_halo,
    z_part,
    senders,
    segments,
    sems,
):
    del packs
    ready = fetch(
        (
            senders_hbm.at[0],
            segments_hbm.at[0],
            nodes_hbm.at[0, 0],
            w_edge1_hbm,
            edges_hbm.at[0, 0],
            w_edge2_hbm,
            w_node1_hbm,
            w_node2_hbm,
            cot_nodes_hbm.at[0, 0],
            cot_edges_hbm.at[0, 0],
        ),
        (
            senders,
            segments,
            node,
            w_edge1,
            edge,
            w_edge2,
            w_node1,
            w_node2,
            cot_node,
            cot_edge,
        ),
        sems,
    )
    count, width = node.shape
    by_send = pick(ready(0)[...], to_ext.shape[0])
    by_recv = pick(ready(1)[...], count)
    to_ext[...] = by_send.astype(BF)
    to_node[...] = by_recv.astype(BF)
    own = by_send[:count].T.astype(BF)
    halo = by_send[count:].T.astype(BF)
    recv = by_recv.T.astype(BF)
    from_halo[...] = jnp.concatenate([halo, halo], axis=1)
    from_node[...] = jnp.concatenate([recv, recv], axis=1)
    wide = jnp.concatenate([own, own, recv, recv], axis=1)
    lat = ready(2)[...]
    ready(3)
    terms = jnp.concatenate(
        [
            hi_lo(dot(lat, w_edge1[width : 2 * width, :])),
            hi_lo(dot(lat, w_edge1[2 * width :, :])),
        ],
        axis=0,
    )
    z_part[...] = dot(ready(4)[...], w_edge1[:width, :]) + dot(wide, terms)
    for i in range(5, 10):
        ready(i)


def put_half(target, side, pairs_of_block):
    for block, (left, right) in enumerate(pairs_of_block):
        part = left.shape[1] // 2
        columns = pl.ds(pl.multiple_of(side * part, part), part)
        target[block * part : (block + 1) * part, :] = dot_rows(
            left[:, columns], right[...]
        ).astype(BF)


def layer_kernel(
    halo0,
    halo1,
    halo2,
    halo3,
    node,
    edge,
    cot_node,
    cot_edge,
    w_edge1,
    w_edge2,
    w_node1,
    w_node2,
    to_ext,
    to_node,
    from_node,
    from_halo,
    z_part,
    node_next,
    send,
    ext_twice,
    node_twice,
    a_one,
    agg,
    a_three,
    dz_one,
    dz_two,
    dz_three,
    dz_four,
    sum_send,
    sum_recv,
    de_new,
    dn_part,
):
    odd = parities()
    count, width = node.shape
    rows = halo0.shape[0]
    reach = ext_twice.shape[0] // 2
    lat = node[...]
    for start in (0, reach):
        ext_twice[start : start + count, :] = lat
        for step, halo in enumerate((halo0, halo1, halo2, halo3)):
            place = start + count + side_of(step, *odd) * rows
            ext_twice[pl.ds(pl.multiple_of(place, rows), rows), :] = halo[...]
    for start in (0, count):
        node_twice[start : start + count, :] = lat

    terms = hi_lo(dot(ext_twice[count:reach, :], w_edge1[width : 2 * width, :]))
    z_one = z_part[...] + dot(from_halo[...], terms)
    act, slope_one = silu_and_slope(z_one)
    a_one[...] = act.astype(BF)
    n_two, s_two = layer_norm(dot(a_one[...], w_edge2[...]))
    e_new = (edge[...].astype(F32) + n_two).astype(BF)
    agg[...] = dot(to_node[...], e_new).astype(BF)
    z_three = dot(lat, w_node1[:width, :]) + dot(agg[...], w_node1[width:, :])
    act, slope_three = silu_and_slope(z_three)
    a_three[...] = act.astype(BF)
    n_four, s_four = layer_norm(dot(a_three[...], w_node2[...]))
    node_next[0, 0] = (lat.astype(F32) + n_four).astype(BF)

    g_node = cot_node[...].astype(F32)
    dz_four[...] = norm_back(g_node, n_four, s_four).astype(BF)
    dz_three[...] = (dot_cols(dz_four[...], w_node2[...]) * slope_three).astype(BF)
    dn_part[...] = g_node + dot_cols(dz_three[...], w_node1[:width, :])
    dy_agg = dot_cols(dz_three[...], w_node1[width:, :])

    de = cot_edge[...].astype(F32) + dot(from_node[...], hi_lo(dy_agg))
    de_new[...] = de
    dz_two[...] = norm_back(de, n_two, s_two).astype(BF)
    dz_one[...] = (dot_cols(dz_two[...], w_edge2[...]) * slope_one).astype(BF)
    sum_send[...] = hi_lo(dot(to_ext[...], dz_one[...]))
    sum_recv[...] = hi_lo(dot(to_node[...], dz_one[...]))
    put_half(
        send,
        1 - odd[0],
        (
            (edge, dz_one),
            (ext_twice, sum_send),
            (node_twice, sum_recv),
            (a_one, dz_two),
            (node, dz_three),
            (agg, dz_three),
            (a_three, dz_four),
        ),
    )


def rest_kernel(
    node,
    edge,
    w_edge1,
    ext_twice,
    node_twice,
    a_one,
    agg,
    a_three,
    dz_one,
    dz_two,
    dz_three,
    dz_four,
    sum_send,
    sum_recv,
    de_new,
    dn_part,
    keep,
    grad_edges,
    d_node,
    back0,
    back1,
    back2,
    back3,
    d_ext,
):
    odd = parities()
    count, width = node.shape
    rows = back0.shape[0]
    put_half(
        keep,
        odd[0],
        (
            (edge, dz_one),
            (ext_twice, sum_send),
            (node_twice, sum_recv),
            (a_one, dz_two),
            (node, dz_three),
            (agg, dz_three),
            (a_three, dz_four),
        ),
    )
    grad_edges[0, 0] = (de_new[...] + dot_cols(dz_one[...], w_edge1[:width, :])).astype(BF)
    d_ext[...] = fold(dot_cols(sum_send[...], w_edge1[width : 2 * width, :]))
    d_recv = fold(dot_cols(sum_recv[...], w_edge1[2 * width :, :]))
    d_node[...] = dn_part[...] + d_recv + d_ext[:count, :]
    for step, back in enumerate((back0, back1, back2, back3)):
        place = count + side_of(step, *odd) * rows
        back[...] = d_ext[pl.ds(pl.multiple_of(place, rows), rows), :].astype(BF)


def pair_sum_kernel(mine, other, out):
    out[...] = (mine[...].astype(F32) + other[...].astype(F32)).astype(BF)


def near_sum_kernel(parts, *refs):
    backs, out, onward = refs[:4], refs[4], refs[5:]
    for back, ref in zip(backs, onward, strict=True):
        ref[...] = back[...]
    total = parts[0].astype(F32)
    for part in range(1, parts.shape[0]):
        total = total + parts[part].astype(F32)
    total = total.astype(BF)
    for part in range(out.shape[0]):
        out[part] = total


def far_sum_kernel(factor, parts, d_node, lists, ret0, ret1, ret2, ret3, out, grad_nodes):
    total = parts[0].astype(F32)
    for part in range(1, parts.shape[0]):
        total = total + parts[part].astype(F32)
    total = (total * factor).astype(BF)
    for part in range(out.shape[0]):
        out[part] = total
    odd = parities()
    grad = d_node[...]
    for step, ret in enumerate((ret0, ret1, ret2, ret3)):
        row = lists[0, 0, pl.ds(side_of(step, *odd), 1), :]
        grad = grad + dot(pick(row, grad.shape[0]).astype(BF), ret[...])
    grad_nodes[0, 0] = grad.astype(BF)


def place_kernel(other_core, half, *refs):
    outs, sems = refs[-5:-1], refs[-1]
    part = outs[0].shape[1] // 2
    side = lax.axis_index("c")
    side = 1 - side if other_core else side
    copies = []
    for out in outs:
        for block in range(out.shape[0] // (2 * part)):
            place = pl.multiple_of((2 * block + side) * part, part)
            start = len(copies) * part
            copies.append(
                pltpu.make_async_copy(
                    half.at[start : start + part], out.at[pl.ds(place, part)], sems.at[len(copies)]
                )
            )
    for copy in copies:
        copy.start()
    for copy in copies:
        copy.wait()


def call(kernel, outs, ins, limit=24, scratch=(), **kwargs):
    return pl.pallas_call(
        kernel,
        out_shape=outs,
        in_specs=ins,
        out_specs=jax.tree.map(lambda _: VMEM, outs),
        scratch_shapes=list(scratch),
        compiler_params=pltpu.CompilerParams(vmem_limit_bytes=limit << 20),
        **kwargs,
    )


def shape(dims, kind=BF):
    return jax.ShapeDtypeStruct(dims, kind)


def in_hbm(*arrays):
    return [pltpu.with_memory_space_constraint(array, pltpu.HBM) for array in arrays]


def pairs(count, first):
    made = []
    for i in range(first, count + first, 2):
        made += [(i, (i + 1) % count), ((i + 1) % count, i)]
    return made


def exchange(blocks):
    nx, ny = lax.axis_size(GX), lax.axis_size(GY)
    return [
        lax.ppermute(blocks[0], GY, pairs(ny, 1)),
        lax.ppermute(blocks[1], GX, pairs(nx, 1)),
        lax.ppermute(blocks[2], GX, pairs(nx, 0)),
        lax.ppermute(blocks[3], GY, pairs(ny, 0)),
    ]


def load(packs, nodes, edges, senders, segments, cot_nodes, cot_edges, weights):
    count, width = nodes.shape[2:]
    lines = edges.shape[2]
    reach = count + 4 * packs.shape[0]
    return call(
        load_kernel,
        [shape((count, width)), shape((lines, width))] * 2
        + [shape(w.shape) for w in weights]
        + [shape((reach, lines)), shape((count, lines))]
        + [shape((lines, 2 * count)), shape((lines, 2 * (reach - count)))]
        + [shape((lines, width), F32)],
        [VMEM] + [ANY] * 10,
        limit=12,
        scratch=[
            pltpu.VMEM((1, lines), jnp.int32),
            pltpu.VMEM((1, lines), jnp.int32),
            pltpu.SemaphoreType.DMA((10,)),
        ],
    )(packs, *in_hbm(nodes, edges, senders, segments, cot_nodes, cot_edges, *weights))


def layer(halos, loaded):
    node, edge, w_edge1 = loaded[0], loaded[1], loaded[4]
    (count, width), lines, rows = node.shape, edge.shape[0], halos[0].shape[0]
    reach = count + 4 * rows
    half = shape((sum(w.shape[0] for w in loaded[4:8]) // 2, width))
    on_edges, on_nodes = shape((lines, width)), shape((count, width))
    node_next, send, *state = call(
        layer_kernel,
        [shape((1, 1, count, width)), half]
        + [shape((2 * reach, width)), shape((2 * count, width)), on_edges, on_nodes, on_nodes]
        + [on_edges, on_edges, on_nodes, on_nodes]
        + [shape((2 * reach, width)), shape((2 * count, width))]
        + [shape((lines, width), F32), shape((count, width), F32)],
        [VMEM] * (4 + len(loaded)),
        limit=16,
    )(*halos, *loaded)
    keep, grad_edges, d_node, *backs = call(
        rest_kernel,
        [half, shape((1, 1, lines, width)), shape((count, width), F32)] + [shape((rows, width))] * 4,
        [VMEM] * (3 + len(state)),
        limit=12,
        scratch=[pltpu.VMEM((reach, width), F32)],
        cost_estimate=pl.CostEstimate(
            flops=2 * width * width * (4 * lines + 8 * reach),
            bytes_accessed=12 << 20,
            transcendentals=0,
        ),
    )(node, edge, w_edge1, *state)
    return node_next, send, keep, grad_edges, d_node, backs


def local(
    nodes,
    edges,
    senders,
    segments,
    send_lists,
    cot_nodes,
    cot_edges,
    w_edge1,
    w_edge2,
    w_node1,
    w_node2,
):
    count, width = nodes.shape[2:]
    lines = edges.shape[2]
    rows = send_lists.shape[3]
    weights = (w_edge1, w_edge2, w_node1, w_node2)
    total = sum(w.shape[0] for w in weights)
    block = [shape((rows, width))] * 4
    packs = call(
        pack_kernel,
        block,
        [ANY] * 2,
        scratch=[
            pltpu.VMEM((count, width), BF),
            pltpu.VMEM((4, rows), jnp.int32),
            pltpu.SemaphoreType.DMA((2,)),
        ],
    )(*in_hbm(nodes, send_lists))
    halos = exchange(packs)
    loaded = load(packs[0], nodes, edges, senders, segments, cot_nodes, cot_edges, weights)
    node_next, send, keep, grad_edges, d_node, backs = layer(halos, loaded)

    got = lax.ppermute(send, "c", pairs(2, 0))
    pair = call(pair_sum_kernel, shape(keep.shape), [VMEM] * 2, limit=8)(keep, got)

    near, far = lax.axis_size(NEAR), lax.axis_size(FAR)
    strip = total // 2 // near
    pieces = lax.all_to_all(pair, NEAR, 0, 0, tiled=True).reshape(near, strip, width)
    pieces, *backs = call(
        near_sum_kernel, [shape((far, strip, width))] + block, [VMEM] * 5, limit=8
    )(pieces, *backs)
    returned = exchange(backs)
    pieces = lax.all_to_all(pieces, FAR, 0, 0, tiled=True)
    factor = float(lines * near * far * 2) ** -0.5
    pieces, grad_nodes = call(
        functools.partial(far_sum_kernel, factor),
        [shape((near, strip, width)), shape(nodes.shape)],
        [VMEM] * 7,
        limit=8,
    )(pieces, d_node, send_lists, *returned)
    mine = lax.all_to_all(pieces, NEAR, 0, 0, tiled=True).reshape(total // 2, width)
    other = lax.ppermute(mine, "c", pairs(2, 0))
    outs = [shape(w.shape) for w in weights]
    sems = [pltpu.SemaphoreType.DMA((total // width,))]
    grads = pl.pallas_call(
        functools.partial(place_kernel, False),
        out_shape=outs,
        in_specs=[VMEM],
        out_specs=[ANY] * 4,
        scratch_shapes=sems,
        compiler_params=pltpu.CompilerParams(vmem_limit_bytes=4 << 20),
    )(mine)
    grads = pl.pallas_call(
        functools.partial(place_kernel, True),
        out_shape=outs,
        in_specs=[VMEM] + [ANY] * 4,
        out_specs=[ANY] * 4,
        scratch_shapes=sems,
        compiler_params=pltpu.CompilerParams(vmem_limit_bytes=4 << 20),
        input_output_aliases={1: 0, 2: 1, 3: 2, 4: 3},
    )(other, *grads)
    return (node_next, grad_nodes, grad_edges, *grads)


def solution(mesh):
    fine = Mesh(mesh.devices.reshape(2, 4, 2, 2, 4, 2), ("yh", "x", "c", "yl", "zh", "zl"))
    tile = P(GX, GY)
    return jax.shard_map(
        local,
        mesh=fine,
        in_specs=(tile,) * 7 + (P(),) * 4,
        out_specs=(tile,) * 3 + (P(),) * 4,
        check_vma=False,
    )
```

```python
import functools

import jax
import jax.numpy as jnp
from jax import lax
from jax.experimental import pallas as pl
from jax.experimental.pallas import tpu as pltpu
from jax.sharding import Mesh
from jax.sharding import PartitionSpec as P

BF = jnp.bfloat16
F32 = jnp.float32
GX = ("yh", "x", "c")
GY = ("yl", "zh", "zl")
ALL = ("yh", "x", "c", "yl", "zh", "zl")


def place(x, y, core, z):
    return ((y // 2 * 4 + x) * 2 + core) * 16 + y % 2 * 8 + z % 8


def groups():
    four, lines = range(4), [(o, k) for o in range(4) for k in range(4)]
    near = [[place(k, o, 0, 2 * p + b) for k in four for b in (0, 1)] for o, p in lines]
    near += [[place(o, k, 1, 2 * p + 1 + b) for k in four for b in (0, 1)] for o, p in lines]
    ring = [[place(o, k, 0, z) for k in four] for o in four for z in range(8)]
    ring += [[place(k, o, 1, z) for k in four] for o in four for z in range(8)]
    far = [[place(x, y, c, 2 * p + b + c) for p in four] for x, y in lines for c in (0, 1) for b in (0, 1)]
    return near, ring, far
VMEM = pl.BlockSpec(memory_space=pltpu.VMEM)
ANY = pl.BlockSpec(memory_space=pl.ANY)


def dot(left, right):
    return jnp.dot(left, right, preferred_element_type=F32)


def dot_rows(left, right):
    return lax.dot_general(left, right, (((0,), (0,)), ((), ())), preferred_element_type=F32)


def dot_cols(left, right):
    return lax.dot_general(left, right, (((1,), (1,)), ((), ())), preferred_element_type=F32)


def hi_lo(values):
    high = values.astype(BF)
    low = (values - high.astype(F32)).astype(BF)
    return jnp.concatenate([high, low], axis=0)


def fold(values):
    half = values.shape[0] // 2
    return values[:half] + values[half:]


def layer_norm(values):
    mean = jnp.mean(values, axis=-1, keepdims=True)
    centred = values - mean
    scale = lax.rsqrt(jnp.mean(centred * centred, axis=-1, keepdims=True) + 1e-05)
    return centred * scale, scale


def norm_back(grad, normed, scale):
    first = jnp.mean(grad, axis=-1, keepdims=True)
    second = jnp.mean(grad * normed, axis=-1, keepdims=True)
    return scale * (grad - first - normed * second)


def silu_and_slope(values):
    sig = 1.0 / (1.0 + jnp.exp(-values))
    return values * sig, sig * (1.0 + values * (1.0 - sig))


def pick(row, count):
    rows = lax.broadcasted_iota(jnp.int32, (count, row.shape[-1]), 0)
    return jnp.where(rows == row, 1.0, 0.0)


def fetch(sources, targets, sems):
    copies = [
        pltpu.make_async_copy(source, target, sems.at[i])
        for i, (source, target) in enumerate(zip(sources, targets, strict=True))
    ]
    for copy in copies:
        copy.start()

    def ready(i):
        copies[i].wait()
        return targets[i]

    return ready


def parities():
    return lax.axis_index("c"), lax.axis_index("zl")


ROW_STEPS, COLUMN_STEPS = (1, 2), (0, 3)


def side_of(step, row_odd, col_odd):
    return (2 + col_odd, row_odd, 1 - row_odd, 3 - col_odd)[step]


def pack_kernel(nodes_hbm, lists_hbm, *refs):
    packs, (nodes, lists, sems) = refs[:4], refs[4:]
    ready = fetch((nodes_hbm.at[0, 0], lists_hbm.at[0, 0]), (nodes, lists), sems)
    odd = parities()
    ready(1)
    lat = ready(0)[...]
    for step in range(4):
        row = lists[pl.ds(side_of(step, *odd), 1), :]
        packs[step][...] = dot_rows(pick(row, lat.shape[0]).astype(BF), lat).astype(BF)


def load_kernel(
    packs,
    nodes_hbm,
    edges_hbm,
    senders_hbm,
    segments_hbm,
    cot_nodes_hbm,
    cot_edges_hbm,
    w_edge1_hbm,
    w_edge2_hbm,
    w_node1_hbm,
    w_node2_hbm,
    node,
    edge,
    cot_node,
    cot_edge,
    w_edge1,
    w_edge2,
    w_node1,
    w_node2,
    to_ext,
    to_node,
    from_node,
    from_halo,
    z_part,
    senders,
    segments,
    sems,
):
    del packs
    ready = fetch(
        (
            senders_hbm.at[0],
            segments_hbm.at[0],
            nodes_hbm.at[0, 0],
            w_edge1_hbm,
            edges_hbm.at[0, 0],
            w_edge2_hbm,
            w_node1_hbm,
            w_node2_hbm,
            cot_nodes_hbm.at[0, 0],
            cot_edges_hbm.at[0, 0],
        ),
        (
            senders,
            segments,
            node,
            w_edge1,
            edge,
            w_edge2,
            w_node1,
            w_node2,
            cot_node,
            cot_edge,
        ),
        sems,
    )
    count, width = node.shape
    by_send = pick(ready(0)[...], to_ext.shape[0])
    by_recv = pick(ready(1)[...], count)
    to_ext[...] = by_send.astype(BF)
    to_node[...] = by_recv.astype(BF)
    own = by_send[:count].T.astype(BF)
    halo = by_send[count:].T.astype(BF)
    recv = by_recv.T.astype(BF)
    from_halo[...] = jnp.concatenate([halo, halo], axis=1)
    from_node[...] = jnp.concatenate([recv, recv], axis=1)
    wide = jnp.concatenate([own, own, recv, recv], axis=1)
    lat = ready(2)[...]
    ready(3)
    terms = jnp.concatenate(
        [
            hi_lo(dot(lat, w_edge1[width : 2 * width, :])),
            hi_lo(dot(lat, w_edge1[2 * width :, :])),
        ],
        axis=0,
    )
    z_part[...] = dot(ready(4)[...], w_edge1[:width, :]) + dot(wide, terms)
    for i in range(5, 10):
        ready(i)


def put_half(target, side, pairs_of_block):
    for block, (left, right) in enumerate(pairs_of_block):
        part = left.shape[1] // 2
        columns = pl.ds(pl.multiple_of(side * part, part), part)
        target[block * part : (block + 1) * part, :] = dot_rows(
            left[:, columns], right[...]
        ).astype(BF)


def layer_kernel(
    halo0,
    halo1,
    halo2,
    halo3,
    node,
    edge,
    cot_node,
    cot_edge,
    w_edge1,
    w_edge2,
    w_node1,
    w_node2,
    to_ext,
    to_node,
    from_node,
    from_halo,
    z_part,
    node_next,
    send,
    ext_twice,
    node_twice,
    a_one,
    agg,
    a_three,
    dz_one,
    dz_two,
    dz_three,
    dz_four,
    sum_send,
    sum_recv,
    de_new,
    dn_part,
):
    odd = parities()
    count, width = node.shape
    rows = halo0.shape[0]
    reach = ext_twice.shape[0] // 2
    lat = node[...]
    for start in (0, reach):
        ext_twice[start : start + count, :] = lat
        for step, halo in enumerate((halo0, halo1, halo2, halo3)):
            place = start + count + side_of(step, *odd) * rows
            ext_twice[pl.ds(pl.multiple_of(place, rows), rows), :] = halo[...]
    for start in (0, count):
        node_twice[start : start + count, :] = lat

    terms = hi_lo(dot(ext_twice[count:reach, :], w_edge1[width : 2 * width, :]))
    z_one = z_part[...] + dot(from_halo[...], terms)
    act, slope_one = silu_and_slope(z_one)
    a_one[...] = act.astype(BF)
    n_two, s_two = layer_norm(dot(a_one[...], w_edge2[...]))
    e_new = (edge[...].astype(F32) + n_two).astype(BF)
    agg[...] = dot(to_node[...], e_new).astype(BF)
    z_three = dot(lat, w_node1[:width, :]) + dot(agg[...], w_node1[width:, :])
    act, slope_three = silu_and_slope(z_three)
    a_three[...] = act.astype(BF)
    n_four, s_four = layer_norm(dot(a_three[...], w_node2[...]))
    node_next[0, 0] = (lat.astype(F32) + n_four).astype(BF)

    g_node = cot_node[...].astype(F32)
    dz_four[...] = norm_back(g_node, n_four, s_four).astype(BF)
    dz_three[...] = (dot_cols(dz_four[...], w_node2[...]) * slope_three).astype(BF)
    dn_part[...] = g_node + dot_cols(dz_three[...], w_node1[:width, :])
    dy_agg = dot_cols(dz_three[...], w_node1[width:, :])

    de = cot_edge[...].astype(F32) + dot(from_node[...], hi_lo(dy_agg))
    de_new[...] = de
    dz_two[...] = norm_back(de, n_two, s_two).astype(BF)
    dz_one[...] = (dot_cols(dz_two[...], w_edge2[...]) * slope_one).astype(BF)
    sum_send[...] = hi_lo(dot(to_ext[...], dz_one[...]))
    sum_recv[...] = hi_lo(dot(to_node[...], dz_one[...]))
    put_half(
        send,
        1 - odd[0],
        (
            (edge, dz_one),
            (ext_twice, sum_send),
            (node_twice, sum_recv),
            (a_one, dz_two),
            (node, dz_three),
            (agg, dz_three),
            (a_three, dz_four),
        ),
    )


def rest_kernel(
    node,
    edge,
    w_edge1,
    ext_twice,
    node_twice,
    a_one,
    agg,
    a_three,
    dz_one,
    dz_two,
    dz_three,
    dz_four,
    sum_send,
    sum_recv,
    de_new,
    dn_part,
    keep,
    grad_edges,
    d_node,
    back0,
    back1,
    back2,
    back3,
    d_ext,
):
    odd = parities()
    count, width = node.shape
    rows = back0.shape[0]
    put_half(
        keep,
        odd[0],
        (
            (edge, dz_one),
            (ext_twice, sum_send),
            (node_twice, sum_recv),
            (a_one, dz_two),
            (node, dz_three),
            (agg, dz_three),
            (a_three, dz_four),
        ),
    )
    grad_edges[0, 0] = (de_new[...] + dot_cols(dz_one[...], w_edge1[:width, :])).astype(BF)
    d_ext[...] = fold(dot_cols(sum_send[...], w_edge1[width : 2 * width, :]))
    d_recv = fold(dot_cols(sum_recv[...], w_edge1[2 * width :, :]))
    d_node[...] = dn_part[...] + d_recv + d_ext[:count, :]
    for step, back in enumerate((back0, back1, back2, back3)):
        place = count + side_of(step, *odd) * rows
        back[...] = d_ext[pl.ds(pl.multiple_of(place, rows), rows), :].astype(BF)


def pair_sum_kernel(mine, other, out):
    out[...] = (mine[...].astype(F32) + other[...].astype(F32)).astype(BF)


def sum_parts(parts):
    total = parts[0].astype(F32)
    for part in range(1, parts.shape[0]):
        total = total + parts[part].astype(F32)
    return total


def near_sum_kernel(parts, out):
    out[...] = sum_parts(parts).astype(BF)


def ring_sum_kernel(parts, back0, back1, out, onward0, onward1):
    onward0[...] = back0[...]
    onward1[...] = back1[...]
    total = sum_parts(parts).astype(BF)
    for part in range(out.shape[0]):
        out[part] = total


def add_returned(grad, lists, steps, returned):
    odd = parities()
    for step, ret in zip(steps, returned, strict=True):
        row = lists[0, 0, pl.ds(side_of(step, *odd), 1), :]
        grad = grad + dot(pick(row, grad.shape[0]).astype(BF), ret[...])
    return grad


def far_sum_kernel(
    factor, parts, d_node, lists, ret0, ret1, back0, back1, out, grad, onward0, onward1
):
    onward0[...] = back0[...]
    onward1[...] = back1[...]
    total = (sum_parts(parts) * factor).astype(BF)
    for part in range(out.shape[0]):
        out[part] = total
    grad[...] = add_returned(d_node[...], lists, ROW_STEPS, (ret0, ret1))


def spread_kernel(whole, grad, lists, ret0, ret1, out, grad_nodes):
    rows = whole[...]
    for part in range(out.shape[0]):
        out[part] = rows
    grad_nodes[0, 0] = add_returned(grad[...], lists, COLUMN_STEPS, (ret0, ret1)).astype(BF)


def place_kernel(other_core, half, *refs):
    outs, sems = refs[-5:-1], refs[-1]
    part = outs[0].shape[1] // 2
    side = lax.axis_index("c")
    side = 1 - side if other_core else side
    copies = []
    for out in outs:
        for block in range(out.shape[0] // (2 * part)):
            place = pl.multiple_of((2 * block + side) * part, part)
            start = len(copies) * part
            copies.append(
                pltpu.make_async_copy(
                    half.at[start : start + part], out.at[pl.ds(place, part)], sems.at[len(copies)]
                )
            )
    for copy in copies:
        copy.start()
    for copy in copies:
        copy.wait()


def call(kernel, outs, ins, limit=24, scratch=(), **kwargs):
    return pl.pallas_call(
        kernel,
        out_shape=outs,
        in_specs=ins,
        out_specs=jax.tree.map(lambda _: VMEM, outs),
        scratch_shapes=list(scratch),
        compiler_params=pltpu.CompilerParams(vmem_limit_bytes=limit << 20),
        **kwargs,
    )


def shape(dims, kind=BF):
    return jax.ShapeDtypeStruct(dims, kind)


def in_hbm(*arrays):
    return [pltpu.with_memory_space_constraint(array, pltpu.HBM) for array in arrays]


def pairs(count, first):
    made = []
    for i in range(first, count - 1, 2):
        made += [(i, i + 1), (i + 1, i)]
    return made


def exchange(blocks, steps):
    axes = (GY, GX, GX, GY)
    first = (1, 1, 0, 0)
    return [
        lax.ppermute(block, axes[step], pairs(lax.axis_size(axes[step]), first[step]))
        for step, block in zip(steps, blocks, strict=True)
    ]


def swap(rows, groups):
    return lax.all_to_all(rows, ALL, 0, 0, axis_index_groups=groups, tiled=True)


def load(packs, nodes, edges, senders, segments, cot_nodes, cot_edges, weights):
    count, width = nodes.shape[2:]
    lines = edges.shape[2]
    reach = count + 4 * packs.shape[0]
    return call(
        load_kernel,
        [shape((count, width)), shape((lines, width))] * 2
        + [shape(w.shape) for w in weights]
        + [shape((reach, lines)), shape((count, lines))]
        + [shape((lines, 2 * count)), shape((lines, 2 * (reach - count)))]
        + [shape((lines, width), F32)],
        [VMEM] + [ANY] * 10,
        limit=12,
        scratch=[
            pltpu.VMEM((1, lines), jnp.int32),
            pltpu.VMEM((1, lines), jnp.int32),
            pltpu.SemaphoreType.DMA((10,)),
        ],
    )(packs, *in_hbm(nodes, edges, senders, segments, cot_nodes, cot_edges, *weights))


def layer(halos, loaded):
    node, edge, w_edge1 = loaded[0], loaded[1], loaded[4]
    (count, width), lines, rows = node.shape, edge.shape[0], halos[0].shape[0]
    reach = count + 4 * rows
    half = shape((sum(w.shape[0] for w in loaded[4:8]) // 2, width))
    on_edges, on_nodes = shape((lines, width)), shape((count, width))
    node_next, send, *state = call(
        layer_kernel,
        [shape((1, 1, count, width)), half]
        + [shape((2 * reach, width)), shape((2 * count, width)), on_edges, on_nodes, on_nodes]
        + [on_edges, on_edges, on_nodes, on_nodes]
        + [shape((2 * reach, width)), shape((2 * count, width))]
        + [shape((lines, width), F32), shape((count, width), F32)],
        [VMEM] * (4 + len(loaded)),
        limit=16,
    )(*halos, *loaded)
    keep, grad_edges, d_node, *backs = call(
        rest_kernel,
        [half, shape((1, 1, lines, width)), shape((count, width), F32)] + [shape((rows, width))] * 4,
        [VMEM] * (3 + len(state)),
        limit=12,
        scratch=[pltpu.VMEM((reach, width), F32)],
        cost_estimate=pl.CostEstimate(
            flops=2 * width * width * (4 * lines + 8 * reach),
            bytes_accessed=12 << 20,
            transcendentals=0,
        ),
    )(node, edge, w_edge1, *state)
    return node_next, send, keep, grad_edges, d_node, backs


def local(
    nodes,
    edges,
    senders,
    segments,
    send_lists,
    cot_nodes,
    cot_edges,
    w_edge1,
    w_edge2,
    w_node1,
    w_node2,
):
    count, width = nodes.shape[2:]
    lines = edges.shape[2]
    rows = send_lists.shape[3]
    weights = (w_edge1, w_edge2, w_node1, w_node2)
    total = sum(w.shape[0] for w in weights)
    block = [shape((rows, width))] * 4
    packs = call(
        pack_kernel,
        block,
        [ANY] * 2,
        scratch=[
            pltpu.VMEM((count, width), BF),
            pltpu.VMEM((4, rows), jnp.int32),
            pltpu.SemaphoreType.DMA((2,)),
        ],
    )(*in_hbm(nodes, send_lists))
    halos = exchange(packs, range(4))
    loaded = load(packs[3], nodes, edges, senders, segments, cot_nodes, cot_edges, weights)
    node_next, send, keep, grad_edges, d_node, backs = layer(halos, loaded)

    got = lax.ppermute(send, "c", pairs(2, 0))
    pair = call(pair_sum_kernel, shape(keep.shape), [VMEM] * 2, limit=8)(keep, got)

    near, ring, far = groups()
    n_near, n_ring, n_far = len(near[0]), len(ring[0]), len(far[0])
    mid = total // 2 // n_near
    strip = mid // n_ring
    factor = float(lines * 2 * n_near * n_ring * n_far) ** -0.5
    two = block[:2]
    pieces = swap(pair, near).reshape(n_near, mid, width)
    pieces = call(near_sum_kernel, shape((mid, width)), [VMEM], limit=8)(pieces)
    pieces = swap(pieces, ring).reshape(n_ring, strip, width)
    pieces, *by_row = call(
        ring_sum_kernel, [shape((n_far, strip, width))] + two, [VMEM] * 3, limit=8
    )(pieces, *[backs[step] for step in ROW_STEPS])
    by_row = exchange(by_row, ROW_STEPS)
    pieces = swap(pieces, far)
    pieces, grad, *by_column = call(
        functools.partial(far_sum_kernel, factor),
        [shape((n_ring, strip, width)), shape(d_node.shape, F32)] + two,
        [VMEM] * 7,
        limit=8,
    )(pieces, d_node, send_lists, *by_row, *[backs[step] for step in COLUMN_STEPS])
    by_column = exchange(by_column, COLUMN_STEPS)
    pieces = swap(pieces, ring).reshape(mid, width)
    pieces, grad_nodes = call(
        spread_kernel, [shape((n_near, mid, width)), shape(nodes.shape)], [VMEM] * 5, limit=8
    )(pieces, grad, send_lists, *by_column)
    mine = swap(pieces, near).reshape(total // 2, width)
    other = lax.ppermute(mine, "c", pairs(2, 0))
    outs = [shape(w.shape) for w in weights]
    sems = [pltpu.SemaphoreType.DMA((total // width,))]
    grads = pl.pallas_call(
        functools.partial(place_kernel, False),
        out_shape=outs,
        in_specs=[VMEM],
        out_specs=[ANY] * 4,
        scratch_shapes=sems,
        compiler_params=pltpu.CompilerParams(vmem_limit_bytes=4 << 20),
    )(mine)
    grads = pl.pallas_call(
        functools.partial(place_kernel, True),
        out_shape=outs,
        in_specs=[VMEM] + [ANY] * 4,
        out_specs=[ANY] * 4,
        scratch_shapes=sems,
        compiler_params=pltpu.CompilerParams(vmem_limit_bytes=4 << 20),
        input_output_aliases={1: 0, 2: 1, 3: 2, 4: 3},
    )(other, *grads)
    return (node_next, grad_nodes, grad_edges, *grads)


def solution(mesh):
    fine = Mesh(mesh.devices.reshape(2, 4, 2, 2, 4, 2), ("yh", "x", "c", "yl", "zh", "zl"))
    tile = P(GX, GY)
    return jax.shard_map(
        local,
        mesh=fine,
        in_specs=(tile,) * 7 + (P(),) * 4,
        out_specs=(tile,) * 3 + (P(),) * 4,
        check_vma=False,
    )
```

```python
import functools

import jax
import jax.numpy as jnp
from jax import lax
from jax.experimental import pallas as pl
from jax.experimental.pallas import tpu as pltpu
from jax.sharding import Mesh
from jax.sharding import PartitionSpec as P

BF = jnp.bfloat16
F32 = jnp.float32
GX = ("yh", "x", "c")
GY = ("yl", "zh", "zl")
ALL = ("yh", "x", "c", "yl", "zh", "zl")


def place(x, y, core, z):
    return ((y // 2 * 4 + x) * 2 + core) * 16 + y % 2 * 8 + z % 8


def groups():
    four, lines = range(4), [(o, k) for o in range(4) for k in range(4)]
    near = [[place(k, o, 0, 2 * p + b) for k in four for b in (0, 1)] for o, p in lines]
    near += [[place(o, k, 1, 2 * p + 1 + b) for k in four for b in (0, 1)] for o, p in lines]
    ring = [[place(o, k, 0, z) for k in four] for o in four for z in range(8)]
    ring += [[place(k, o, 1, z) for k in four] for o in four for z in range(8)]
    far = [[place(x, y, c, 2 * p + b + c) for p in four] for x, y in lines for c in (0, 1) for b in (0, 1)]
    return near, ring, far
VMEM = pl.BlockSpec(memory_space=pltpu.VMEM)
ANY = pl.BlockSpec(memory_space=pl.ANY)


def dot(left, right):
    return jnp.dot(left, right, preferred_element_type=F32)


def dot_rows(left, right):
    return lax.dot_general(left, right, (((0,), (0,)), ((), ())), preferred_element_type=F32)


def dot_cols(left, right):
    return lax.dot_general(left, right, (((1,), (1,)), ((), ())), preferred_element_type=F32)


def hi_lo(values):
    high = values.astype(BF)
    low = (values - high.astype(F32)).astype(BF)
    return jnp.concatenate([high, low], axis=0)


def fold(values):
    half = values.shape[0] // 2
    return values[:half] + values[half:]


def layer_norm(values):
    mean = jnp.mean(values, axis=-1, keepdims=True)
    centred = values - mean
    scale = lax.rsqrt(jnp.mean(centred * centred, axis=-1, keepdims=True) + 1e-05)
    return centred * scale, scale


def norm_back(grad, normed, scale):
    first = jnp.mean(grad, axis=-1, keepdims=True)
    second = jnp.mean(grad * normed, axis=-1, keepdims=True)
    return scale * (grad - first - normed * second)


def silu_and_slope(values):
    sig = 1.0 / (1.0 + jnp.exp(-values))
    return values * sig, sig * (1.0 + values * (1.0 - sig))


def pick(row, count):
    rows = lax.broadcasted_iota(jnp.int32, (count, row.shape[-1]), 0)
    return jnp.where(rows == row, 1.0, 0.0)


def fetch(sources, targets, sems):
    copies = [
        pltpu.make_async_copy(source, target, sems.at[i])
        for i, (source, target) in enumerate(zip(sources, targets, strict=True))
    ]
    for copy in copies:
        copy.start()

    def ready(i):
        copies[i].wait()
        return targets[i]

    return ready


def parities():
    return lax.axis_index("c"), lax.axis_index("zl")


CORE_STEP, CHIP_STEPS = 2, (0, 1, 3)


def side_of(step, row_odd, col_odd):
    return (2 + col_odd, row_odd, 1 - row_odd, 3 - col_odd)[step]


def pack_kernel(nodes_hbm, lists_hbm, *refs):
    packs, (nodes, lists, sems) = refs[:4], refs[4:]
    ready = fetch((nodes_hbm.at[0, 0], lists_hbm.at[0, 0]), (nodes, lists), sems)
    odd = parities()
    ready(1)
    lat = ready(0)[...]
    for step in range(4):
        row = lists[pl.ds(side_of(step, *odd), 1), :]
        packs[step][...] = dot_rows(pick(row, lat.shape[0]).astype(BF), lat).astype(BF)


def load_kernel(
    packs,
    nodes_hbm,
    edges_hbm,
    senders_hbm,
    segments_hbm,
    cot_nodes_hbm,
    cot_edges_hbm,
    w_edge1_hbm,
    w_edge2_hbm,
    w_node1_hbm,
    w_node2_hbm,
    node,
    edge,
    cot_node,
    cot_edge,
    w_edge1,
    w_edge2,
    w_node1,
    w_node2,
    to_ext,
    to_node,
    from_node,
    from_halo,
    z_part,
    senders,
    segments,
    sems,
):
    del packs
    ready = fetch(
        (
            senders_hbm.at[0],
            segments_hbm.at[0],
            nodes_hbm.at[0, 0],
            w_edge1_hbm,
            edges_hbm.at[0, 0],
            w_edge2_hbm,
            w_node1_hbm,
            w_node2_hbm,
            cot_nodes_hbm.at[0, 0],
            cot_edges_hbm.at[0, 0],
        ),
        (
            senders,
            segments,
            node,
            w_edge1,
            edge,
            w_edge2,
            w_node1,
            w_node2,
            cot_node,
            cot_edge,
        ),
        sems,
    )
    count, width = node.shape
    by_send = pick(ready(0)[...], to_ext.shape[0])
    by_recv = pick(ready(1)[...], count)
    to_ext[...] = by_send.astype(BF)
    to_node[...] = by_recv.astype(BF)
    own = by_send[:count].T.astype(BF)
    halo = by_send[count:].T.astype(BF)
    recv = by_recv.T.astype(BF)
    from_halo[...] = jnp.concatenate([halo, halo], axis=1)
    from_node[...] = jnp.concatenate([recv, recv], axis=1)
    wide = jnp.concatenate([own, own, recv, recv], axis=1)
    lat = ready(2)[...]
    ready(3)
    terms = jnp.concatenate(
        [
            hi_lo(dot(lat, w_edge1[width : 2 * width, :])),
            hi_lo(dot(lat, w_edge1[2 * width :, :])),
        ],
        axis=0,
    )
    z_part[...] = dot(ready(4)[...], w_edge1[:width, :]) + dot(wide, terms)
    for i in range(5, 10):
        ready(i)


def put_half(target, side, pairs_of_block):
    for block, (left, right) in enumerate(pairs_of_block):
        part = left.shape[1] // 2
        columns = pl.ds(pl.multiple_of(side * part, part), part)
        target[block * part : (block + 1) * part, :] = dot_rows(
            left[:, columns], right[...]
        ).astype(BF)


def layer_kernel(
    halo0,
    halo1,
    halo2,
    halo3,
    node,
    edge,
    cot_node,
    cot_edge,
    w_edge1,
    w_edge2,
    w_node1,
    w_node2,
    to_ext,
    to_node,
    from_node,
    from_halo,
    z_part,
    node_next,
    send,
    ext_twice,
    node_twice,
    a_one,
    agg,
    a_three,
    dz_one,
    dz_two,
    dz_three,
    dz_four,
    sum_send,
    sum_recv,
    de_new,
    dn_part,
):
    odd = parities()
    count, width = node.shape
    rows = halo0.shape[0]
    reach = ext_twice.shape[0] // 2
    lat = node[...]
    for start in (0, reach):
        ext_twice[start : start + count, :] = lat
        for step, halo in enumerate((halo0, halo1, halo2, halo3)):
            place = start + count + side_of(step, *odd) * rows
            ext_twice[pl.ds(pl.multiple_of(place, rows), rows), :] = halo[...]
    for start in (0, count):
        node_twice[start : start + count, :] = lat

    terms = hi_lo(dot(ext_twice[count:reach, :], w_edge1[width : 2 * width, :]))
    z_one = z_part[...] + dot(from_halo[...], terms)
    act, slope_one = silu_and_slope(z_one)
    a_one[...] = act.astype(BF)
    n_two, s_two = layer_norm(dot(a_one[...], w_edge2[...]))
    e_new = (edge[...].astype(F32) + n_two).astype(BF)
    agg[...] = dot(to_node[...], e_new).astype(BF)
    z_three = dot(lat, w_node1[:width, :]) + dot(agg[...], w_node1[width:, :])
    act, slope_three = silu_and_slope(z_three)
    a_three[...] = act.astype(BF)
    n_four, s_four = layer_norm(dot(a_three[...], w_node2[...]))
    node_next[0, 0] = (lat.astype(F32) + n_four).astype(BF)

    g_node = cot_node[...].astype(F32)
    dz_four[...] = norm_back(g_node, n_four, s_four).astype(BF)
    dz_three[...] = (dot_cols(dz_four[...], w_node2[...]) * slope_three).astype(BF)
    dn_part[...] = g_node + dot_cols(dz_three[...], w_node1[:width, :])
    dy_agg = dot_cols(dz_three[...], w_node1[width:, :])

    de = cot_edge[...].astype(F32) + dot(from_node[...], hi_lo(dy_agg))
    de_new[...] = de
    dz_two[...] = norm_back(de, n_two, s_two).astype(BF)
    dz_one[...] = (dot_cols(dz_two[...], w_edge2[...]) * slope_one).astype(BF)
    sum_send[...] = hi_lo(dot(to_ext[...], dz_one[...]))
    sum_recv[...] = hi_lo(dot(to_node[...], dz_one[...]))
    first = count + side_of(CORE_STEP, *odd) * rows
    ride = jnp.concatenate(
        [
            sum_send[pl.ds(pl.multiple_of(first, rows), rows), :],
            sum_send[pl.ds(pl.multiple_of(reach + first, rows), rows), :],
        ],
        axis=0,
    )
    send[send.shape[0] - rows :, :] = fold(dot_cols(ride, w_edge1[width : 2 * width, :])).astype(BF)
    put_half(
        send,
        1 - odd[0],
        (
            (edge, dz_one),
            (ext_twice, sum_send),
            (node_twice, sum_recv),
            (a_one, dz_two),
            (node, dz_three),
            (agg, dz_three),
            (a_three, dz_four),
        ),
    )


def rest_kernel(
    node,
    edge,
    w_edge1,
    ext_twice,
    node_twice,
    a_one,
    agg,
    a_three,
    dz_one,
    dz_two,
    dz_three,
    dz_four,
    sum_send,
    sum_recv,
    de_new,
    dn_part,
    keep,
    grad_edges,
    d_node,
    back0,
    back1,
    back2,
    d_ext,
):
    odd = parities()
    count, width = node.shape
    rows = back0.shape[0]
    put_half(
        keep,
        odd[0],
        (
            (edge, dz_one),
            (ext_twice, sum_send),
            (node_twice, sum_recv),
            (a_one, dz_two),
            (node, dz_three),
            (agg, dz_three),
            (a_three, dz_four),
        ),
    )
    grad_edges[0, 0] = (de_new[...] + dot_cols(dz_one[...], w_edge1[:width, :])).astype(BF)
    d_ext[...] = fold(dot_cols(sum_send[...], w_edge1[width : 2 * width, :]))
    d_recv = fold(dot_cols(sum_recv[...], w_edge1[2 * width :, :]))
    d_node[...] = dn_part[...] + d_recv + d_ext[:count, :]
    for step, back in zip(CHIP_STEPS, (back0, back1, back2), strict=True):
        place = count + side_of(step, *odd) * rows
        back[...] = d_ext[pl.ds(pl.multiple_of(place, rows), rows), :].astype(BF)


def pair_sum_kernel(mine, other, out, ret):
    rows = mine.shape[0]
    out[...] = (mine[...].astype(F32) + other[:rows, :].astype(F32)).astype(BF)
    ret[...] = other[rows:, :]


def sum_parts(parts):
    total = parts[0].astype(F32)
    for part in range(1, parts.shape[0]):
        total = total + parts[part].astype(F32)
    return total


def near_sum_kernel(parts, out):
    out[...] = sum_parts(parts).astype(BF)


def ring_sum_kernel(parts, *refs):
    backs, out, onward = refs[:3], refs[3], refs[4:]
    for back, ref in zip(backs, onward, strict=True):
        ref[...] = back[...]
    total = sum_parts(parts).astype(BF)
    for part in range(out.shape[0]):
        out[part] = total


def far_sum_kernel(factor, parts, d_node, lists, ret0, ret1, ret2, ret3, out, grad_nodes):
    total = (sum_parts(parts) * factor).astype(BF)
    for part in range(out.shape[0]):
        out[part] = total
    odd = parities()
    grad = d_node[...]
    for step, ret in zip((CORE_STEP, *CHIP_STEPS), (ret0, ret1, ret2, ret3), strict=True):
        row = lists[0, 0, pl.ds(side_of(step, *odd), 1), :]
        grad = grad + dot(pick(row, grad.shape[0]).astype(BF), ret[...])
    grad_nodes[0, 0] = grad.astype(BF)


def spread_kernel(whole, out):
    rows = whole[...]
    for part in range(out.shape[0]):
        out[part] = rows


def place_kernel(other_core, half, *refs):
    outs, sems = refs[-5:-1], refs[-1]
    part = outs[0].shape[1] // 2
    side = lax.axis_index("c")
    side = 1 - side if other_core else side
    copies = []
    for out in outs:
        for block in range(out.shape[0] // (2 * part)):
            place = pl.multiple_of((2 * block + side) * part, part)
            start = len(copies) * part
            copies.append(
                pltpu.make_async_copy(
                    half.at[start : start + part], out.at[pl.ds(place, part)], sems.at[len(copies)]
                )
            )
    for copy in copies:
        copy.start()
    for copy in copies:
        copy.wait()


def call(kernel, outs, ins, limit=24, scratch=(), **kwargs):
    return pl.pallas_call(
        kernel,
        out_shape=outs,
        in_specs=ins,
        out_specs=jax.tree.map(lambda _: VMEM, outs),
        scratch_shapes=list(scratch),
        compiler_params=pltpu.CompilerParams(vmem_limit_bytes=limit << 20),
        **kwargs,
    )


def shape(dims, kind=BF):
    return jax.ShapeDtypeStruct(dims, kind)


def in_hbm(*arrays):
    return [pltpu.with_memory_space_constraint(array, pltpu.HBM) for array in arrays]


def pairs(count, first):
    made = []
    for i in range(first, count + first, 2):
        made += [(i, (i + 1) % count), ((i + 1) % count, i)]
    return made


def exchange(blocks, steps):
    axes = (GY, GX, GX, GY)
    first = (1, 1, 0, 0)
    return [
        lax.ppermute(block, axes[step], pairs(lax.axis_size(axes[step]), first[step]))
        for step, block in zip(steps, blocks, strict=True)
    ]


def swap(rows, groups):
    return lax.all_to_all(rows, ALL, 0, 0, axis_index_groups=groups, tiled=True)


def load(packs, nodes, edges, senders, segments, cot_nodes, cot_edges, weights):
    count, width = nodes.shape[2:]
    lines = edges.shape[2]
    reach = count + 4 * packs.shape[0]
    return call(
        load_kernel,
        [shape((count, width)), shape((lines, width))] * 2
        + [shape(w.shape) for w in weights]
        + [shape((reach, lines)), shape((count, lines))]
        + [shape((lines, 2 * count)), shape((lines, 2 * (reach - count)))]
        + [shape((lines, width), F32)],
        [VMEM] + [ANY] * 10,
        limit=12,
        scratch=[
            pltpu.VMEM((1, lines), jnp.int32),
            pltpu.VMEM((1, lines), jnp.int32),
            pltpu.SemaphoreType.DMA((10,)),
        ],
    )(packs, *in_hbm(nodes, edges, senders, segments, cot_nodes, cot_edges, *weights))


def layer(halos, loaded):
    node, edge, w_edge1 = loaded[0], loaded[1], loaded[4]
    (count, width), lines, rows = node.shape, edge.shape[0], halos[0].shape[0]
    reach = count + 4 * rows
    half = sum(w.shape[0] for w in loaded[4:8]) // 2
    on_edges, on_nodes = shape((lines, width)), shape((count, width))
    node_next, send, *state = call(
        layer_kernel,
        [shape((1, 1, count, width)), shape((half + rows, width))]
        + [shape((2 * reach, width)), shape((2 * count, width)), on_edges, on_nodes, on_nodes]
        + [on_edges, on_edges, on_nodes, on_nodes]
        + [shape((2 * reach, width)), shape((2 * count, width))]
        + [shape((lines, width), F32), shape((count, width), F32)],
        [VMEM] * (4 + len(loaded)),
        limit=16,
    )(*halos, *loaded)
    keep, grad_edges, d_node, *backs = call(
        rest_kernel,
        [shape((half, width)), shape((1, 1, lines, width)), shape((count, width), F32)]
        + [shape((rows, width))] * 3,
        [VMEM] * (3 + len(state)),
        limit=12,
        scratch=[pltpu.VMEM((reach, width), F32)],
        cost_estimate=pl.CostEstimate(
            flops=2 * width * width * (4 * lines + 8 * reach),
            bytes_accessed=12 << 20,
            transcendentals=0,
        ),
    )(node, edge, w_edge1, *state)
    return node_next, send, keep, grad_edges, d_node, backs


def local(
    nodes,
    edges,
    senders,
    segments,
    send_lists,
    cot_nodes,
    cot_edges,
    w_edge1,
    w_edge2,
    w_node1,
    w_node2,
):
    count, width = nodes.shape[2:]
    lines = edges.shape[2]
    rows = send_lists.shape[3]
    weights = (w_edge1, w_edge2, w_node1, w_node2)
    total = sum(w.shape[0] for w in weights)
    block = [shape((rows, width))] * 4
    packs = call(
        pack_kernel,
        block,
        [ANY] * 2,
        scratch=[
            pltpu.VMEM((count, width), BF),
            pltpu.VMEM((4, rows), jnp.int32),
            pltpu.SemaphoreType.DMA((2,)),
        ],
    )(*in_hbm(nodes, send_lists))
    halos = exchange(packs, range(4))
    loaded = load(packs[3], nodes, edges, senders, segments, cot_nodes, cot_edges, weights)
    node_next, send, keep, grad_edges, d_node, backs = layer(halos, loaded)

    got = lax.ppermute(send, "c", pairs(2, 0))
    pair, core_back = call(
        pair_sum_kernel, [shape(keep.shape), shape((rows, width))], [VMEM] * 2, limit=8
    )(keep, got)

    near, ring, far = groups()
    n_near, n_ring, n_far = len(near[0]), len(ring[0]), len(far[0])
    mid = total // 2 // n_near
    strip = mid // n_ring
    factor = float(lines * 2 * n_near * n_ring * n_far) ** -0.5
    pieces = swap(pair, near).reshape(n_near, mid, width)
    pieces = call(near_sum_kernel, shape((mid, width)), [VMEM], limit=8)(pieces)
    pieces = swap(pieces, ring).reshape(n_ring, strip, width)
    pieces, *backs = call(
        ring_sum_kernel, [shape((n_far, strip, width))] + block[:3], [VMEM] * 4, limit=8
    )(pieces, *backs)
    returned = exchange(backs, CHIP_STEPS)
    pieces = swap(pieces, far)
    pieces, grad_nodes = call(
        functools.partial(far_sum_kernel, factor),
        [shape((n_ring, strip, width)), shape(nodes.shape)],
        [VMEM] * 7,
        limit=8,
    )(pieces, d_node, send_lists, core_back, *returned)
    pieces = swap(pieces, ring).reshape(mid, width)
    pieces = call(spread_kernel, shape((n_near, mid, width)), [VMEM], limit=8)(pieces)
    mine = swap(pieces, near).reshape(total // 2, width)
    other = lax.ppermute(mine, "c", pairs(2, 0))
    outs = [shape(w.shape) for w in weights]
    sems = [pltpu.SemaphoreType.DMA((total // width,))]
    grads = pl.pallas_call(
        functools.partial(place_kernel, False),
        out_shape=outs,
        in_specs=[VMEM],
        out_specs=[ANY] * 4,
        scratch_shapes=sems,
        compiler_params=pltpu.CompilerParams(vmem_limit_bytes=4 << 20),
    )(mine)
    grads = pl.pallas_call(
        functools.partial(place_kernel, True),
        out_shape=outs,
        in_specs=[VMEM] + [ANY] * 4,
        out_specs=[ANY] * 4,
        scratch_shapes=sems,
        compiler_params=pltpu.CompilerParams(vmem_limit_bytes=4 << 20),
        input_output_aliases={1: 0, 2: 1, 3: 2, 4: 3},
    )(other, *grads)
    return (node_next, grad_nodes, grad_edges, *grads)


def solution(mesh):
    fine = Mesh(mesh.devices.reshape(2, 4, 2, 2, 4, 2), ("yh", "x", "c", "yl", "zh", "zl"))
    tile = P(GX, GY)
    return jax.shard_map(
        local,
        mesh=fine,
        in_specs=(tile,) * 7 + (P(),) * 4,
        out_specs=(tile,) * 3 + (P(),) * 4,
        check_vma=False,
    )
```

```python
import functools

import jax
import jax.numpy as jnp
from jax import lax
from jax.experimental import pallas as pl
from jax.experimental.pallas import tpu as pltpu
from jax.sharding import Mesh
from jax.sharding import PartitionSpec as P

BF = jnp.bfloat16
F32 = jnp.float32
GX = ("yh", "x", "c")
GY = ("yl", "zh", "zl")
ALL = ("yh", "x", "c", "yl", "zh", "zl")


def place(x, y, core, z):
    return ((y // 2 * 4 + x) * 2 + core) * 16 + y % 2 * 8 + z % 8


def groups():
    four, lines = range(4), [(o, k) for o in range(4) for k in range(4)]
    near = [[place(k, o, 0, 2 * p + b) for k in four for b in (0, 1)] for o, p in lines]
    near += [[place(o, k, 1, 2 * p + 1 + b) for k in four for b in (0, 1)] for o, p in lines]
    ring = [[place(o, k, 0, z) for k in four] for o in four for z in range(8)]
    ring += [[place(k, o, 1, z) for k in four] for o in four for z in range(8)]
    far = [[place(x, y, c, 2 * p + b + c) for p in four] for x, y in lines for c in (0, 1) for b in (0, 1)]
    return near, ring, far
VMEM = pl.BlockSpec(memory_space=pltpu.VMEM)
ANY = pl.BlockSpec(memory_space=pl.ANY)


def dot(left, right):
    return jnp.dot(left, right, preferred_element_type=F32)


def dot_rows(left, right):
    return lax.dot_general(left, right, (((0,), (0,)), ((), ())), preferred_element_type=F32)


def dot_cols(left, right):
    return lax.dot_general(left, right, (((1,), (1,)), ((), ())), preferred_element_type=F32)


def hi_lo(values):
    high = values.astype(BF)
    low = (values - high.astype(F32)).astype(BF)
    return jnp.concatenate([high, low], axis=0)


def fold(values):
    half = values.shape[0] // 2
    return values[:half] + values[half:]


def layer_norm(values):
    mean = jnp.mean(values, axis=-1, keepdims=True)
    centred = values - mean
    scale = lax.rsqrt(jnp.mean(centred * centred, axis=-1, keepdims=True) + 1e-05)
    return centred * scale, scale


def norm_back(grad, normed, scale):
    first = jnp.mean(grad, axis=-1, keepdims=True)
    second = jnp.mean(grad * normed, axis=-1, keepdims=True)
    return scale * (grad - first - normed * second)


def silu_and_slope(values):
    sig = 1.0 / (1.0 + jnp.exp(-values))
    return values * sig, sig * (1.0 + values * (1.0 - sig))


def pick(row, count):
    rows = lax.broadcasted_iota(jnp.int32, (count, row.shape[-1]), 0)
    return jnp.where(rows == row, 1.0, 0.0)


def fetch(sources, targets, sems):
    copies = [
        pltpu.make_async_copy(source, target, sems.at[i])
        for i, (source, target) in enumerate(zip(sources, targets, strict=True))
    ]
    for copy in copies:
        copy.start()

    def ready(i):
        copies[i].wait()
        return targets[i]

    return ready


def parities():
    return lax.axis_index("c"), lax.axis_index("zl")


CORE_STEP, CHIP_STEPS = 2, (0, 1, 3)


def side_of(step, row_odd, col_odd):
    return (2 + col_odd, row_odd, 1 - row_odd, 3 - col_odd)[step]


def pack_kernel(nodes_hbm, lists_hbm, *refs):
    packs, (nodes, lists, sems) = refs[:4], refs[4:]
    ready = fetch((nodes_hbm.at[0, 0], lists_hbm.at[0, 0]), (nodes, lists), sems)
    odd = parities()
    ready(1)
    lat = ready(0)[...]
    for step in range(4):
        row = lists[pl.ds(side_of(step, *odd), 1), :]
        packs[step][...] = dot_rows(pick(row, lat.shape[0]).astype(BF), lat).astype(BF)


def load_kernel(
    packs,
    nodes_hbm,
    edges_hbm,
    senders_hbm,
    segments_hbm,
    cot_nodes_hbm,
    cot_edges_hbm,
    w_edge1_hbm,
    w_edge2_hbm,
    w_node1_hbm,
    w_node2_hbm,
    node,
    edge,
    cot_node,
    cot_edge,
    w_edge1,
    w_edge2,
    w_node1,
    w_node2,
    to_ext,
    to_node,
    from_node,
    from_halo,
    z_part,
    senders,
    segments,
    sems,
):
    del packs
    ready = fetch(
        (
            senders_hbm.at[0],
            segments_hbm.at[0],
            nodes_hbm.at[0, 0],
            w_edge1_hbm,
            edges_hbm.at[0, 0],
            w_edge2_hbm,
            w_node1_hbm,
            w_node2_hbm,
            cot_nodes_hbm.at[0, 0],
            cot_edges_hbm.at[0, 0],
        ),
        (
            senders,
            segments,
            node,
            w_edge1,
            edge,
            w_edge2,
            w_node1,
            w_node2,
            cot_node,
            cot_edge,
        ),
        sems,
    )
    count, width = node.shape
    by_send = pick(ready(0)[...], to_ext.shape[0])
    by_recv = pick(ready(1)[...], count)
    to_ext[...] = by_send.astype(BF)
    to_node[...] = by_recv.astype(BF)
    own = by_send[:count].T.astype(BF)
    halo = by_send[count:].T.astype(BF)
    recv = by_recv.T.astype(BF)
    from_halo[...] = jnp.concatenate([halo, halo], axis=1)
    from_node[...] = jnp.concatenate([recv, recv], axis=1)
    wide = jnp.concatenate([own, own, recv, recv], axis=1)
    lat = ready(2)[...]
    ready(3)
    terms = jnp.concatenate(
        [
            hi_lo(dot(lat, w_edge1[width : 2 * width, :])),
            hi_lo(dot(lat, w_edge1[2 * width :, :])),
        ],
        axis=0,
    )
    z_part[...] = dot(ready(4)[...], w_edge1[:width, :]) + dot(wide, terms)
    for i in range(5, 10):
        ready(i)


def put_half(target, side, pairs_of_block):
    for block, (left, right) in enumerate(pairs_of_block):
        part = left.shape[1] // 2
        columns = pl.ds(pl.multiple_of(side * part, part), part)
        target[block * part : (block + 1) * part, :] = dot_rows(
            left[:, columns], right[...]
        ).astype(BF)


def layer_kernel(
    halo0,
    halo1,
    halo2,
    halo3,
    node,
    edge,
    cot_node,
    cot_edge,
    w_edge1,
    w_edge2,
    w_node1,
    w_node2,
    to_ext,
    to_node,
    from_node,
    from_halo,
    z_part,
    send,
    next_node,
    ext_twice,
    node_twice,
    a_one,
    agg,
    a_three,
    dz_one,
    dz_two,
    dz_three,
    dz_four,
    sum_send,
    sum_recv,
    de_new,
    dn_part,
):
    odd = parities()
    count, width = node.shape
    rows = halo0.shape[0]
    reach = ext_twice.shape[0] // 2
    lat = node[...]
    for start in (0, reach):
        ext_twice[start : start + count, :] = lat
        for step, halo in enumerate((halo0, halo1, halo2, halo3)):
            place = start + count + side_of(step, *odd) * rows
            ext_twice[pl.ds(pl.multiple_of(place, rows), rows), :] = halo[...]
    for start in (0, count):
        node_twice[start : start + count, :] = lat

    terms = hi_lo(dot(ext_twice[count:reach, :], w_edge1[width : 2 * width, :]))
    z_one = z_part[...] + dot(from_halo[...], terms)
    act, slope_one = silu_and_slope(z_one)
    a_one[...] = act.astype(BF)
    n_two, s_two = layer_norm(dot(a_one[...], w_edge2[...]))
    e_new = (edge[...].astype(F32) + n_two).astype(BF)
    agg[...] = dot(to_node[...], e_new).astype(BF)
    z_three = dot(lat, w_node1[:width, :]) + dot(agg[...], w_node1[width:, :])
    act, slope_three = silu_and_slope(z_three)
    a_three[...] = act.astype(BF)
    n_four, s_four = layer_norm(dot(a_three[...], w_node2[...]))
    next_node[...] = (lat.astype(F32) + n_four).astype(BF)

    g_node = cot_node[...].astype(F32)
    dz_four[...] = norm_back(g_node, n_four, s_four).astype(BF)
    dz_three[...] = (dot_cols(dz_four[...], w_node2[...]) * slope_three).astype(BF)
    dn_part[...] = g_node + dot_cols(dz_three[...], w_node1[:width, :])
    dy_agg = dot_cols(dz_three[...], w_node1[width:, :])

    de = cot_edge[...].astype(F32) + dot(from_node[...], hi_lo(dy_agg))
    de_new[...] = de
    dz_two[...] = norm_back(de, n_two, s_two).astype(BF)
    dz_one[...] = (dot_cols(dz_two[...], w_edge2[...]) * slope_one).astype(BF)
    sum_send[...] = hi_lo(dot(to_ext[...], dz_one[...]))
    sum_recv[...] = hi_lo(dot(to_node[...], dz_one[...]))
    first = count + side_of(CORE_STEP, *odd) * rows
    ride = jnp.concatenate(
        [
            sum_send[pl.ds(pl.multiple_of(first, rows), rows), :],
            sum_send[pl.ds(pl.multiple_of(reach + first, rows), rows), :],
        ],
        axis=0,
    )
    send[send.shape[0] - rows :, :] = fold(dot_cols(ride, w_edge1[width : 2 * width, :])).astype(BF)
    put_half(
        send,
        1 - odd[0],
        (
            (edge, dz_one),
            (ext_twice, sum_send),
            (node_twice, sum_recv),
            (a_one, dz_two),
            (node, dz_three),
            (agg, dz_three),
            (a_three, dz_four),
        ),
    )


def rest_kernel(
    node,
    edge,
    w_edge1,
    next_node,
    ext_twice,
    node_twice,
    a_one,
    agg,
    a_three,
    dz_one,
    dz_two,
    dz_three,
    dz_four,
    sum_send,
    sum_recv,
    de_new,
    dn_part,
    keep,
    node_next,
    grad_edges,
    d_node,
    back0,
    back1,
    back2,
    d_ext,
):
    node_next[0, 0] = next_node[...]
    odd = parities()
    count, width = node.shape
    rows = back0.shape[0]
    put_half(
        keep,
        odd[0],
        (
            (edge, dz_one),
            (ext_twice, sum_send),
            (node_twice, sum_recv),
            (a_one, dz_two),
            (node, dz_three),
            (agg, dz_three),
            (a_three, dz_four),
        ),
    )
    grad_edges[0, 0] = (de_new[...] + dot_cols(dz_one[...], w_edge1[:width, :])).astype(BF)
    d_ext[...] = fold(dot_cols(sum_send[...], w_edge1[width : 2 * width, :]))
    d_recv = fold(dot_cols(sum_recv[...], w_edge1[2 * width :, :]))
    d_node[...] = dn_part[...] + d_recv + d_ext[:count, :]
    for step, back in zip(CHIP_STEPS, (back0, back1, back2), strict=True):
        place = count + side_of(step, *odd) * rows
        back[...] = d_ext[pl.ds(pl.multiple_of(place, rows), rows), :].astype(BF)


def pair_sum_kernel(mine, other, out, ret):
    rows = mine.shape[0]
    out[...] = (mine[...].astype(F32) + other[:rows, :].astype(F32)).astype(BF)
    ret[...] = other[rows:, :]


def sum_parts(parts):
    total = parts[0].astype(F32)
    for part in range(1, parts.shape[0]):
        total = total + parts[part].astype(F32)
    return total


def near_sum_kernel(parts, out):
    out[...] = sum_parts(parts).astype(BF)


def ring_sum_kernel(parts, *refs):
    backs, out, onward = refs[:3], refs[3], refs[4:]
    for back, ref in zip(backs, onward, strict=True):
        ref[...] = back[...]
    total = sum_parts(parts).astype(BF)
    for part in range(out.shape[0]):
        out[part] = total


def far_sum_kernel(factor, parts, *refs):
    returned, out, onward = refs[:3], refs[3], refs[4:]
    for ret, ref in zip(returned, onward, strict=True):
        ref[...] = ret[...]
    total = (sum_parts(parts) * factor).astype(BF)
    for part in range(out.shape[0]):
        out[part] = total


def spread_kernel(whole, out):
    rows = whole[...]
    for part in range(out.shape[0]):
        out[part] = rows


def place_half(side, half, outs, sems):
    part = outs[0].shape[1] // 2
    copies = []
    for out in outs:
        for block in range(out.shape[0] // (2 * part)):
            target = pl.multiple_of((2 * block + side) * part, part)
            start = len(copies) * part
            copies.append(
                pltpu.make_async_copy(
                    half.at[start : start + part], out.at[pl.ds(target, part)], sems.at[len(copies)]
                )
            )
    for copy in copies:
        copy.start()
    return copies


def own_kernel(half, d_node, lists, ret0, ret1, ret2, ret3, *refs):
    outs, grad_nodes, sems = refs[:4], refs[4], refs[5]
    odd = parities()
    copies = place_half(odd[0], half, outs, sems)
    grad = d_node[...]
    for step, ret in zip((CORE_STEP, *CHIP_STEPS), (ret0, ret1, ret2, ret3), strict=True):
        row = lists[0, 0, pl.ds(side_of(step, *odd), 1), :]
        grad = grad + dot(pick(row, grad.shape[0]).astype(BF), ret[...])
    grad_nodes[0, 0] = grad.astype(BF)
    for copy in copies:
        copy.wait()


def other_kernel(half, *refs):
    outs, sems = refs[-5:-1], refs[-1]
    for copy in place_half(1 - parities()[0], half, outs, sems):
        copy.wait()


def call(kernel, outs, ins, limit=24, scratch=(), **kwargs):
    return pl.pallas_call(
        kernel,
        out_shape=outs,
        in_specs=ins,
        out_specs=jax.tree.map(lambda _: VMEM, outs),
        scratch_shapes=list(scratch),
        compiler_params=pltpu.CompilerParams(vmem_limit_bytes=limit << 20),
        **kwargs,
    )


def shape(dims, kind=BF):
    return jax.ShapeDtypeStruct(dims, kind)


def in_hbm(*arrays):
    return [pltpu.with_memory_space_constraint(array, pltpu.HBM) for array in arrays]


def pairs(count, first):
    made = []
    for i in range(first, count + first, 2):
        made += [(i, (i + 1) % count), ((i + 1) % count, i)]
    return made


def exchange(blocks, steps):
    axes = (GY, GX, GX, GY)
    first = (1, 1, 0, 0)
    return [
        lax.ppermute(block, axes[step], pairs(lax.axis_size(axes[step]), first[step]))
        for step, block in zip(steps, blocks, strict=True)
    ]


def swap(rows, groups):
    return lax.all_to_all(rows, ALL, 0, 0, axis_index_groups=groups, tiled=True)


def load(packs, nodes, edges, senders, segments, cot_nodes, cot_edges, weights):
    count, width = nodes.shape[2:]
    lines = edges.shape[2]
    reach = count + 4 * packs.shape[0]
    return call(
        load_kernel,
        [shape((count, width)), shape((lines, width))] * 2
        + [shape(w.shape) for w in weights]
        + [shape((reach, lines)), shape((count, lines))]
        + [shape((lines, 2 * count)), shape((lines, 2 * (reach - count)))]
        + [shape((lines, width), F32)],
        [VMEM] + [ANY] * 10,
        limit=12,
        scratch=[
            pltpu.VMEM((1, lines), jnp.int32),
            pltpu.VMEM((1, lines), jnp.int32),
            pltpu.SemaphoreType.DMA((10,)),
        ],
    )(packs, *in_hbm(nodes, edges, senders, segments, cot_nodes, cot_edges, *weights))


def layer(halos, loaded):
    node, edge, w_edge1 = loaded[0], loaded[1], loaded[4]
    (count, width), lines, rows = node.shape, edge.shape[0], halos[0].shape[0]
    reach = count + 4 * rows
    half = sum(w.shape[0] for w in loaded[4:8]) // 2
    on_edges, on_nodes = shape((lines, width)), shape((count, width))
    send, *state = call(
        layer_kernel,
        [shape((half + rows, width)), on_nodes]
        + [shape((2 * reach, width)), shape((2 * count, width)), on_edges, on_nodes, on_nodes]
        + [on_edges, on_edges, on_nodes, on_nodes]
        + [shape((2 * reach, width)), shape((2 * count, width))]
        + [shape((lines, width), F32), shape((count, width), F32)],
        [VMEM] * (4 + len(loaded)),
        limit=16,
    )(*halos, *loaded)
    keep, node_next, grad_edges, d_node, *backs = call(
        rest_kernel,
        [shape((half, width)), shape((1, 1, count, width)), shape((1, 1, lines, width))]
        + [shape((count, width), F32)]
        + [shape((rows, width))] * 3,
        [VMEM] * (3 + len(state)),
        limit=12,
        scratch=[pltpu.VMEM((reach, width), F32)],
        cost_estimate=pl.CostEstimate(
            flops=2 * width * width * (4 * lines + 8 * reach),
            bytes_accessed=12 << 20,
            transcendentals=0,
        ),
    )(node, edge, w_edge1, *state)
    return node_next, send, keep, grad_edges, d_node, backs


def local(
    nodes,
    edges,
    senders,
    segments,
    send_lists,
    cot_nodes,
    cot_edges,
    w_edge1,
    w_edge2,
    w_node1,
    w_node2,
):
    count, width = nodes.shape[2:]
    lines = edges.shape[2]
    rows = send_lists.shape[3]
    weights = (w_edge1, w_edge2, w_node1, w_node2)
    total = sum(w.shape[0] for w in weights)
    block = [shape((rows, width))] * 4
    packs = call(
        pack_kernel,
        block,
        [ANY] * 2,
        scratch=[
            pltpu.VMEM((count, width), BF),
            pltpu.VMEM((4, rows), jnp.int32),
            pltpu.SemaphoreType.DMA((2,)),
        ],
    )(*in_hbm(nodes, send_lists))
    halos = exchange(packs, range(4))
    loaded = load(packs[3], nodes, edges, senders, segments, cot_nodes, cot_edges, weights)
    node_next, send, keep, grad_edges, d_node, backs = layer(halos, loaded)

    got = lax.ppermute(send, "c", pairs(2, 0))
    pair, core_back = call(
        pair_sum_kernel, [shape(keep.shape), shape((rows, width))], [VMEM] * 2, limit=8
    )(keep, got)

    near, ring, far = groups()
    n_near, n_ring, n_far = len(near[0]), len(ring[0]), len(far[0])
    mid = total // 2 // n_near
    strip = mid // n_ring
    factor = float(lines * 2 * n_near * n_ring * n_far) ** -0.5
    pieces = swap(pair, near).reshape(n_near, mid, width)
    pieces = call(near_sum_kernel, shape((mid, width)), [VMEM], limit=8)(pieces)
    pieces = swap(pieces, ring).reshape(n_ring, strip, width)
    pieces, *backs = call(
        ring_sum_kernel, [shape((n_far, strip, width))] + block[:3], [VMEM] * 4, limit=8
    )(pieces, *backs)
    returned = exchange(backs, CHIP_STEPS)
    pieces = swap(pieces, far)
    pieces, *returned = call(
        functools.partial(far_sum_kernel, factor),
        [shape((n_ring, strip, width))] + block[:3],
        [VMEM] * 4,
        limit=8,
    )(pieces, *returned)
    pieces = swap(pieces, ring).reshape(mid, width)
    pieces = call(spread_kernel, shape((n_near, mid, width)), [VMEM], limit=8)(pieces)
    mine = swap(pieces, near).reshape(total // 2, width)
    other = lax.ppermute(mine, "c", pairs(2, 0))
    outs = [shape(w.shape) for w in weights]
    small = pltpu.CompilerParams(vmem_limit_bytes=4 << 20)
    sems = [pltpu.SemaphoreType.DMA((total // width,))]
    *grads, grad_nodes = pl.pallas_call(
        own_kernel,
        out_shape=outs + [shape(nodes.shape)],
        in_specs=[VMEM] * 7,
        out_specs=[ANY] * 4 + [VMEM],
        scratch_shapes=sems,
        compiler_params=small,
    )(mine, d_node, send_lists, core_back, *returned)
    grads = pl.pallas_call(
        other_kernel,
        out_shape=outs,
        in_specs=[VMEM] + [ANY] * 4,
        out_specs=[ANY] * 4,
        scratch_shapes=sems,
        compiler_params=small,
        input_output_aliases={1: 0, 2: 1, 3: 2, 4: 3},
    )(other, *grads)
    return (node_next, grad_nodes, grad_edges, *grads)


def solution(mesh):
    fine = Mesh(mesh.devices.reshape(2, 4, 2, 2, 4, 2), ("yh", "x", "c", "yl", "zh", "zl"))
    tile = P(GX, GY)
    return jax.shard_map(
        local,
        mesh=fine,
        in_specs=(tile,) * 7 + (P(),) * 4,
        out_specs=(tile,) * 3 + (P(),) * 4,
        check_vma=False,
    )
```

```python
import functools

import jax
import jax.numpy as jnp
from jax import lax
from jax.experimental import pallas as pl
from jax.experimental.pallas import tpu as pltpu
from jax.sharding import Mesh
from jax.sharding import PartitionSpec as P

BF = jnp.bfloat16
F32 = jnp.float32
GX = ("yh", "x", "c")
GY = ("yl", "zh", "zl")
ALL = ("yh", "x", "c", "yl", "zh", "zl")


def place(x, y, core, z):
    return ((y // 2 * 4 + x) * 2 + core) * 16 + y % 2 * 8 + z % 8


def groups():
    four, lines = range(4), [(o, k) for o in range(4) for k in range(4)]
    near = [[place(k, o, 0, 2 * p + b) for k in four for b in (0, 1)] for o, p in lines]
    near += [[place(o, k, 1, 2 * p + 1 + b) for k in four for b in (0, 1)] for o, p in lines]
    ring = [[place(o, k, 0, z) for k in four] for o in four for z in range(8)]
    ring += [[place(k, o, 1, z) for k in four] for o in four for z in range(8)]
    far = [[place(x, y, c, 2 * p + b + c) for p in four] for x, y in lines for c in (0, 1) for b in (0, 1)]
    return near, ring, far
VMEM = pl.BlockSpec(memory_space=pltpu.VMEM)
ANY = pl.BlockSpec(memory_space=pl.ANY)


def dot(left, right):
    return jnp.dot(left, right, preferred_element_type=F32)


def dot_rows(left, right):
    return lax.dot_general(left, right, (((0,), (0,)), ((), ())), preferred_element_type=F32)


def dot_cols(left, right):
    return lax.dot_general(left, right, (((1,), (1,)), ((), ())), preferred_element_type=F32)


def hi_lo(values):
    high = values.astype(BF)
    low = (values - high.astype(F32)).astype(BF)
    return jnp.concatenate([high, low], axis=0)


def fold(values):
    half = values.shape[0] // 2
    return values[:half] + values[half:]


def layer_norm(values):
    mean = jnp.mean(values, axis=-1, keepdims=True)
    centred = values - mean
    scale = lax.rsqrt(jnp.mean(centred * centred, axis=-1, keepdims=True) + 1e-05)
    return centred * scale, scale


def norm_back(grad, normed, scale):
    first = jnp.mean(grad, axis=-1, keepdims=True)
    second = jnp.mean(grad * normed, axis=-1, keepdims=True)
    return scale * (grad - first - normed * second)


def silu_and_slope(values):
    sig = 1.0 / (1.0 + jnp.exp(-values))
    return values * sig, sig * (1.0 + values * (1.0 - sig))


def pick(row, count):
    rows = lax.broadcasted_iota(jnp.int32, (count, row.shape[-1]), 0)
    return jnp.where(rows == row, 1.0, 0.0)


def fetch(sources, targets, sems):
    copies = [
        pltpu.make_async_copy(source, target, sems.at[i])
        for i, (source, target) in enumerate(zip(sources, targets, strict=True))
    ]
    for copy in copies:
        copy.start()

    def ready(i):
        copies[i].wait()
        return targets[i]

    return ready


def parities():
    return lax.axis_index("c"), lax.axis_index("zl")


CORE_STEP, CHIP_STEPS = 2, (0, 1, 3)


def side_of(step, row_odd, col_odd):
    return (2 + col_odd, row_odd, 1 - row_odd, 3 - col_odd)[step]


def pack_kernel(nodes_hbm, lists_hbm, *refs):
    packs, (nodes, lists, sems) = refs[:4], refs[4:]
    ready = fetch((nodes_hbm.at[0, 0], lists_hbm.at[0, 0]), (nodes, lists), sems)
    odd = parities()
    ready(1)
    lat = ready(0)[...]
    for step in range(4):
        row = lists[pl.ds(side_of(step, *odd), 1), :]
        packs[step][...] = dot_rows(pick(row, lat.shape[0]).astype(BF), lat).astype(BF)


def load_kernel(
    packs,
    nodes_hbm,
    edges_hbm,
    senders_hbm,
    segments_hbm,
    cot_nodes_hbm,
    cot_edges_hbm,
    w_edge1_hbm,
    w_edge2_hbm,
    w_node1_hbm,
    w_node2_hbm,
    node,
    edge,
    cot_node,
    cot_edge,
    w_edge1,
    w_edge2,
    w_node1,
    w_node2,
    to_ext,
    to_node,
    from_node,
    from_halo,
    z_part,
    senders,
    segments,
    sems,
):
    del packs
    ready = fetch(
        (
            senders_hbm.at[0],
            segments_hbm.at[0],
            nodes_hbm.at[0, 0],
            w_edge1_hbm,
            edges_hbm.at[0, 0],
            w_edge2_hbm,
            w_node1_hbm,
            w_node2_hbm,
            cot_nodes_hbm.at[0, 0],
            cot_edges_hbm.at[0, 0],
        ),
        (
            senders,
            segments,
            node,
            w_edge1,
            edge,
            w_edge2,
            w_node1,
            w_node2,
            cot_node,
            cot_edge,
        ),
        sems,
    )
    count, width = node.shape
    by_send = pick(ready(0)[...], to_ext.shape[0])
    by_recv = pick(ready(1)[...], count)
    to_ext[...] = by_send.astype(BF)
    to_node[...] = by_recv.astype(BF)
    own = by_send[:count].T.astype(BF)
    halo = by_send[count:].T.astype(BF)
    recv = by_recv.T.astype(BF)
    from_halo[...] = jnp.concatenate([halo, halo], axis=1)
    from_node[...] = jnp.concatenate([recv, recv], axis=1)
    wide = jnp.concatenate([own, own, recv, recv], axis=1)
    lat = ready(2)[...]
    ready(3)
    terms = jnp.concatenate(
        [
            hi_lo(dot(lat, w_edge1[width : 2 * width, :])),
            hi_lo(dot(lat, w_edge1[2 * width :, :])),
        ],
        axis=0,
    )
    z_part[...] = dot(ready(4)[...], w_edge1[:width, :]) + dot(wide, terms)
    for i in range(5, 10):
        ready(i)


def put_half(target, side, pairs_of_block):
    for block, (left, right) in enumerate(pairs_of_block):
        part = left.shape[1] // 2
        columns = pl.ds(pl.multiple_of(side * part, part), part)
        target[block * part : (block + 1) * part, :] = dot_rows(
            left[:, columns], right[...]
        ).astype(BF)


def layer_kernel(
    halo0,
    halo1,
    halo2,
    halo3,
    node,
    edge,
    cot_node,
    cot_edge,
    w_edge1,
    w_edge2,
    w_node1,
    w_node2,
    to_node,
    from_node,
    from_halo,
    z_part,
    send,
    next_node,
    ext_twice,
    node_twice,
    a_one,
    agg,
    a_three,
    dz_two,
    dz_three,
    dz_four,
    de_new,
    slope_one,
):
    odd = parities()
    count, width = node.shape
    rows = halo0.shape[0]
    reach = ext_twice.shape[0] // 2
    lat = node[...]
    for start in (0, reach):
        ext_twice[start : start + count, :] = lat
        for step, halo in enumerate((halo0, halo1, halo2, halo3)):
            place = start + count + side_of(step, *odd) * rows
            ext_twice[pl.ds(pl.multiple_of(place, rows), rows), :] = halo[...]
    for start in (0, count):
        node_twice[start : start + count, :] = lat

    terms = hi_lo(dot(ext_twice[count:reach, :], w_edge1[width : 2 * width, :]))
    z_one = z_part[...] + dot(from_halo[...], terms)
    act, slope_one[...] = silu_and_slope(z_one)
    a_one[...] = act.astype(BF)
    n_two, s_two = layer_norm(dot(a_one[...], w_edge2[...]))
    e_new = (edge[...].astype(F32) + n_two).astype(BF)
    agg[...] = dot(to_node[...], e_new).astype(BF)
    z_three = dot(lat, w_node1[:width, :]) + dot(agg[...], w_node1[width:, :])
    act, slope_three = silu_and_slope(z_three)
    a_three[...] = act.astype(BF)
    n_four, s_four = layer_norm(dot(a_three[...], w_node2[...]))
    next_node[...] = (lat.astype(F32) + n_four).astype(BF)

    g_node = cot_node[...].astype(F32)
    dz_four[...] = norm_back(g_node, n_four, s_four).astype(BF)
    dz_three[...] = (dot_cols(dz_four[...], w_node2[...]) * slope_three).astype(BF)
    dy_agg = dot_cols(dz_three[...], w_node1[width:, :])

    de = cot_edge[...].astype(F32) + dot(from_node[...], hi_lo(dy_agg))
    de_new[...] = de
    dz_two[...] = norm_back(de, n_two, s_two).astype(BF)
    put_half(
        send,
        1 - odd[0],
        ((a_one, dz_two), (node, dz_three), (agg, dz_three), (a_three, dz_four)),
    )


def first_kernel(
    edge,
    w_edge1,
    w_edge2,
    to_ext,
    to_node,
    ext_twice,
    node_twice,
    dz_two,
    slope_one,
    send,
    dz_one,
    sum_send,
    sum_recv,
):
    odd = parities()
    width = edge.shape[1]
    reach, count = to_ext.shape[0], to_node.shape[0]
    dz_one[...] = (dot_cols(dz_two[...], w_edge2[...]) * slope_one[...]).astype(BF)
    sum_send[...] = hi_lo(dot(to_ext[...], dz_one[...]))
    sum_recv[...] = hi_lo(dot(to_node[...], dz_one[...]))
    rows = (reach - count) // 4
    first = count + side_of(CORE_STEP, *odd) * rows
    ride = jnp.concatenate(
        [
            sum_send[pl.ds(pl.multiple_of(first, rows), rows), :],
            sum_send[pl.ds(pl.multiple_of(reach + first, rows), rows), :],
        ],
        axis=0,
    )
    send[send.shape[0] - rows :, :] = fold(dot_cols(ride, w_edge1[width : 2 * width, :])).astype(BF)
    put_half(
        send, 1 - odd[0], ((edge, dz_one), (ext_twice, sum_send), (node_twice, sum_recv))
    )


def rest_kernel(
    node,
    edge,
    cot_node,
    w_edge1,
    w_node1,
    next_node,
    ext_twice,
    node_twice,
    a_one,
    agg,
    a_three,
    dz_two,
    dz_three,
    dz_four,
    de_new,
    dz_one,
    sum_send,
    sum_recv,
    keep,
    node_next,
    grad_edges,
    d_node,
    back0,
    back1,
    back2,
    d_ext,
):
    node_next[0, 0] = next_node[...]
    odd = parities()
    count, width = node.shape
    rows = back0.shape[0]
    put_half(
        keep,
        odd[0],
        (
            (edge, dz_one),
            (ext_twice, sum_send),
            (node_twice, sum_recv),
            (a_one, dz_two),
            (node, dz_three),
            (agg, dz_three),
            (a_three, dz_four),
        ),
    )
    grad_edges[0, 0] = (de_new[...] + dot_cols(dz_one[...], w_edge1[:width, :])).astype(BF)
    d_ext[...] = fold(dot_cols(sum_send[...], w_edge1[width : 2 * width, :]))
    d_recv = fold(dot_cols(sum_recv[...], w_edge1[2 * width :, :]))
    dy_node = dot_cols(dz_three[...], w_node1[:width, :])
    d_node[...] = cot_node[...].astype(F32) + dy_node + d_recv + d_ext[:count, :]
    for step, back in zip(CHIP_STEPS, (back0, back1, back2), strict=True):
        place = count + side_of(step, *odd) * rows
        back[...] = d_ext[pl.ds(pl.multiple_of(place, rows), rows), :].astype(BF)


def pair_sum_kernel(mine, first, later, out, ret):
    rows = later.shape[0] - ret.shape[0]
    out[:rows, :] = (mine[:rows, :].astype(F32) + later[:rows, :].astype(F32)).astype(BF)
    out[rows:, :] = (mine[rows:, :].astype(F32) + first[...].astype(F32)).astype(BF)
    ret[...] = later[rows:, :]


def sum_parts(parts):
    total = parts[0].astype(F32)
    for part in range(1, parts.shape[0]):
        total = total + parts[part].astype(F32)
    return total


def near_sum_kernel(parts, out):
    out[...] = sum_parts(parts).astype(BF)


def ring_sum_kernel(parts, *refs):
    backs, out, onward = refs[:3], refs[3], refs[4:]
    for back, ref in zip(backs, onward, strict=True):
        ref[...] = back[...]
    total = sum_parts(parts).astype(BF)
    for part in range(out.shape[0]):
        out[part] = total


def far_sum_kernel(factor, parts, *refs):
    returned, out, onward = refs[:3], refs[3], refs[4:]
    for ret, ref in zip(returned, onward, strict=True):
        ref[...] = ret[...]
    total = (sum_parts(parts) * factor).astype(BF)
    for part in range(out.shape[0]):
        out[part] = total


def spread_kernel(whole, out):
    rows = whole[...]
    for part in range(out.shape[0]):
        out[part] = rows


def place_half(side, half, outs, sems):
    part = outs[0].shape[1] // 2
    copies = []
    for out in outs:
        for block in range(out.shape[0] // (2 * part)):
            target = pl.multiple_of((2 * block + side) * part, part)
            start = len(copies) * part
            copies.append(
                pltpu.make_async_copy(
                    half.at[start : start + part], out.at[pl.ds(target, part)], sems.at[len(copies)]
                )
            )
    for copy in copies:
        copy.start()
    return copies


def own_kernel(half, d_node, lists, ret0, ret1, ret2, ret3, *refs):
    outs, grad_nodes, sems = refs[:4], refs[4], refs[5]
    odd = parities()
    copies = place_half(odd[0], half, outs, sems)
    grad = d_node[...]
    for step, ret in zip((CORE_STEP, *CHIP_STEPS), (ret0, ret1, ret2, ret3), strict=True):
        row = lists[0, 0, pl.ds(side_of(step, *odd), 1), :]
        grad = grad + dot(pick(row, grad.shape[0]).astype(BF), ret[...])
    grad_nodes[0, 0] = grad.astype(BF)
    for copy in copies:
        copy.wait()


def other_kernel(half, *refs):
    outs, sems = refs[-5:-1], refs[-1]
    for copy in place_half(1 - parities()[0], half, outs, sems):
        copy.wait()


def call(kernel, outs, ins, limit=24, scratch=(), **kwargs):
    return pl.pallas_call(
        kernel,
        out_shape=outs,
        in_specs=ins,
        out_specs=jax.tree.map(lambda _: VMEM, outs),
        scratch_shapes=list(scratch),
        compiler_params=pltpu.CompilerParams(vmem_limit_bytes=limit << 20),
        **kwargs,
    )


def shape(dims, kind=BF):
    return jax.ShapeDtypeStruct(dims, kind)


def in_hbm(*arrays):
    return [pltpu.with_memory_space_constraint(array, pltpu.HBM) for array in arrays]


def pairs(count, first):
    made = []
    for i in range(first, count + first, 2):
        made += [(i, (i + 1) % count), ((i + 1) % count, i)]
    return made


def exchange(blocks, steps):
    axes = (GY, GX, GX, GY)
    first = (1, 1, 0, 0)
    return [
        lax.ppermute(block, axes[step], pairs(lax.axis_size(axes[step]), first[step]))
        for step, block in zip(steps, blocks, strict=True)
    ]


def swap(rows, groups):
    return lax.all_to_all(rows, ALL, 0, 0, axis_index_groups=groups, tiled=True)


def load(packs, nodes, edges, senders, segments, cot_nodes, cot_edges, weights):
    count, width = nodes.shape[2:]
    lines = edges.shape[2]
    reach = count + 4 * packs.shape[0]
    return call(
        load_kernel,
        [shape((count, width)), shape((lines, width))] * 2
        + [shape(w.shape) for w in weights]
        + [shape((reach, lines)), shape((count, lines))]
        + [shape((lines, 2 * count)), shape((lines, 2 * (reach - count)))]
        + [shape((lines, width), F32)],
        [VMEM] + [ANY] * 10,
        limit=12,
        scratch=[
            pltpu.VMEM((1, lines), jnp.int32),
            pltpu.VMEM((1, lines), jnp.int32),
            pltpu.SemaphoreType.DMA((10,)),
        ],
    )(packs, *in_hbm(nodes, edges, senders, segments, cot_nodes, cot_edges, *weights))


def cost(flops):
    return pl.CostEstimate(flops=flops, bytes_accessed=12 << 20, transcendentals=0)


def layer(halos, loaded):
    node, edge, cot_node, _, w_edge1, w_edge2, w_node1, _, to_ext, to_node = loaded[:10]
    (count, width), lines, rows = node.shape, edge.shape[0], halos[0].shape[0]
    reach = count + 4 * rows
    later = w_edge1.shape[0] // 2
    half = sum(w.shape[0] for w in loaded[4:8]) // 2
    on_edges, on_nodes = shape((lines, width)), shape((count, width))
    on_sums = [shape((2 * reach, width)), shape((2 * count, width))]
    send_first, *state, slope_one = call(
        layer_kernel,
        [shape((half - later, width)), on_nodes]
        + on_sums
        + [on_edges, on_nodes, on_nodes, on_edges, on_nodes, on_nodes]
        + [shape((lines, width), F32)] * 2,
        [VMEM] * (3 + len(loaded)),
        limit=16,
    )(*halos, *loaded[:8], *loaded[9:])
    got_first = lax.ppermute(send_first, "c", pairs(2, 0))
    _, ext_twice, node_twice, _, _, _, dz_two, *_ = state
    send_later, *more = call(
        first_kernel,
        [shape((later + rows, width)), on_edges] + on_sums,
        [VMEM] * 9,
        limit=12,
        cost_estimate=cost(2 * width * width * (2 * lines + 4 * reach)),
    )(edge, w_edge1, w_edge2, to_ext, to_node, ext_twice, node_twice, dz_two, slope_one)
    got_later = lax.ppermute(send_later, "c", pairs(2, 0))
    keep, node_next, grad_edges, d_node, *backs = call(
        rest_kernel,
        [shape((half, width)), shape((1, 1, count, width)), shape((1, 1, lines, width))]
        + [shape((count, width), F32)]
        + [shape((rows, width))] * 3,
        [VMEM] * (5 + len(state) + len(more)),
        limit=12,
        scratch=[pltpu.VMEM((reach, width), F32)],
        cost_estimate=cost(2 * width * width * (4 * lines + 8 * reach)),
    )(node, edge, cot_node, w_edge1, w_node1, *state, *more)
    pair, core_back = call(
        pair_sum_kernel, [shape((half, width)), shape((rows, width))], [VMEM] * 3, limit=8
    )(keep, got_first, got_later)
    return node_next, grad_edges, d_node, backs, pair, core_back


def local(
    nodes,
    edges,
    senders,
    segments,
    send_lists,
    cot_nodes,
    cot_edges,
    w_edge1,
    w_edge2,
    w_node1,
    w_node2,
):
    count, width = nodes.shape[2:]
    lines = edges.shape[2]
    rows = send_lists.shape[3]
    weights = (w_edge1, w_edge2, w_node1, w_node2)
    total = sum(w.shape[0] for w in weights)
    block = [shape((rows, width))] * 4
    packs = call(
        pack_kernel,
        block,
        [ANY] * 2,
        scratch=[
            pltpu.VMEM((count, width), BF),
            pltpu.VMEM((4, rows), jnp.int32),
            pltpu.SemaphoreType.DMA((2,)),
        ],
    )(*in_hbm(nodes, send_lists))
    halos = exchange(packs, range(4))
    loaded = load(packs[3], nodes, edges, senders, segments, cot_nodes, cot_edges, weights)
    node_next, grad_edges, d_node, backs, pair, core_back = layer(halos, loaded)

    near, ring, far = groups()
    n_near, n_ring, n_far = len(near[0]), len(ring[0]), len(far[0])
    mid = total // 2 // n_near
    strip = mid // n_ring
    factor = float(lines * 2 * n_near * n_ring * n_far) ** -0.5
    pieces = swap(pair, near).reshape(n_near, mid, width)
    pieces = call(near_sum_kernel, shape((mid, width)), [VMEM], limit=8)(pieces)
    pieces = swap(pieces, ring).reshape(n_ring, strip, width)
    pieces, *backs = call(
        ring_sum_kernel, [shape((n_far, strip, width))] + block[:3], [VMEM] * 4, limit=8
    )(pieces, *backs)
    returned = exchange(backs, CHIP_STEPS)
    pieces = swap(pieces, far)
    pieces, *returned = call(
        functools.partial(far_sum_kernel, factor),
        [shape((n_ring, strip, width))] + block[:3],
        [VMEM] * 4,
        limit=8,
    )(pieces, *returned)
    pieces = swap(pieces, ring).reshape(mid, width)
    pieces = call(spread_kernel, shape((n_near, mid, width)), [VMEM], limit=8)(pieces)
    mine = swap(pieces, near).reshape(total // 2, width)
    other = lax.ppermute(mine, "c", pairs(2, 0))
    outs = [shape(w.shape) for w in weights]
    small = pltpu.CompilerParams(vmem_limit_bytes=4 << 20)
    sems = [pltpu.SemaphoreType.DMA((total // width,))]
    *grads, grad_nodes = pl.pallas_call(
        own_kernel,
        out_shape=outs + [shape(nodes.shape)],
        in_specs=[VMEM] * 7,
        out_specs=[ANY] * 4 + [VMEM],
        scratch_shapes=sems,
        compiler_params=small,
    )(mine, d_node, send_lists, core_back, *returned)
    grads = pl.pallas_call(
        other_kernel,
        out_shape=outs,
        in_specs=[VMEM] + [ANY] * 4,
        out_specs=[ANY] * 4,
        scratch_shapes=sems,
        compiler_params=small,
        input_output_aliases={1: 0, 2: 1, 3: 2, 4: 3},
    )(other, *grads)
    return (node_next, grad_nodes, grad_edges, *grads)


def solution(mesh):
    fine = Mesh(mesh.devices.reshape(2, 4, 2, 2, 4, 2), ("yh", "x", "c", "yl", "zh", "zl"))
    tile = P(GX, GY)
    return jax.shard_map(
        local,
        mesh=fine,
        in_specs=(tile,) * 7 + (P(),) * 4,
        out_specs=(tile,) * 3 + (P(),) * 4,
        check_vma=False,
    )
```

```python
import functools

import jax
import jax.numpy as jnp
from jax import lax
from jax.experimental import pallas as pl
from jax.experimental.pallas import tpu as pltpu
from jax.sharding import Mesh
from jax.sharding import PartitionSpec as P

BF = jnp.bfloat16
F32 = jnp.float32
GX = ("yh", "x", "c")
GY = ("yl", "zh", "zl")
ALL = ("yh", "x", "c", "yl", "zh", "zl")


def place(x, y, core, z):
    return ((y // 2 * 4 + x) * 2 + core) * 16 + y % 2 * 8 + z % 8


def groups():
    four, lines = range(4), [(o, k) for o in range(4) for k in range(4)]
    both = ((0, 0), (2, 1), (1, 1), (3, 0), (0, 1), (2, 0), (1, 0), (3, 1))
    turn = (0, 1, 3, 2)
    near = [[place(k, o, 0, 2 * p + b) for k, b in both] for o, p in lines]
    near += [[place(o, k, 1, 2 * p + 1 + b) for k, b in both] for o, p in lines]
    ring = [[place(o, k, 0, z) for k in turn] for o in four for z in range(8)]
    ring += [[place(k, o, 1, z) for k in turn] for o in four for z in range(8)]
    far = [[place(x, y, c, 2 * p + b + c) for p in four] for x, y in lines for c in (0, 1) for b in (0, 1)]
    return near, ring, far
VMEM = pl.BlockSpec(memory_space=pltpu.VMEM)
ANY = pl.BlockSpec(memory_space=pl.ANY)


def dot(left, right):
    return jnp.dot(left, right, preferred_element_type=F32)


def dot_rows(left, right):
    return lax.dot_general(left, right, (((0,), (0,)), ((), ())), preferred_element_type=F32)


def dot_cols(left, right):
    return lax.dot_general(left, right, (((1,), (1,)), ((), ())), preferred_element_type=F32)


def hi_lo(values):
    high = values.astype(BF)
    low = (values - high.astype(F32)).astype(BF)
    return jnp.concatenate([high, low], axis=0)


def fold(values):
    half = values.shape[0] // 2
    return values[:half] + values[half:]


def layer_norm(values):
    mean = jnp.mean(values, axis=-1, keepdims=True)
    centred = values - mean
    scale = lax.rsqrt(jnp.mean(centred * centred, axis=-1, keepdims=True) + 1e-05)
    return centred * scale, scale


def norm_back(grad, normed, scale):
    first = jnp.mean(grad, axis=-1, keepdims=True)
    second = jnp.mean(grad * normed, axis=-1, keepdims=True)
    return scale * (grad - first - normed * second)


def silu_and_slope(values):
    sig = 1.0 / (1.0 + jnp.exp(-values))
    return values * sig, sig * (1.0 + values * (1.0 - sig))


def pick(row, count):
    rows = lax.broadcasted_iota(jnp.int32, (count, row.shape[-1]), 0)
    return jnp.where(rows == row, 1.0, 0.0)


def fetch(sources, targets, sems):
    copies = [
        pltpu.make_async_copy(source, target, sems.at[i])
        for i, (source, target) in enumerate(zip(sources, targets, strict=True))
    ]
    for copy in copies:
        copy.start()

    def ready(i):
        copies[i].wait()
        return targets[i]

    return ready


def parities():
    return lax.axis_index("c"), lax.axis_index("zl")


CORE_STEP, CHIP_STEPS = 2, (0, 1, 3)


def side_of(step, row_odd, col_odd):
    return (2 + col_odd, row_odd, 1 - row_odd, 3 - col_odd)[step]


def pack_kernel(nodes_hbm, lists_hbm, *refs):
    packs, (nodes, lists, sems) = refs[:4], refs[4:]
    ready = fetch((nodes_hbm.at[0, 0], lists_hbm.at[0, 0]), (nodes, lists), sems)
    odd = parities()
    ready(1)
    lat = ready(0)[...]
    for step in range(4):
        row = lists[pl.ds(side_of(step, *odd), 1), :]
        packs[step][...] = dot_rows(pick(row, lat.shape[0]).astype(BF), lat).astype(BF)


def load_kernel(
    packs,
    nodes_hbm,
    edges_hbm,
    senders_hbm,
    segments_hbm,
    cot_nodes_hbm,
    cot_edges_hbm,
    w_edge1_hbm,
    w_edge2_hbm,
    w_node1_hbm,
    w_node2_hbm,
    node,
    edge,
    cot_node,
    cot_edge,
    w_edge1,
    w_edge2,
    w_node1,
    w_node2,
    to_ext,
    to_node,
    from_node,
    from_halo,
    z_part,
    senders,
    segments,
    sems,
):
    del packs
    ready = fetch(
        (
            senders_hbm.at[0],
            segments_hbm.at[0],
            nodes_hbm.at[0, 0],
            w_edge1_hbm,
            edges_hbm.at[0, 0],
            w_edge2_hbm,
            w_node1_hbm,
            w_node2_hbm,
            cot_nodes_hbm.at[0, 0],
            cot_edges_hbm.at[0, 0],
        ),
        (
            senders,
            segments,
            node,
            w_edge1,
            edge,
            w_edge2,
            w_node1,
            w_node2,
            cot_node,
            cot_edge,
        ),
        sems,
    )
    count, width = node.shape
    by_send = pick(ready(0)[...], to_ext.shape[0])
    by_recv = pick(ready(1)[...], count)
    to_ext[...] = by_send.astype(BF)
    to_node[...] = by_recv.astype(BF)
    own = by_send[:count].T.astype(BF)
    halo = by_send[count:].T.astype(BF)
    recv = by_recv.T.astype(BF)
    from_halo[...] = jnp.concatenate([halo, halo], axis=1)
    from_node[...] = jnp.concatenate([recv, recv], axis=1)
    wide = jnp.concatenate([own, own, recv, recv], axis=1)
    lat = ready(2)[...]
    ready(3)
    terms = jnp.concatenate(
        [
            hi_lo(dot(lat, w_edge1[width : 2 * width, :])),
            hi_lo(dot(lat, w_edge1[2 * width :, :])),
        ],
        axis=0,
    )
    z_part[...] = dot(ready(4)[...], w_edge1[:width, :]) + dot(wide, terms)
    for i in range(5, 10):
        ready(i)


def put_half(target, side, pairs_of_block):
    for block, (left, right) in enumerate(pairs_of_block):
        part = left.shape[1] // 2
        columns = pl.ds(pl.multiple_of(side * part, part), part)
        target[block * part : (block + 1) * part, :] = dot_rows(
            left[:, columns], right[...]
        ).astype(BF)


def layer_kernel(
    halo0,
    halo1,
    halo2,
    halo3,
    node,
    edge,
    cot_node,
    cot_edge,
    w_edge1,
    w_edge2,
    w_node1,
    w_node2,
    to_node,
    from_node,
    from_halo,
    z_part,
    send,
    next_node,
    ext_twice,
    node_twice,
    a_one,
    agg,
    a_three,
    dz_two,
    dz_three,
    dz_four,
    de_new,
    slope_one,
):
    odd = parities()
    count, width = node.shape
    rows = halo0.shape[0]
    reach = ext_twice.shape[0] // 2
    lat = node[...]
    for start in (0, reach):
        ext_twice[start : start + count, :] = lat
        for step, halo in enumerate((halo0, halo1, halo2, halo3)):
            place = start + count + side_of(step, *odd) * rows
            ext_twice[pl.ds(pl.multiple_of(place, rows), rows), :] = halo[...]
    for start in (0, count):
        node_twice[start : start + count, :] = lat

    terms = hi_lo(dot(ext_twice[count:reach, :], w_edge1[width : 2 * width, :]))
    z_one = z_part[...] + dot(from_halo[...], terms)
    act, slope_one[...] = silu_and_slope(z_one)
    a_one[...] = act.astype(BF)
    n_two, s_two = layer_norm(dot(a_one[...], w_edge2[...]))
    e_new = (edge[...].astype(F32) + n_two).astype(BF)
    agg[...] = dot(to_node[...], e_new).astype(BF)
    z_three = dot(lat, w_node1[:width, :]) + dot(agg[...], w_node1[width:, :])
    act, slope_three = silu_and_slope(z_three)
    a_three[...] = act.astype(BF)
    n_four, s_four = layer_norm(dot(a_three[...], w_node2[...]))
    next_node[...] = (lat.astype(F32) + n_four).astype(BF)

    g_node = cot_node[...].astype(F32)
    dz_four[...] = norm_back(g_node, n_four, s_four).astype(BF)
    dz_three[...] = (dot_cols(dz_four[...], w_node2[...]) * slope_three).astype(BF)
    dy_agg = dot_cols(dz_three[...], w_node1[width:, :])

    de = cot_edge[...].astype(F32) + dot(from_node[...], hi_lo(dy_agg))
    de_new[...] = de
    dz_two[...] = norm_back(de, n_two, s_two).astype(BF)
    put_half(
        send,
        1 - odd[0],
        ((a_one, dz_two), (node, dz_three), (agg, dz_three), (a_three, dz_four)),
    )


def first_kernel(
    edge,
    w_edge1,
    w_edge2,
    to_ext,
    to_node,
    ext_twice,
    node_twice,
    dz_two,
    slope_one,
    send,
    dz_one,
    sum_send,
    sum_recv,
):
    odd = parities()
    width = edge.shape[1]
    reach, count = to_ext.shape[0], to_node.shape[0]
    dz_one[...] = (dot_cols(dz_two[...], w_edge2[...]) * slope_one[...]).astype(BF)
    sum_send[...] = hi_lo(dot(to_ext[...], dz_one[...]))
    sum_recv[...] = hi_lo(dot(to_node[...], dz_one[...]))
    rows = (reach - count) // 4
    first = count + side_of(CORE_STEP, *odd) * rows
    ride = jnp.concatenate(
        [
            sum_send[pl.ds(pl.multiple_of(first, rows), rows), :],
            sum_send[pl.ds(pl.multiple_of(reach + first, rows), rows), :],
        ],
        axis=0,
    )
    send[send.shape[0] - rows :, :] = fold(dot_cols(ride, w_edge1[width : 2 * width, :])).astype(BF)
    put_half(
        send, 1 - odd[0], ((edge, dz_one), (ext_twice, sum_send), (node_twice, sum_recv))
    )


def rest_kernel(
    node,
    edge,
    cot_node,
    w_edge1,
    w_node1,
    next_node,
    ext_twice,
    node_twice,
    a_one,
    agg,
    a_three,
    dz_two,
    dz_three,
    dz_four,
    de_new,
    dz_one,
    sum_send,
    sum_recv,
    keep,
    node_next,
    grad_edges,
    d_node,
    back0,
    back1,
    back2,
    d_ext,
):
    node_next[0, 0] = next_node[...]
    odd = parities()
    count, width = node.shape
    rows = back0.shape[0]
    put_half(
        keep,
        odd[0],
        (
            (edge, dz_one),
            (ext_twice, sum_send),
            (node_twice, sum_recv),
            (a_one, dz_two),
            (node, dz_three),
            (agg, dz_three),
            (a_three, dz_four),
        ),
    )
    grad_edges[0, 0] = (de_new[...] + dot_cols(dz_one[...], w_edge1[:width, :])).astype(BF)
    d_ext[...] = fold(dot_cols(sum_send[...], w_edge1[width : 2 * width, :]))
    d_recv = fold(dot_cols(sum_recv[...], w_edge1[2 * width :, :]))
    dy_node = dot_cols(dz_three[...], w_node1[:width, :])
    d_node[...] = cot_node[...].astype(F32) + dy_node + d_recv + d_ext[:count, :]
    for step, back in zip(CHIP_STEPS, (back0, back1, back2), strict=True):
        place = count + side_of(step, *odd) * rows
        back[...] = d_ext[pl.ds(pl.multiple_of(place, rows), rows), :].astype(BF)


def pair_sum_kernel(mine, first, later, out, ret):
    rows = later.shape[0] - ret.shape[0]
    out[:rows, :] = (mine[:rows, :].astype(F32) + later[:rows, :].astype(F32)).astype(BF)
    out[rows:, :] = (mine[rows:, :].astype(F32) + first[...].astype(F32)).astype(BF)
    ret[...] = later[rows:, :]


def sum_parts(parts):
    total = parts[0].astype(F32)
    for part in range(1, parts.shape[0]):
        total = total + parts[part].astype(F32)
    return total


def near_sum_kernel(parts, out):
    out[...] = sum_parts(parts).astype(BF)


def ring_sum_kernel(parts, *refs):
    backs, out, onward = refs[:3], refs[3], refs[4:]
    for back, ref in zip(backs, onward, strict=True):
        ref[...] = back[...]
    total = sum_parts(parts).astype(BF)
    for part in range(out.shape[0]):
        out[part] = total


def far_sum_kernel(factor, parts, *refs):
    returned, out, onward = refs[:3], refs[3], refs[4:]
    for ret, ref in zip(returned, onward, strict=True):
        ref[...] = ret[...]
    total = (sum_parts(parts) * factor).astype(BF)
    for part in range(out.shape[0]):
        out[part] = total


def spread_kernel(whole, out):
    rows = whole[...]
    for part in range(out.shape[0]):
        out[part] = rows


def place_half(side, half, outs, sems):
    part = outs[0].shape[1] // 2
    copies = []
    for out in outs:
        for block in range(out.shape[0] // (2 * part)):
            target = pl.multiple_of((2 * block + side) * part, part)
            start = len(copies) * part
            copies.append(
                pltpu.make_async_copy(
                    half.at[start : start + part], out.at[pl.ds(target, part)], sems.at[len(copies)]
                )
            )
    for copy in copies:
        copy.start()
    return copies


def own_kernel(half, d_node, lists, ret0, ret1, ret2, ret3, *refs):
    outs, grad_nodes, sems = refs[:4], refs[4], refs[5]
    odd = parities()
    copies = place_half(odd[0], half, outs, sems)
    grad = d_node[...]
    for step, ret in zip((CORE_STEP, *CHIP_STEPS), (ret0, ret1, ret2, ret3), strict=True):
        row = lists[0, 0, pl.ds(side_of(step, *odd), 1), :]
        grad = grad + dot(pick(row, grad.shape[0]).astype(BF), ret[...])
    grad_nodes[0, 0] = grad.astype(BF)
    for copy in copies:
        copy.wait()


def other_kernel(half, *refs):
    outs, sems = refs[-5:-1], refs[-1]
    for copy in place_half(1 - parities()[0], half, outs, sems):
        copy.wait()


def call(kernel, outs, ins, limit=24, scratch=(), **kwargs):
    return pl.pallas_call(
        kernel,
        out_shape=outs,
        in_specs=ins,
        out_specs=jax.tree.map(lambda _: VMEM, outs),
        scratch_shapes=list(scratch),
        compiler_params=pltpu.CompilerParams(vmem_limit_bytes=limit << 20),
        **kwargs,
    )


def shape(dims, kind=BF):
    return jax.ShapeDtypeStruct(dims, kind)


def in_hbm(*arrays):
    return [pltpu.with_memory_space_constraint(array, pltpu.HBM) for array in arrays]


def pairs(count, first):
    made = []
    for i in range(first, count + first, 2):
        made += [(i, (i + 1) % count), ((i + 1) % count, i)]
    return made


def exchange(blocks, steps):
    axes = (GY, GX, GX, GY)
    first = (1, 1, 0, 0)
    return [
        lax.ppermute(block, axes[step], pairs(lax.axis_size(axes[step]), first[step]))
        for step, block in zip(steps, blocks, strict=True)
    ]


def swap(rows, groups):
    return lax.all_to_all(rows, ALL, 0, 0, axis_index_groups=groups, tiled=True)


def load(packs, nodes, edges, senders, segments, cot_nodes, cot_edges, weights):
    count, width = nodes.shape[2:]
    lines = edges.shape[2]
    reach = count + 4 * packs.shape[0]
    return call(
        load_kernel,
        [shape((count, width)), shape((lines, width))] * 2
        + [shape(w.shape) for w in weights]
        + [shape((reach, lines)), shape((count, lines))]
        + [shape((lines, 2 * count)), shape((lines, 2 * (reach - count)))]
        + [shape((lines, width), F32)],
        [VMEM] + [ANY] * 10,
        limit=12,
        scratch=[
            pltpu.VMEM((1, lines), jnp.int32),
            pltpu.VMEM((1, lines), jnp.int32),
            pltpu.SemaphoreType.DMA((10,)),
        ],
    )(packs, *in_hbm(nodes, edges, senders, segments, cot_nodes, cot_edges, *weights))


def cost(flops):
    return pl.CostEstimate(flops=flops, bytes_accessed=12 << 20, transcendentals=0)


def layer(halos, loaded):
    node, edge, cot_node, _, w_edge1, w_edge2, w_node1, _, to_ext, to_node = loaded[:10]
    (count, width), lines, rows = node.shape, edge.shape[0], halos[0].shape[0]
    reach = count + 4 * rows
    later = w_edge1.shape[0] // 2
    half = sum(w.shape[0] for w in loaded[4:8]) // 2
    on_edges, on_nodes = shape((lines, width)), shape((count, width))
    on_sums = [shape((2 * reach, width)), shape((2 * count, width))]
    send_first, *state, slope_one = call(
        layer_kernel,
        [shape((half - later, width)), on_nodes]
        + on_sums
        + [on_edges, on_nodes, on_nodes, on_edges, on_nodes, on_nodes]
        + [shape((lines, width), F32)] * 2,
        [VMEM] * (3 + len(loaded)),
        limit=16,
    )(*halos, *loaded[:8], *loaded[9:])
    got_first = lax.ppermute(send_first, "c", pairs(2, 0))
    _, ext_twice, node_twice, _, _, _, dz_two, *_ = state
    send_later, *more = call(
        first_kernel,
        [shape((later + rows, width)), on_edges] + on_sums,
        [VMEM] * 9,
        limit=12,
        cost_estimate=cost(2 * width * width * (2 * lines + 4 * reach)),
    )(edge, w_edge1, w_edge2, to_ext, to_node, ext_twice, node_twice, dz_two, slope_one)
    got_later = lax.ppermute(send_later, "c", pairs(2, 0))
    keep, node_next, grad_edges, d_node, *backs = call(
        rest_kernel,
        [shape((half, width)), shape((1, 1, count, width)), shape((1, 1, lines, width))]
        + [shape((count, width), F32)]
        + [shape((rows, width))] * 3,
        [VMEM] * (5 + len(state) + len(more)),
        limit=12,
        scratch=[pltpu.VMEM((reach, width), F32)],
        cost_estimate=cost(2 * width * width * (4 * lines + 8 * reach)),
    )(node, edge, cot_node, w_edge1, w_node1, *state, *more)
    pair, core_back = call(
        pair_sum_kernel, [shape((half, width)), shape((rows, width))], [VMEM] * 3, limit=8
    )(keep, got_first, got_later)
    return node_next, grad_edges, d_node, backs, pair, core_back


def local(
    nodes,
    edges,
    senders,
    segments,
    send_lists,
    cot_nodes,
    cot_edges,
    w_edge1,
    w_edge2,
    w_node1,
    w_node2,
):
    count, width = nodes.shape[2:]
    lines = edges.shape[2]
    rows = send_lists.shape[3]
    weights = (w_edge1, w_edge2, w_node1, w_node2)
    total = sum(w.shape[0] for w in weights)
    block = [shape((rows, width))] * 4
    packs = call(
        pack_kernel,
        block,
        [ANY] * 2,
        scratch=[
            pltpu.VMEM((count, width), BF),
            pltpu.VMEM((4, rows), jnp.int32),
            pltpu.SemaphoreType.DMA((2,)),
        ],
    )(*in_hbm(nodes, send_lists))
    halos = exchange(packs, range(4))
    loaded = load(packs[3], nodes, edges, senders, segments, cot_nodes, cot_edges, weights)
    node_next, grad_edges, d_node, backs, pair, core_back = layer(halos, loaded)

    near, ring, far = groups()
    n_near, n_ring, n_far = len(near[0]), len(ring[0]), len(far[0])
    mid = total // 2 // n_near
    strip = mid // n_ring
    factor = float(lines * 2 * n_near * n_ring * n_far) ** -0.5
    pieces = swap(pair, near).reshape(n_near, mid, width)
    pieces = call(near_sum_kernel, shape((mid, width)), [VMEM], limit=8)(pieces)
    pieces = swap(pieces, ring).reshape(n_ring, strip, width)
    pieces, *backs = call(
        ring_sum_kernel, [shape((n_far, strip, width))] + block[:3], [VMEM] * 4, limit=8
    )(pieces, *backs)
    returned = exchange(backs, CHIP_STEPS)
    pieces = swap(pieces, far)
    pieces, *returned = call(
        functools.partial(far_sum_kernel, factor),
        [shape((n_ring, strip, width))] + block[:3],
        [VMEM] * 4,
        limit=8,
    )(pieces, *returned)
    pieces = swap(pieces, ring).reshape(mid, width)
    pieces = call(spread_kernel, shape((n_near, mid, width)), [VMEM], limit=8)(pieces)
    mine = swap(pieces, near).reshape(total // 2, width)
    other = lax.ppermute(mine, "c", pairs(2, 0))
    outs = [shape(w.shape) for w in weights]
    small = pltpu.CompilerParams(vmem_limit_bytes=4 << 20)
    sems = [pltpu.SemaphoreType.DMA((total // width,))]
    *grads, grad_nodes = pl.pallas_call(
        own_kernel,
        out_shape=outs + [shape(nodes.shape)],
        in_specs=[VMEM] * 7,
        out_specs=[ANY] * 4 + [VMEM],
        scratch_shapes=sems,
        compiler_params=small,
    )(mine, d_node, send_lists, core_back, *returned)
    grads = pl.pallas_call(
        other_kernel,
        out_shape=outs,
        in_specs=[VMEM] + [ANY] * 4,
        out_specs=[ANY] * 4,
        scratch_shapes=sems,
        compiler_params=small,
        input_output_aliases={1: 0, 2: 1, 3: 2, 4: 3},
    )(other, *grads)
    return (node_next, grad_nodes, grad_edges, *grads)


def solution(mesh):
    fine = Mesh(mesh.devices.reshape(2, 4, 2, 2, 4, 2), ("yh", "x", "c", "yl", "zh", "zl"))
    tile = P(GX, GY)
    return jax.shard_map(
        local,
        mesh=fine,
        in_specs=(tile,) * 7 + (P(),) * 4,
        out_specs=(tile,) * 3 + (P(),) * 4,
        check_vma=False,
    )
```

```python
import functools

import jax
import jax.numpy as jnp
from jax import lax
from jax.experimental import pallas as pl
from jax.experimental.pallas import tpu as pltpu
from jax.sharding import Mesh
from jax.sharding import PartitionSpec as P

BF = jnp.bfloat16
F32 = jnp.float32
GX = ("yh", "x", "c")
GY = ("yl", "zh", "zl")
ALL = ("yh", "x", "c", "yl", "zh", "zl")


def place(x, y, core, z):
    return ((y // 2 * 4 + x) * 2 + core) * 16 + y % 2 * 8 + z % 8


def groups():
    four, lines = range(4), [(o, k) for o in range(4) for k in range(4)]
    both = ((0, 0), (3, 1), (2, 0), (1, 1), (0, 1), (3, 0), (2, 1), (1, 0))
    turn = (0, 1, 3, 2)
    near = [[place(k, o, 0, 2 * p + b) for k, b in both] for o, p in lines]
    near += [[place(o, k, 1, 2 * p + 1 + b) for k, b in both] for o, p in lines]
    ring = [[place(o, k, 0, z) for k in turn] for o in four for z in range(8)]
    ring += [[place(k, o, 1, z) for k in turn] for o in four for z in range(8)]
    far = [[place(x, y, c, 2 * p + b + c) for p in four] for x, y in lines for c in (0, 1) for b in (0, 1)]
    return near, ring, far
VMEM = pl.BlockSpec(memory_space=pltpu.VMEM)
ANY = pl.BlockSpec(memory_space=pl.ANY)


def dot(left, right):
    return jnp.dot(left, right, preferred_element_type=F32)


def dot_rows(left, right):
    return lax.dot_general(left, right, (((0,), (0,)), ((), ())), preferred_element_type=F32)


def dot_cols(left, right):
    return lax.dot_general(left, right, (((1,), (1,)), ((), ())), preferred_element_type=F32)


def hi_lo(values):
    high = values.astype(BF)
    low = (values - high.astype(F32)).astype(BF)
    return jnp.concatenate([high, low], axis=0)


def fold(values):
    half = values.shape[0] // 2
    return values[:half] + values[half:]


def layer_norm(values):
    mean = jnp.mean(values, axis=-1, keepdims=True)
    centred = values - mean
    scale = lax.rsqrt(jnp.mean(centred * centred, axis=-1, keepdims=True) + 1e-05)
    return centred * scale, scale


def norm_back(grad, normed, scale):
    first = jnp.mean(grad, axis=-1, keepdims=True)
    second = jnp.mean(grad * normed, axis=-1, keepdims=True)
    return scale * (grad - first - normed * second)


def silu_and_slope(values):
    sig = 1.0 / (1.0 + jnp.exp(-values))
    return values * sig, sig * (1.0 + values * (1.0 - sig))


def pick(row, count):
    rows = lax.broadcasted_iota(jnp.int32, (count, row.shape[-1]), 0)
    return jnp.where(rows == row, 1.0, 0.0)


def fetch(sources, targets, sems):
    copies = [
        pltpu.make_async_copy(source, target, sems.at[i])
        for i, (source, target) in enumerate(zip(sources, targets, strict=True))
    ]
    for copy in copies:
        copy.start()

    def ready(i):
        copies[i].wait()
        return targets[i]

    return ready


def parities():
    return lax.axis_index("c"), lax.axis_index("zl")


CORE_STEP, CHIP_STEPS = 2, (0, 1, 3)


def side_of(step, row_odd, col_odd):
    return (2 + col_odd, row_odd, 1 - row_odd, 3 - col_odd)[step]


def pack_kernel(nodes_hbm, lists_hbm, *refs):
    packs, (nodes, lists, sems) = refs[:4], refs[4:]
    ready = fetch((nodes_hbm.at[0, 0], lists_hbm.at[0, 0]), (nodes, lists), sems)
    odd = parities()
    ready(1)
    lat = ready(0)[...]
    for step in range(4):
        row = lists[pl.ds(side_of(step, *odd), 1), :]
        packs[step][...] = dot_rows(pick(row, lat.shape[0]).astype(BF), lat).astype(BF)


def load_kernel(
    packs,
    nodes_hbm,
    edges_hbm,
    senders_hbm,
    segments_hbm,
    cot_nodes_hbm,
    cot_edges_hbm,
    w_edge1_hbm,
    w_edge2_hbm,
    w_node1_hbm,
    w_node2_hbm,
    node,
    edge,
    cot_node,
    cot_edge,
    w_edge1,
    w_edge2,
    w_node1,
    w_node2,
    to_ext,
    to_node,
    from_node,
    from_halo,
    z_part,
    senders,
    segments,
    sems,
):
    del packs
    ready = fetch(
        (
            senders_hbm.at[0],
            segments_hbm.at[0],
            nodes_hbm.at[0, 0],
            w_edge1_hbm,
            edges_hbm.at[0, 0],
            w_edge2_hbm,
            w_node1_hbm,
            w_node2_hbm,
            cot_nodes_hbm.at[0, 0],
            cot_edges_hbm.at[0, 0],
        ),
        (
            senders,
            segments,
            node,
            w_edge1,
            edge,
            w_edge2,
            w_node1,
            w_node2,
            cot_node,
            cot_edge,
        ),
        sems,
    )
    count, width = node.shape
    by_send = pick(ready(0)[...], to_ext.shape[0])
    by_recv = pick(ready(1)[...], count)
    to_ext[...] = by_send.astype(BF)
    to_node[...] = by_recv.astype(BF)
    own = by_send[:count].T.astype(BF)
    halo = by_send[count:].T.astype(BF)
    recv = by_recv.T.astype(BF)
    from_halo[...] = jnp.concatenate([halo, halo], axis=1)
    from_node[...] = jnp.concatenate([recv, recv], axis=1)
    wide = jnp.concatenate([own, own, recv, recv], axis=1)
    lat = ready(2)[...]
    ready(3)
    terms = jnp.concatenate(
        [
            hi_lo(dot(lat, w_edge1[width : 2 * width, :])),
            hi_lo(dot(lat, w_edge1[2 * width :, :])),
        ],
        axis=0,
    )
    z_part[...] = dot(ready(4)[...], w_edge1[:width, :]) + dot(wide, terms)
    for i in range(5, 10):
        ready(i)


def put_half(target, side, pairs_of_block):
    for block, (left, right) in enumerate(pairs_of_block):
        part = left.shape[1] // 2
        columns = pl.ds(pl.multiple_of(side * part, part), part)
        target[block * part : (block + 1) * part, :] = dot_rows(
            left[:, columns], right[...]
        ).astype(BF)


def layer_kernel(
    halo0,
    halo1,
    halo2,
    halo3,
    node,
    edge,
    cot_node,
    cot_edge,
    w_edge1,
    w_edge2,
    w_node1,
    w_node2,
    to_node,
    from_node,
    from_halo,
    z_part,
    send,
    next_node,
    ext_twice,
    node_twice,
    a_one,
    agg,
    a_three,
    dz_two,
    dz_three,
    dz_four,
    de_new,
    slope_one,
):
    odd = parities()
    count, width = node.shape
    rows = halo0.shape[0]
    reach = ext_twice.shape[0] // 2
    lat = node[...]
    for start in (0, reach):
        ext_twice[start : start + count, :] = lat
        for step, halo in enumerate((halo0, halo1, halo2, halo3)):
            place = start + count + side_of(step, *odd) * rows
            ext_twice[pl.ds(pl.multiple_of(place, rows), rows), :] = halo[...]
    for start in (0, count):
        node_twice[start : start + count, :] = lat

    terms = hi_lo(dot(ext_twice[count:reach, :], w_edge1[width : 2 * width, :]))
    z_one = z_part[...] + dot(from_halo[...], terms)
    act, slope_one[...] = silu_and_slope(z_one)
    a_one[...] = act.astype(BF)
    n_two, s_two = layer_norm(dot(a_one[...], w_edge2[...]))
    e_new = (edge[...].astype(F32) + n_two).astype(BF)
    agg[...] = dot(to_node[...], e_new).astype(BF)
    z_three = dot(lat, w_node1[:width, :]) + dot(agg[...], w_node1[width:, :])
    act, slope_three = silu_and_slope(z_three)
    a_three[...] = act.astype(BF)
    n_four, s_four = layer_norm(dot(a_three[...], w_node2[...]))
    next_node[...] = (lat.astype(F32) + n_four).astype(BF)

    g_node = cot_node[...].astype(F32)
    dz_four[...] = norm_back(g_node, n_four, s_four).astype(BF)
    dz_three[...] = (dot_cols(dz_four[...], w_node2[...]) * slope_three).astype(BF)
    dy_agg = dot_cols(dz_three[...], w_node1[width:, :])

    de = cot_edge[...].astype(F32) + dot(from_node[...], hi_lo(dy_agg))
    de_new[...] = de
    dz_two[...] = norm_back(de, n_two, s_two).astype(BF)
    put_half(
        send,
        1 - odd[0],
        ((a_one, dz_two), (node, dz_three), (agg, dz_three), (a_three, dz_four)),
    )


def first_kernel(
    edge,
    w_edge1,
    w_edge2,
    to_ext,
    to_node,
    ext_twice,
    node_twice,
    dz_two,
    slope_one,
    send,
    dz_one,
    sum_send,
    sum_recv,
):
    odd = parities()
    width = edge.shape[1]
    reach, count = to_ext.shape[0], to_node.shape[0]
    dz_one[...] = (dot_cols(dz_two[...], w_edge2[...]) * slope_one[...]).astype(BF)
    sum_send[...] = hi_lo(dot(to_ext[...], dz_one[...]))
    sum_recv[...] = hi_lo(dot(to_node[...], dz_one[...]))
    rows = (reach - count) // 4
    first = count + side_of(CORE_STEP, *odd) * rows
    ride = jnp.concatenate(
        [
            sum_send[pl.ds(pl.multiple_of(first, rows), rows), :],
            sum_send[pl.ds(pl.multiple_of(reach + first, rows), rows), :],
        ],
        axis=0,
    )
    send[send.shape[0] - rows :, :] = fold(dot_cols(ride, w_edge1[width : 2 * width, :])).astype(BF)
    put_half(
        send, 1 - odd[0], ((edge, dz_one), (ext_twice, sum_send), (node_twice, sum_recv))
    )


def rest_kernel(
    node,
    edge,
    cot_node,
    w_edge1,
    w_node1,
    next_node,
    ext_twice,
    node_twice,
    a_one,
    agg,
    a_three,
    dz_two,
    dz_three,
    dz_four,
    de_new,
    dz_one,
    sum_send,
    sum_recv,
    keep,
    node_next,
    grad_edges,
    d_node,
    back0,
    back1,
    back2,
    d_ext,
):
    node_next[0, 0] = next_node[...]
    odd = parities()
    count, width = node.shape
    rows = back0.shape[0]
    put_half(
        keep,
        odd[0],
        (
            (edge, dz_one),
            (ext_twice, sum_send),
            (node_twice, sum_recv),
            (a_one, dz_two),
            (node, dz_three),
            (agg, dz_three),
            (a_three, dz_four),
        ),
    )
    grad_edges[0, 0] = (de_new[...] + dot_cols(dz_one[...], w_edge1[:width, :])).astype(BF)
    d_ext[...] = fold(dot_cols(sum_send[...], w_edge1[width : 2 * width, :]))
    d_recv = fold(dot_cols(sum_recv[...], w_edge1[2 * width :, :]))
    dy_node = dot_cols(dz_three[...], w_node1[:width, :])
    d_node[...] = cot_node[...].astype(F32) + dy_node + d_recv + d_ext[:count, :]
    for step, back in zip(CHIP_STEPS, (back0, back1, back2), strict=True):
        place = count + side_of(step, *odd) * rows
        back[...] = d_ext[pl.ds(pl.multiple_of(place, rows), rows), :].astype(BF)


def pair_sum_kernel(mine, first, later, out, ret):
    rows = later.shape[0] - ret.shape[0]
    out[:rows, :] = (mine[:rows, :].astype(F32) + later[:rows, :].astype(F32)).astype(BF)
    out[rows:, :] = (mine[rows:, :].astype(F32) + first[...].astype(F32)).astype(BF)
    ret[...] = later[rows:, :]


def sum_parts(parts):
    total = parts[0].astype(F32)
    for part in range(1, parts.shape[0]):
        total = total + parts[part].astype(F32)
    return total


def near_sum_kernel(parts, out):
    out[...] = sum_parts(parts).astype(BF)


def ring_sum_kernel(parts, *refs):
    backs, out, onward = refs[:3], refs[3], refs[4:]
    for back, ref in zip(backs, onward, strict=True):
        ref[...] = back[...]
    total = sum_parts(parts).astype(BF)
    for part in range(out.shape[0]):
        out[part] = total


def far_sum_kernel(factor, parts, *refs):
    returned, out, onward = refs[:3], refs[3], refs[4:]
    for ret, ref in zip(returned, onward, strict=True):
        ref[...] = ret[...]
    total = (sum_parts(parts) * factor).astype(BF)
    for part in range(out.shape[0]):
        out[part] = total


def spread_kernel(whole, out):
    rows = whole[...]
    for part in range(out.shape[0]):
        out[part] = rows


def place_half(side, half, outs, sems):
    part = outs[0].shape[1] // 2
    copies = []
    for out in outs:
        for block in range(out.shape[0] // (2 * part)):
            target = pl.multiple_of((2 * block + side) * part, part)
            start = len(copies) * part
            copies.append(
                pltpu.make_async_copy(
                    half.at[start : start + part], out.at[pl.ds(target, part)], sems.at[len(copies)]
                )
            )
    for copy in copies:
        copy.start()
    return copies


def own_kernel(half, d_node, lists, ret0, ret1, ret2, ret3, *refs):
    outs, grad_nodes, sems = refs[:4], refs[4], refs[5]
    odd = parities()
    copies = place_half(odd[0], half, outs, sems)
    grad = d_node[...]
    for step, ret in zip((CORE_STEP, *CHIP_STEPS), (ret0, ret1, ret2, ret3), strict=True):
        row = lists[0, 0, pl.ds(side_of(step, *odd), 1), :]
        grad = grad + dot(pick(row, grad.shape[0]).astype(BF), ret[...])
    grad_nodes[0, 0] = grad.astype(BF)
    for copy in copies:
        copy.wait()


def other_kernel(half, *refs):
    outs, sems = refs[-5:-1], refs[-1]
    for copy in place_half(1 - parities()[0], half, outs, sems):
        copy.wait()


def call(kernel, outs, ins, limit=24, scratch=(), **kwargs):
    return pl.pallas_call(
        kernel,
        out_shape=outs,
        in_specs=ins,
        out_specs=jax.tree.map(lambda _: VMEM, outs),
        scratch_shapes=list(scratch),
        compiler_params=pltpu.CompilerParams(vmem_limit_bytes=limit << 20),
        **kwargs,
    )


def shape(dims, kind=BF):
    return jax.ShapeDtypeStruct(dims, kind)


def in_hbm(*arrays):
    return [pltpu.with_memory_space_constraint(array, pltpu.HBM) for array in arrays]


def pairs(count, first):
    made = []
    for i in range(first, count + first, 2):
        made += [(i, (i + 1) % count), ((i + 1) % count, i)]
    return made


def exchange(blocks, steps):
    axes = (GY, GX, GX, GY)
    first = (1, 1, 0, 0)
    return [
        lax.ppermute(block, axes[step], pairs(lax.axis_size(axes[step]), first[step]))
        for step, block in zip(steps, blocks, strict=True)
    ]


def swap(rows, groups):
    return lax.all_to_all(rows, ALL, 0, 0, axis_index_groups=groups, tiled=True)


def load(packs, nodes, edges, senders, segments, cot_nodes, cot_edges, weights):
    count, width = nodes.shape[2:]
    lines = edges.shape[2]
    reach = count + 4 * packs.shape[0]
    return call(
        load_kernel,
        [shape((count, width)), shape((lines, width))] * 2
        + [shape(w.shape) for w in weights]
        + [shape((reach, lines)), shape((count, lines))]
        + [shape((lines, 2 * count)), shape((lines, 2 * (reach - count)))]
        + [shape((lines, width), F32)],
        [VMEM] + [ANY] * 10,
        limit=12,
        scratch=[
            pltpu.VMEM((1, lines), jnp.int32),
            pltpu.VMEM((1, lines), jnp.int32),
            pltpu.SemaphoreType.DMA((10,)),
        ],
    )(packs, *in_hbm(nodes, edges, senders, segments, cot_nodes, cot_edges, *weights))


def cost(flops):
    return pl.CostEstimate(flops=flops, bytes_accessed=12 << 20, transcendentals=0)


def layer(halos, loaded):
    node, edge, cot_node, _, w_edge1, w_edge2, w_node1, _, to_ext, to_node = loaded[:10]
    (count, width), lines, rows = node.shape, edge.shape[0], halos[0].shape[0]
    reach = count + 4 * rows
    later = w_edge1.shape[0] // 2
    half = sum(w.shape[0] for w in loaded[4:8]) // 2
    on_edges, on_nodes = shape((lines, width)), shape((count, width))
    on_sums = [shape((2 * reach, width)), shape((2 * count, width))]
    send_first, *state, slope_one = call(
        layer_kernel,
        [shape((half - later, width)), on_nodes]
        + on_sums
        + [on_edges, on_nodes, on_nodes, on_edges, on_nodes, on_nodes]
        + [shape((lines, width), F32)] * 2,
        [VMEM] * (3 + len(loaded)),
        limit=16,
    )(*halos, *loaded[:8], *loaded[9:])
    got_first = lax.ppermute(send_first, "c", pairs(2, 0))
    _, ext_twice, node_twice, _, _, _, dz_two, *_ = state
    send_later, *more = call(
        first_kernel,
        [shape((later + rows, width)), on_edges] + on_sums,
        [VMEM] * 9,
        limit=12,
        cost_estimate=cost(2 * width * width * (2 * lines + 4 * reach)),
    )(edge, w_edge1, w_edge2, to_ext, to_node, ext_twice, node_twice, dz_two, slope_one)
    got_later = lax.ppermute(send_later, "c", pairs(2, 0))
    keep, node_next, grad_edges, d_node, *backs = call(
        rest_kernel,
        [shape((half, width)), shape((1, 1, count, width)), shape((1, 1, lines, width))]
        + [shape((count, width), F32)]
        + [shape((rows, width))] * 3,
        [VMEM] * (5 + len(state) + len(more)),
        limit=12,
        scratch=[pltpu.VMEM((reach, width), F32)],
        cost_estimate=cost(2 * width * width * (4 * lines + 8 * reach)),
    )(node, edge, cot_node, w_edge1, w_node1, *state, *more)
    pair, core_back = call(
        pair_sum_kernel, [shape((half, width)), shape((rows, width))], [VMEM] * 3, limit=8
    )(keep, got_first, got_later)
    return node_next, grad_edges, d_node, backs, pair, core_back


def local(
    nodes,
    edges,
    senders,
    segments,
    send_lists,
    cot_nodes,
    cot_edges,
    w_edge1,
    w_edge2,
    w_node1,
    w_node2,
):
    count, width = nodes.shape[2:]
    lines = edges.shape[2]
    rows = send_lists.shape[3]
    weights = (w_edge1, w_edge2, w_node1, w_node2)
    total = sum(w.shape[0] for w in weights)
    block = [shape((rows, width))] * 4
    packs = call(
        pack_kernel,
        block,
        [ANY] * 2,
        scratch=[
            pltpu.VMEM((count, width), BF),
            pltpu.VMEM((4, rows), jnp.int32),
            pltpu.SemaphoreType.DMA((2,)),
        ],
    )(*in_hbm(nodes, send_lists))
    halos = exchange(packs, range(4))
    loaded = load(packs[3], nodes, edges, senders, segments, cot_nodes, cot_edges, weights)
    node_next, grad_edges, d_node, backs, pair, core_back = layer(halos, loaded)

    near, ring, far = groups()
    n_near, n_ring, n_far = len(near[0]), len(ring[0]), len(far[0])
    mid = total // 2 // n_near
    strip = mid // n_ring
    factor = float(lines * 2 * n_near * n_ring * n_far) ** -0.5
    pieces = swap(pair, near).reshape(n_near, mid, width)
    pieces = call(near_sum_kernel, shape((mid, width)), [VMEM], limit=8)(pieces)
    pieces = swap(pieces, ring).reshape(n_ring, strip, width)
    pieces, *backs = call(
        ring_sum_kernel, [shape((n_far, strip, width))] + block[:3], [VMEM] * 4, limit=8
    )(pieces, *backs)
    returned = exchange(backs, CHIP_STEPS)
    pieces = swap(pieces, far)
    pieces, *returned = call(
        functools.partial(far_sum_kernel, factor),
        [shape((n_ring, strip, width))] + block[:3],
        [VMEM] * 4,
        limit=8,
    )(pieces, *returned)
    pieces = swap(pieces, ring).reshape(mid, width)
    pieces = call(spread_kernel, shape((n_near, mid, width)), [VMEM], limit=8)(pieces)
    mine = swap(pieces, near).reshape(total // 2, width)
    other = lax.ppermute(mine, "c", pairs(2, 0))
    outs = [shape(w.shape) for w in weights]
    small = pltpu.CompilerParams(vmem_limit_bytes=4 << 20)
    sems = [pltpu.SemaphoreType.DMA((total // width,))]
    *grads, grad_nodes = pl.pallas_call(
        own_kernel,
        out_shape=outs + [shape(nodes.shape)],
        in_specs=[VMEM] * 7,
        out_specs=[ANY] * 4 + [VMEM],
        scratch_shapes=sems,
        compiler_params=small,
    )(mine, d_node, send_lists, core_back, *returned)
    grads = pl.pallas_call(
        other_kernel,
        out_shape=outs,
        in_specs=[VMEM] + [ANY] * 4,
        out_specs=[ANY] * 4,
        scratch_shapes=sems,
        compiler_params=small,
        input_output_aliases={1: 0, 2: 1, 3: 2, 4: 3},
    )(other, *grads)
    return (node_next, grad_nodes, grad_edges, *grads)


def solution(mesh):
    fine = Mesh(mesh.devices.reshape(2, 4, 2, 2, 4, 2), ("yh", "x", "c", "yl", "zh", "zl"))
    tile = P(GX, GY)
    return jax.shard_map(
        local,
        mesh=fine,
        in_specs=(tile,) * 7 + (P(),) * 4,
        out_specs=(tile,) * 3 + (P(),) * 4,
        check_vma=False,
    )
```
